32 devices in a mesh: dp: 8 (over z, y), shard: 4 (over x, core).
Axes of the slice: x: 2, y: 2, z: 4, core: 2. Of those that a mesh axis runs over, the one named last changes fastest.
Arguments:
- tokens: bfloat16 [32768, 512], P(('dp', 'shard')), may hold values from -6 to 6
- out_grad: bfloat16 [32768, 512], P(('dp', 'shard')), may hold values from -6 to 6
- domain_ids: int32 [32], P(('dp', 'shard')), may hold values from 0 to 7
- domain_weight: float32 [8], replicated, may hold values from 0.3 to 3
- attn_master: float32 [5, 512, 512], P(None, 'shard')
- attn_first: float32 [5, 512, 512], P(None, 'shard'), may hold values from -0.0078125 to 0.0078125
- attn_second: float32 [5, 512, 512], P(None, 'shard'), may hold values from 1.4663101e-07 to 1.1730481e-06
- up_master: float32 [512, 2048], P('shard'), may hold values from -0.25 to 0.25
- up_first: float32 [512, 2048], P('shard'), may hold values from -0.0078125 to 0.0078125
- up_second: float32 [512, 2048], P('shard'), may hold values from 1.4663101e-07 to 1.1730481e-06
- down_master: float32 [2048, 512], P('shard'), may hold values from -0.125 to 0.125
- down_first: float32 [2048, 512], P('shard'), may hold values from -0.0078125 to 0.0078125
- down_second: float32 [2048, 512], P('shard'), may hold values from 1.4663101e-07 to 1.1730481e-06
- norm_master: float32 [4, 512], P(None, 'shard')
- norm_first: float32 [4, 512], P(None, 'shard'), may hold values from -0.03125 to 0.03125
- norm_second: float32 [4, 512], P(None, 'shard'), may hold values from 2.3460962e-06 to 1.876877e-05
Outputs:
- block_out: bfloat16 [32768, 512], P(('dp', 'shard'))
- input_grad: float32 [32768, 512], P(('dp', 'shard'))
- attn_new: float32 [5, 512, 512], P(None, 'shard')
- attn_first_new: float32 [5, 512, 512], P(None, 'shard')
- attn_second_new: float32 [5, 512, 512], P(None, 'shard')
- up_new: float32 [512, 2048], P('shard')
- up_first_new: float32 [512, 2048], P('shard')
- up_second_new: float32 [512, 2048], P('shard')
- down_new: float32 [2048, 512], P('shard')
- down_first_new: float32 [2048, 512], P('shard')
- down_second_new: float32 [2048, 512], P('shard')
- norm_new: float32 [4, 512], P(None, 'shard')
- norm_first_new: float32 [4, 512], P(None, 'shard')
- norm_second_new: float32 [4, 512], P(None, 'shard')
- clip_norm: float32 [], replicated
- attn_copy: bfloat16 [5, 512, 512], replicated
- up_copy: bfloat16 [512, 2048], replicated
- down_copy: bfloat16 [2048, 512], replicated
- norm_copy: bfloat16 [4, 512], replicated
The draws below stay inside these ranges and needn't reach their ends.
All inputs are finite; a program needn't handle non-finite values.
Results may differ from the reference program's by a relative error of at most 0.02.
The reference program's roundings to bfloat16 on the way count: a program that leaves them out, or rounds other values in their place, can miss the bound.
Values may be sent and summed in bfloat16 or wider, within the bound.
No kernel may reach another device: no remote copies, remote signals or barrier semaphores. Data moves between devices by JAX's collectives and lax.ppermute only.
A program may use at most 128 MiB of HBM per device.

```python
import math
import jax
import jax.numpy as jnp
from jax import lax

D = 512
HEADS = 8
FF = 2048
DOMAINS = 8
STEP = 10
SEQ_LEN = 1024
SEQS = 32
TOKENS = 32768


def draw_attn_master(key, part):
    key = jax.random.fold_in(key, 11)
    scales = jnp.array([2.0, 1.0, 1.0, 2.0, 4.0], jnp.float32)
    entries = jax.random.normal(key, (5, D, D), jnp.float32)
    return entries * scales[:, None, None] / jnp.sqrt(jnp.float32(D))


def draw_norm_master(key, part):
    key = jax.random.fold_in(key, 23)
    first_key, second_key = jax.random.split(key)
    ramp = 0.6 + 1.2 * jnp.arange(D, dtype=jnp.float32) / D
    gains = ramp[None, :] * jax.random.uniform(first_key, (2, D), jnp.float32, 0.8, 1.25)
    shifts = 0.3 * jax.random.normal(second_key, (2, D), jnp.float32)
    return jnp.stack([gains[0], shifts[0], gains[1], shifts[1]])


def touch_ends(values, own_key, smallest, top_value):
    index_at = [jax.random.randint(jax.random.fold_in(own_key, axis), (), 0, length) for axis, length in enumerate(values.shape)]
    longest = values.shape.index(max(values.shape))
    beside = index_at[:longest] + [(index_at[longest] + 1) % values.shape[longest]] + index_at[longest + 1:]
    return values.at[tuple(index_at)].set(smallest).at[tuple(beside)].set(top_value)


def steps_of(key, dims, cuts, least, top_value):
    factor_of = 1.0
    for position, shards_of in cuts:
        steps = jax.random.uniform(jax.random.fold_in(jax.random.fold_in(key, 6), position), (shards_of,), jnp.float32, least / len(cuts), top_value / len(cuts))
        factor_of = factor_of * jnp.repeat(jnp.exp(steps), dims[position] // shards_of).reshape((-1,) + (1,) * (len(dims) - 1 - position))
    return factor_of


def bell_draw(own_key, shape, deviation, bound, cuts=(), held_as=jnp.bfloat16):
    values = deviation * jax.random.normal(own_key, shape, jnp.float32)
    if cuts:
        values = values * steps_of(own_key, shape, cuts, -0.22, 0.18)
    return jnp.clip(values, -bound, bound).astype(held_as)


def setup_inputs(seed: int = 0) -> dict:
    keys = jax.random.split(jax.random.key(seed), 17)
    tokens = bell_draw(keys[0], (TOKENS, D), 1.0, 6.0, ((0, 32),))
    out_grad = bell_draw(keys[1], (TOKENS, D), 1.0, 6.0, ((0, 32),))
    domain_ids = touch_ends(jax.random.randint(keys[2], (SEQS,), 0, DOMAINS), jax.random.fold_in(keys[2], 1), 0, DOMAINS - 1).astype(jnp.int32)
    domain_weight = jnp.clip(jnp.exp(jax.random.uniform(keys[3], (DOMAINS,), jnp.float32, math.log(0.3), math.log(3.0))), 0.3, 3.0)
    attn_master = draw_attn_master(jax.random.fold_in(keys[16], 71), 0)
    attn_first = bell_draw(keys[5], (5, D, D), (1 / (5 * D * D + 2 * D * FF + 4 * D) ** 0.5), 0.0078125, ((1, 4),), jnp.float32)
    attn_second = jnp.clip(jnp.exp(math.log(1.1730480764526874e-06) - 2.0794415 * jax.random.uniform(keys[6], (5, D, D), jnp.float32) ** steps_of(keys[6], (5, D, D), ((1, 4),), -0.2, 0.2)), 1.4663100955658592e-07, 1.1730480764526874e-06)
    up_master = bell_draw(keys[7], (D, FF), D ** -0.5, 0.25, ((0, 4),), jnp.float32)
    up_first = bell_draw(keys[8], (D, FF), (1 / (5 * D * D + 2 * D * FF + 4 * D) ** 0.5), 0.0078125, ((0, 4),), jnp.float32)
    up_second = jnp.clip(jnp.exp(math.log(1.1730480764526874e-06) - 2.0794415 * jax.random.uniform(keys[9], (D, FF), jnp.float32) ** steps_of(keys[9], (D, FF), ((0, 4),), -0.2, 0.2)), 1.4663100955658592e-07, 1.1730480764526874e-06)
    down_master = bell_draw(keys[10], (FF, D), FF ** -0.5, 0.125, ((0, 4),), jnp.float32)
    down_first = bell_draw(keys[11], (FF, D), (1 / (5 * D * D + 2 * D * FF + 4 * D) ** 0.5), 0.0078125, ((0, 4),), jnp.float32)
    down_second = jnp.clip(jnp.exp(math.log(1.1730480764526874e-06) - 2.0794415 * jax.random.uniform(keys[12], (FF, D), jnp.float32) ** steps_of(keys[12], (FF, D), ((0, 4),), -0.2, 0.2)), 1.4663100955658592e-07, 1.1730480764526874e-06)
    norm_master = draw_norm_master(jax.random.fold_in(keys[16], 71), 0)
    norm_first = bell_draw(keys[14], (4, D), (4 / (5 * D * D + 2 * D * FF + 4 * D) ** 0.5), 0.03125, ((1, 4),), jnp.float32)
    norm_second = jnp.clip(jnp.exp(math.log(1.8768769223242998e-05) - 2.0794415 * jax.random.uniform(keys[15], (4, D), jnp.float32) ** steps_of(keys[15], (4, D), ((1, 4),), -0.2, 0.2)), 2.3460961529053748e-06, 1.8768769223242998e-05)
    return {"tokens": tokens, "out_grad": out_grad, "domain_ids": domain_ids, "domain_weight": domain_weight, "attn_master": attn_master, "attn_first": attn_first, "attn_second": attn_second, "up_master": up_master, "up_first": up_first, "up_second": up_second, "down_master": down_master, "down_first": down_first, "down_second": down_second, "norm_master": norm_master, "norm_first": norm_first, "norm_second": norm_second}


@jax.custom_vjp
def low(v):
    return lax.optimization_barrier(v.astype(jnp.bfloat16)).astype(jnp.float32)

@jax.custom_vjp
def low_back(v):
    return v

def low_keep(v):
    return (low(v), None)

def low_pass(kept, grad):
    return (grad,)

def back_keep(v):
    return (v, None)

def back_low(kept, grad):
    return (low(grad),)
low.defvjp(low_keep, low_pass)
low_back.defvjp(back_keep, back_low)

def product(left, right):
    return low_back(jnp.dot(low(left), low(right), precision=lax.Precision.HIGHEST))

def layer_norm(values, gain, shift):
    centred = values - lax.optimization_barrier(jnp.mean(values, axis=-1, keepdims=True))
    spread = lax.optimization_barrier(jnp.mean(centred * centred, axis=-1, keepdims=True))
    return centred * lax.rsqrt(spread + 1e-05) * gain + shift

def mix_head(operands):
    queries, key_rows, value_rows, slot_exp, slot_sum = operands
    length = queries.shape[0]
    causal = jnp.arange(length)[:, None] >= jnp.arange(length)[None, :]
    affinity = jnp.where(causal, product(queries, key_rows.T), 0.0)
    numerator = product(affinity, slot_exp)
    scores = numerator / (slot_sum * math.sqrt(queries.shape[1]))
    weights = jax.nn.softmax(scores, axis=-1)
    spreads = jnp.where(causal, product(weights / slot_sum, slot_exp.T), 0.0)
    return product(spreads, value_rows)

def forward(inputs, attn_w, up_w, down_w, norm_w):
    gains = low(norm_w)
    length = inputs.shape[0]
    normed = layer_norm(inputs, gains[0], gains[1])
    queries = product(normed, attn_w[0])
    key_rows = product(normed, attn_w[1])
    value_rows = product(normed, attn_w[2])
    control = product(normed, attn_w[3])
    slot_exp = jnp.exp(control)
    slot_sum = jnp.cumsum(slot_exp, axis=0)

    def split_heads(array):
        return array.reshape(length, HEADS, -1).transpose(1, 0, 2)
    mixed = lax.map(jax.checkpoint(mix_head), (split_heads(queries), split_heads(key_rows), split_heads(value_rows), split_heads(slot_exp), split_heads(slot_sum)))
    mixed = mixed.transpose(1, 0, 2).reshape(length, -1)
    branch = inputs + product(mixed, attn_w[4])
    normed_two = layer_norm(branch, gains[2], gains[3])
    hidden = jax.nn.gelu(product(normed_two, up_w), approximate=True)
    return branch + product(hidden, down_w)

def adam_step(master, first, second, grad, rate, decay):
    first_new = 0.5 * first + 0.5 * grad
    second_new = 0.5 * second + 0.5 * grad * grad
    correction = 1.0 - 0.5 ** STEP
    update = first_new / correction / (jnp.sqrt(second_new / correction) + 1e-08)
    return (master - rate * (update + decay * master), first_new, second_new)

def reference(tokens, out_grad, domain_ids, domain_weight, attn_master, attn_first, attn_second, up_master, up_first, up_second, down_master, down_first, down_second, norm_master, norm_first, norm_second):
    onehot = (domain_ids[:, None] == jnp.arange(DOMAINS, dtype=jnp.int32)[None, :]).astype(jnp.float32)
    counts = lax.optimization_barrier(jnp.sum(onehot, axis=0))
    per_domain = domain_weight * SEQS / (DOMAINS * jnp.maximum(counts, 1.0))
    seq_weight = jnp.dot(onehot, per_domain, precision=lax.Precision.HIGHEST)
    inputs = tokens.astype(jnp.float32).reshape(SEQS, SEQ_LEN, D)
    cotangent = out_grad.astype(jnp.float32).reshape(SEQS, SEQ_LEN, D)
    params = (attn_master, up_master, down_master, norm_master)

    def per_sequence(totals, item):
        seq_in, seq_cot, factor = item
        result, pull = jax.vjp(forward, seq_in, *params)
        grads = pull(seq_cot * factor)
        totals = tuple((total + grad for total, grad in zip(totals, grads[1:])))
        return (totals, (result.astype(jnp.bfloat16), grads[0]))
    start = tuple((jnp.zeros_like(param) for param in params))
    totals, (outputs, in_grads) = lax.scan(per_sequence, start, (inputs, cotangent, seq_weight))
    total_sq = sum((jnp.sum(grad * grad) for grad in totals))
    clip_norm = jnp.sqrt(total_sq)
    factor = jnp.minimum(1.0, 1.0 / (clip_norm + 1e-06))
    attn_new = adam_step(attn_master, attn_first, attn_second, totals[0] * factor, 0.05, 0.01)
    up_new = adam_step(up_master, up_first, up_second, totals[1] * factor, 0.05, 0.01)
    down_new = adam_step(down_master, down_first, down_second, totals[2] * factor, 0.05, 0.01)
    norm_new = adam_step(norm_master, norm_first, norm_second, totals[3] * factor, 0.3, 0.0)
    return (outputs.reshape(TOKENS, D), in_grads.reshape(TOKENS, D), attn_new[0], attn_new[1], attn_new[2], up_new[0], up_new[1], up_new[2], down_new[0], down_new[1], down_new[2], norm_new[0], norm_new[1], norm_new[2], clip_norm, attn_new[0].astype(jnp.bfloat16), up_new[0].astype(jnp.bfloat16), down_new[0].astype(jnp.bfloat16), norm_new[0].astype(jnp.bfloat16))
```

```python
import functools
import jax
import jax.numpy as jnp
from jax import lax
from jax.experimental import pallas as pl
from jax.experimental.pallas import tpu as pltpu
from jax.sharding import PartitionSpec as P

BF = jnp.bfloat16
F32 = jnp.float32
VMEM_LIMIT = 56 * 1024 * 1024
CHUNK = 256
SLOT = 64
GROUP = 256
SMALL = 16
STEP = 10


def dot(a, b):
    return jnp.dot(a, b, preferred_element_type=F32)


def dot_nt(a, b):
    return lax.dot_general(a, b, (((1,), (1,)), ((), ())), preferred_element_type=F32)


def dot_tn(a, b):
    return lax.dot_general(a, b, (((0,), (0,)), ((), ())), preferred_element_type=F32)


def head_of(shape, dim):
    return lax.broadcasted_iota(jnp.int32, shape, dim) // SLOT


def block_diagonal(state):
    return jnp.where(head_of(state.shape, 0) == head_of(state.shape, 1), state, 0.0).astype(BF)


def only_head(rows, head):
    return jnp.where(head_of(rows.shape, 1) == head, rows, jnp.zeros_like(rows))


def lower(square):
    row = lax.broadcasted_iota(jnp.int32, square.shape, 0)
    col = lax.broadcasted_iota(jnp.int32, square.shape, 1)
    return jnp.where(row >= col, square, 0.0).astype(BF)


def upper(square):
    row = lax.broadcasted_iota(jnp.int32, square.shape, 0)
    col = lax.broadcasted_iota(jnp.int32, square.shape, 1)
    return jnp.where(row <= col, square, 0.0).astype(BF)


def split_dot(ones, values):
    high = values.astype(BF)
    low = (values - high.astype(F32)).astype(BF)
    return dot(ones, high) + dot(ones, low)


def head_sums(values):
    ones = jnp.where(
        head_of((GROUP, GROUP), 0) == head_of((GROUP, GROUP), 1), 1.0, 0.0
    ).astype(BF)
    high = values.astype(BF)
    low = (values - high.astype(F32)).astype(BF)
    return dot(high, ones) + dot(low, ones)


def head_max(values):
    top = None
    head = head_of(values.shape, 1)
    for index in range(GROUP // SLOT):
        mine = jnp.max(jnp.where(head == index, values, -jnp.inf), axis=1, keepdims=True)
        top = mine if top is None else jnp.where(head == index, mine, top)
    return top


def normalise(values):
    centred = values - jnp.mean(values, axis=-1, keepdims=True)
    inv = lax.rsqrt(jnp.mean(centred * centred, axis=-1, keepdims=True) + 1e-05)
    return centred * inv, inv


def normalise_back(grad, unit, inv, gain):
    scaled = grad * gain
    return inv * (
        scaled
        - jnp.mean(scaled, axis=-1, keepdims=True)
        - unit * jnp.mean(scaled * unit, axis=-1, keepdims=True)
    )


def project_kernel(
    pos_ref, x_ref, p0, p1, p2, p3, q_ref, k_ref, v_ref, n_ref, e_ref, eb_ref, z_ref, w_ref, norm_ref, carry
):
    width = x_ref.shape[1]
    part = width // 4

    @pl.when(pl.program_id(0) == 0)
    def _():
        for index, piece in enumerate((p0, p1, p2, p3)):
            rows = pl.ds(pl.multiple_of(pos_ref[index] * part, part), part)
            for m in range(4):
                w_ref[m, rows, :] = piece[m * part : (m + 1) * part, :]
            norm_ref[0:4, rows] = piece[4 * part : 4 * part + 4, 0:part].astype(F32)
        carry[...] = jnp.zeros_like(carry)

    unit, _ = normalise(x_ref[...].astype(F32))
    normed = (unit * norm_ref[0:1, :] + norm_ref[1:2, :]).astype(BF)
    n_ref[...] = normed
    q_ref[...] = dot(normed, w_ref[0]).astype(BF)
    k_ref[...] = dot(normed, w_ref[1]).astype(BF)
    v_ref[...] = dot(normed, w_ref[2]).astype(BF)
    e = jnp.exp(dot(normed, w_ref[3]))
    e_ref[...] = e
    eb_ref[...] = e.astype(BF)
    rows = e.shape[0]
    ones = lower(jnp.ones((rows, rows), F32))
    z = split_dot(ones, e) + carry[0:1, :]
    z_ref[...] = z
    carry[0:1, :] = z[rows - 1 : rows, :]


def project(pos, x, pieces):
    length, width = x.shape
    steps = length // CHUNK
    rows = lambda dtype: jax.ShapeDtypeStruct((length, width), dtype)
    block = pl.BlockSpec((CHUNK, width), lambda i: (i, 0))
    whole = lambda a: pl.BlockSpec(a.shape, lambda i: (0,) * len(a.shape))
    return pl.pallas_call(
        project_kernel,
        grid=(steps,),
        in_specs=[pl.BlockSpec(memory_space=pltpu.SMEM), block] + [whole(p) for p in pieces],
        out_specs=[block] * 7
        + [
            pl.BlockSpec((4, width, width), lambda i: (0, 0, 0)),
            pl.BlockSpec((8, width), lambda i: (0, 0)),
        ],
        out_shape=[rows(BF), rows(BF), rows(BF), rows(BF), rows(F32), rows(BF), rows(F32)]
        + [jax.ShapeDtypeStruct((4, width, width), BF), jax.ShapeDtypeStruct((8, width), F32)],
        scratch_shapes=[pltpu.VMEM((8, width), F32)],
        compiler_params=pltpu.CompilerParams(
            dimension_semantics=("arbitrary",), vmem_limit_bytes=VMEM_LIMIT
        ),
        name="project",
    )(pos, x, *pieces)


def mix_kernel(q_ref, k_ref, v_ref, e_ref, z_ref, o_ref, w_ref, s_ref, keys_ref, values_ref, keys, values):
    @pl.when(pl.program_id(1) == 0)
    def _():
        keys[...] = jnp.zeros_like(keys)
        values[...] = jnp.zeros_like(values)

    q, k, v, e = q_ref[...], k_ref[...], v_ref[...], e_ref[...]
    inv = 1.0 / z_ref[...]
    heads = GROUP // SLOT
    es = [only_head(e, h) for h in range(heads)]
    key_state = block_diagonal(keys[...])
    value_state = block_diagonal(values[...])
    keys_ref[0, 0] = key_state
    values_ref[0, 0] = value_state
    total = dot(q, key_state)
    for h in range(heads):
        total += dot(lower(dot_nt(q, only_head(k, h))), es[h])
    scores = total * inv * 0.125
    s_ref[...] = scores
    raised = jnp.exp(scores - head_max(scores))
    weights = raised / head_sums(raised)
    w_ref[...] = weights
    ratio = (weights * inv).astype(BF)
    out = dot(ratio, value_state)
    for h in range(heads):
        out += dot(lower(dot_nt(ratio, es[h])), only_head(v, h))
    o_ref[...] = out.astype(BF)
    keys[...] += dot_tn(k, e)
    values[...] += dot_tn(e, v)


def mix(q, k, v, e, z):
    length, width = q.shape
    steps, groups = length // CHUNK, width // GROUP
    block = pl.BlockSpec((CHUNK, GROUP), lambda g, i: (i, g))
    state = pl.BlockSpec((1, 1, GROUP, GROUP), lambda g, i: (g, i, 0, 0))
    rows = lambda dtype: jax.ShapeDtypeStruct((length, width), dtype)
    states = jax.ShapeDtypeStruct((groups, steps, GROUP, GROUP), BF)
    return pl.pallas_call(
        mix_kernel,
        grid=(groups, steps),
        in_specs=[block] * 5,
        out_specs=[block] * 3 + [state] * 2,
        out_shape=[rows(BF), rows(F32), rows(F32), states, states],
        scratch_shapes=[pltpu.VMEM((GROUP, GROUP), F32)] * 2,
        compiler_params=pltpu.CompilerParams(
            dimension_semantics=("arbitrary", "arbitrary"), vmem_limit_bytes=VMEM_LIMIT
        ),
        name="mix",
    )(q, k, v, e, z)


def mix_back_kernel(
    g_ref, q_ref, k_ref, v_ref, eb_ref, e_ref, z_ref, w_ref, s_ref, keys_ref, values_ref,
    dq_ref, dk_ref, dv_ref, dc_ref, later_v, later_k, carry
):
    @pl.when(pl.program_id(1) == 0)
    def _():
        later_v[...] = jnp.zeros_like(later_v)
        later_k[...] = jnp.zeros_like(later_k)
        carry[...] = jnp.zeros_like(carry)

    g, q, k, v, e = g_ref[...], q_ref[...], k_ref[...], v_ref[...], eb_ref[...]
    inv = 1.0 / z_ref[...]
    weights = w_ref[...]
    ratio = (weights * inv).astype(BF)
    heads = GROUP // SLOT
    es = [only_head(e, h) for h in range(heads)]
    state = block_diagonal(later_v[...])
    d_ratio = dot_nt(g, values_ref[0, 0])
    dv = dot(e, state)
    de = dot_nt(v, state)
    for h in range(heads):
        vh = only_head(v, h)
        d_ratio += dot(lower(dot_nt(g, vh)), es[h])
        de += dot(upper(dot_nt(vh, g)), only_head(ratio, h))
        dv += dot(upper(dot_nt(es[h], ratio)), only_head(g, h))
    dv_ref[...] = dv.astype(BF)
    d_weights = d_ratio * inv
    both = d_weights * weights
    d_scores = weights * (d_weights - head_sums(both))
    dn = (d_scores * inv * 0.125).astype(BF)
    dz = -(both + d_scores * s_ref[...]) * inv
    state = block_diagonal(later_k[...])
    dq = dot_nt(dn, keys_ref[0, 0])
    dk = dot(e, state)
    de += dot_nt(k, state)
    for h in range(heads):
        kh = only_head(k, h)
        dq += dot(lower(dot_nt(dn, es[h])), kh)
        dk += dot(upper(dot_nt(es[h], dn)), only_head(q, h))
        de += dot(upper(dot_nt(kh, q)), only_head(dn, h))
    dq_ref[...] = dq.astype(BF)
    dk_ref[...] = dk.astype(BF)
    rows = dz.shape[0]
    ones = upper(jnp.ones((rows, rows), F32))
    z_sum = split_dot(ones, dz) + carry[0:1, :]
    carry[0:1, :] = z_sum[0:1, :]
    dc_ref[...] = ((de + z_sum) * e_ref[...]).astype(BF)
    later_v[...] += dot_tn(ratio, g)
    later_k[...] += dot_tn(dn, q)


def mix_back(g, q, k, v, eb, e, z, w, s, keys, values):
    length, width = q.shape
    steps, groups = length // CHUNK, width // GROUP
    block = pl.BlockSpec((CHUNK, GROUP), lambda g, i: (steps - 1 - i, g))
    state = pl.BlockSpec((1, 1, GROUP, GROUP), lambda g, i: (g, steps - 1 - i, 0, 0))
    rows = jax.ShapeDtypeStruct((length, width), BF)
    return pl.pallas_call(
        mix_back_kernel,
        grid=(groups, steps),
        in_specs=[block] * 9 + [state] * 2,
        out_specs=[block] * 4,
        out_shape=[rows] * 4,
        scratch_shapes=[pltpu.VMEM((GROUP, GROUP), F32)] * 2 + [pltpu.VMEM((8, GROUP), F32)],
        compiler_params=pltpu.CompilerParams(
            dimension_semantics=("arbitrary", "arbitrary"), vmem_limit_bytes=VMEM_LIMIT
        ),
        name="mix_back",
    )(g, q, k, v, eb, e, z, w, s, keys, values)


def scatter_parts(pos_ref, grads, send_ref, keep_ref, half, offset, part):
    for index in range(4):
        pos = pos_ref[index]
        target = send_ref if index % 2 else keep_ref
        rows = pl.ds(pl.multiple_of((pos // 2) * half + offset, part), part)
        target[rows, :] = grads[pl.ds(pl.multiple_of(pos * part, part), part), :]


def feed_kernel(
    pos_ref, factor_ref, x_ref, g_ref, o_ref, norm_ref, p0, p1, p2, p3,
    y_ref, dh_ref, do_ref, send_ref, keep_ref, dnorm_ref,
    wo, w1, w2, branch, unit_ref, inv_ref, n2, gb, n2_t, gb_t, dn2, grads
):
    step = pl.program_id(0)
    last = pl.num_programs(0) - 1
    length, width = x_ref.shape
    part = width // 4
    block = w1.shape[2]
    tiles = length // 256

    @pl.when(step == 0)
    def _():
        for index, piece in enumerate((p0, p1, p2, p3)):
            pos = pos_ref[index]
            rows = pl.ds(pl.multiple_of(pos * part, part), part)
            wo[rows, :] = piece[0:part, :]
            for j in range(4):
                w1[j, rows, :] = piece[(j + 1) * part : (j + 2) * part, :]
            w2[pos] = piece[5 * part : 5 * part + block, :]

        def before(i, _):
            rows = pl.ds(pl.multiple_of(i * 256, 256), 256)
            h1 = x_ref[rows, :].astype(F32) + dot(o_ref[rows, :], wo[...])
            branch[rows, :] = h1
            unit, inv = normalise(h1)
            unit_ref[rows, :] = unit
            inv_ref[rows, :] = jnp.broadcast_to(inv, (256, 128))
            normed = (unit * norm_ref[2:3, :] + norm_ref[3:4, :]).astype(BF)
            n2[rows, :] = normed
            n2_t[:, rows] = normed.T
            grad = (g_ref[rows, :].astype(F32) * factor_ref[0]).astype(BF)
            gb[rows, :] = grad
            gb_t[:, rows] = grad.T
            dn2[rows, :] = jnp.zeros((256, width), F32)
            return 0

        lax.fori_loop(0, tiles, before, 0)

    up = w1[step]
    down = w2[step]
    up_grad = jnp.zeros((width, block), F32)
    down_grad = jnp.zeros((width, block), F32)
    for i in range(tiles):
        rows = slice(i * 256, (i + 1) * 256)
        a = dot(n2[rows, :], up)
        inner = 0.7978845608 * (a + 0.044715 * a * a * a)
        t = jnp.tanh(inner)
        u = (0.5 * a * (1.0 + t)).astype(BF)
        slope = 0.5 * (1.0 + t) + 0.5 * a * (1.0 - t * t) * (
            0.7978845608 + (3.0 * 0.044715 * 0.7978845608) * a * a
        )
        da = (dot_nt(gb[rows, :], down) * slope).astype(BF)
        branch[rows, :] += dot(u, down)
        dn2[rows, :] += dot_nt(da, up)
        up_grad += dot(n2_t[:, rows], da)
        down_grad += dot(gb_t[:, rows], u)
    half = send_ref.shape[0] // 2
    grads[...] = up_grad.astype(BF)
    scatter_parts(pos_ref, grads, send_ref, keep_ref, half, (step + 1) * part, part)
    place = pl.ds(pl.multiple_of((step // 2) * half + 5 * part, part), width)
    mine = (step ^ pos_ref[0]) & 1 == 0

    @pl.when(mine)
    def _():
        keep_ref[place, :] = down_grad.astype(BF)

    @pl.when(jnp.logical_not(mine))
    def _():
        send_ref[place, :] = down_grad.astype(BF)

    @pl.when(step == last)
    def _():
        gain = norm_ref[2:3, :]

        def after(i, sums):
            rows = pl.ds(pl.multiple_of(i * 256, 256), 256)
            y_ref[rows, :] = branch[rows, :].astype(BF)
            grad = dn2[rows, :]
            unit = unit_ref[rows, :]
            dh = g_ref[rows, :].astype(F32) * factor_ref[0] + normalise_back(
                grad, unit, inv_ref[rows, 0:1], gain
            )
            dh_ref[rows, :] = dh
            dh_low = dh.astype(BF)
            do_ref[rows, :] = dot_nt(dh_low, wo[...]).astype(BF)
            return (
                sums[0] + jnp.sum(grad * unit, axis=0, keepdims=True),
                sums[1] + jnp.sum(grad, axis=0, keepdims=True),
                sums[2] + dot_tn(o_ref[rows, :], dh_low),
            )

        empty = jnp.zeros((1, width), F32)
        sums = lax.fori_loop(0, tiles, after, (empty, empty, jnp.zeros((width, width), F32)))
        dnorm_ref[...] = jnp.zeros_like(dnorm_ref)
        dnorm_ref[0:1, :] = sums[0]
        dnorm_ref[1:2, :] = sums[1]
        grads[...] = sums[2].astype(BF)
        scatter_parts(pos_ref, grads, send_ref, keep_ref, half, 0, part)


def feed(pos, factor, x, g, o, norm, pieces):
    length, width = x.shape
    block = (pieces[0].shape[0] - 5 * (width // 4))
    rows = lambda dtype: jax.ShapeDtypeStruct((length, width), dtype)
    whole = lambda a: pl.BlockSpec(a.shape, lambda i: (0,) * len(a.shape))
    out = [
        rows(BF), rows(F32), rows(BF),
        jax.ShapeDtypeStruct((2 * pieces[0].shape[0], width), BF),
        jax.ShapeDtypeStruct((2 * pieces[0].shape[0], width), BF),
        jax.ShapeDtypeStruct((8, width), F32),
    ]
    args = (x, g, o, norm) + tuple(pieces)
    return pl.pallas_call(
        feed_kernel,
        grid=(4,),
        in_specs=[pl.BlockSpec(memory_space=pltpu.SMEM)] * 2 + [whole(a) for a in args],
        out_specs=[whole(a) for a in out],
        out_shape=out,
        scratch_shapes=[
            pltpu.VMEM((width, width), BF),
            pltpu.VMEM((4, width, block), BF),
            pltpu.VMEM((4, block, width), BF),
            pltpu.VMEM((length, width), F32),
            pltpu.VMEM((length, width), F32),
            pltpu.VMEM((length, 128), F32),
            pltpu.VMEM((length, width), BF),
            pltpu.VMEM((length, width), BF),
            pltpu.VMEM((width, length), BF),
            pltpu.VMEM((width, length), BF),
            pltpu.VMEM((length, width), F32),
            pltpu.VMEM((width, block), BF),
        ],
        compiler_params=pltpu.CompilerParams(
            dimension_semantics=("arbitrary",), vmem_limit_bytes=VMEM_LIMIT
        ),
        name="feed",
    )(pos, factor, *args)


def project_back_kernel(
    pos_ref, x_ref, n_ref, dq_ref, dk_ref, dv_ref, dc_ref, dh_ref, w_ref, norm_ref, dnorm_ref,
    dx_ref, send_ref, keep_ref, w_grad, sums
):
    step = pl.program_id(0)
    width = x_ref.shape[1]
    part = width // 4

    @pl.when(step == 0)
    def _():
        w_grad[...] = jnp.zeros_like(w_grad)
        sums[...] = jnp.zeros_like(sums)

    n_t = n_ref[...].T
    dn = None
    for m, ref in enumerate((dq_ref, dk_ref, dv_ref, dc_ref)):
        d = ref[...]
        w_grad[m] += dot(n_t, d)
        term = dot_nt(d, w_ref[m])
        dn = term if dn is None else dn + term
    unit, inv = normalise(x_ref[...].astype(F32))
    dx_ref[...] = dh_ref[...] + normalise_back(dn, unit, inv, norm_ref[0:1, :])
    sums[0:1, :] += jnp.sum(dn * unit, axis=0, keepdims=True)
    sums[1:2, :] += jnp.sum(dn, axis=0, keepdims=True)

    @pl.when(step == pl.num_programs(0) - 1)
    def _():
        for index in range(4):
            pos = pos_ref[index]
            target = send_ref if index % 2 else keep_ref
            for m in range(4):
                rows = pl.ds(pl.multiple_of((pos // 2) * width + m * part, part), part)
                target[rows, :] = w_grad[m, pl.ds(pl.multiple_of(pos * part, part), part), :].astype(BF)
        small = jnp.concatenate(
            [sums[0:2, :], dnorm_ref[0:2, :], jnp.zeros((SMALL - 4, width), F32)], axis=0
        ).astype(BF)
        send_ref[2 * width : 2 * width + SMALL, :] = small
        keep_ref[2 * width : 2 * width + SMALL, :] = small


def project_back(pos, x, n, dq, dk, dv, dc, dh, w, norm, dnorm):
    length, width = x.shape
    tile = 256
    block = pl.BlockSpec((tile, width), lambda i: (i, 0))
    whole = lambda a: pl.BlockSpec(a.shape, lambda i: (0,) * len(a.shape))
    out = [
        jax.ShapeDtypeStruct((2 * width + SMALL, width), BF),
        jax.ShapeDtypeStruct((2 * width + SMALL, width), BF),
    ]
    return pl.pallas_call(
        project_back_kernel,
        grid=(length // tile,),
        in_specs=[pl.BlockSpec(memory_space=pltpu.SMEM)]
        + [block] * 7
        + [whole(w), whole(norm), whole(dnorm)],
        out_specs=[block] + [whole(a) for a in out],
        out_shape=[jax.ShapeDtypeStruct((length, width), F32)] + out,
        scratch_shapes=[pltpu.VMEM((4, width, width), F32), pltpu.VMEM((8, width), F32)],
        compiler_params=pltpu.CompilerParams(
            dimension_semantics=("arbitrary",), vmem_limit_bytes=VMEM_LIMIT
        ),
        name="project_back",
    )(pos, x, n, dq, dk, dv, dc, dh, w, norm, dnorm)


def exchange(values, even, odd):
    dp, shard = lax.axis_size("dp"), lax.axis_size("shard")
    perm = []
    for d in range(dp):
        for s in range(shard):
            axis, bit = odd if s % 2 else even
            other = (d ^ bit, s) if axis == "dp" else (d, s ^ bit)
            perm.append((d * shard + s, other[0] * shard + other[1]))
    return lax.ppermute(values, ("dp", "shard"), perm)


def swap(values, axis, bit):
    return exchange(values, (axis, bit), (axis, bit))


def fold_kernel(index_ref, acc_ref, got_ref, send_ref, keep_ref, *, pieces, extra):
    half = pieces // 2
    rows = (send_ref.shape[0] - extra) // half
    for j in range(half):
        for target, index in ((send_ref, j), (keep_ref, half + j)):
            source = pl.ds(pl.multiple_of(index_ref[index] * rows, rows), rows)
            total = acc_ref[source, :].astype(F32) + got_ref[source, :].astype(F32)
            target[j * rows : (j + 1) * rows, :] = total.astype(BF)
    if extra:
        last = pieces * rows
        total = acc_ref[last : last + extra, :].astype(F32) + got_ref[last : last + extra, :].astype(F32)
        send_ref[half * rows : half * rows + extra, :] = total.astype(BF)
        keep_ref[half * rows : half * rows + extra, :] = total.astype(BF)


def fold(index, acc, got, pieces, extra):
    height, width = acc.shape
    rows = (height - extra) // pieces
    out = jax.ShapeDtypeStruct((rows * pieces // 2 + extra, width), BF)
    whole = pl.BlockSpec(memory_space=pltpu.VMEM)
    return pl.pallas_call(
        functools.partial(fold_kernel, pieces=pieces, extra=extra),
        in_specs=[pl.BlockSpec(memory_space=pltpu.SMEM), whole, whole],
        out_specs=[whole, whole],
        out_shape=[out, out],
        compiler_params=pltpu.CompilerParams(vmem_limit_bytes=VMEM_LIMIT),
        name="fold",
    )(index, acc, got)


def add_low(left, right):
    return (left.astype(F32) + right.astype(F32)).astype(BF)


def bits_of(size):
    return [1 << b for b in range(size.bit_length() - 1)]


def reduce_scatter(send, keep, extra):
    dp, shard = lax.axis_index("dp"), lax.axis_index("shard")
    dp_bits = bits_of(lax.axis_size("dp"))
    split = dp_bits[:3]
    odd = shard % 2
    even_plan = [("shard", 2)] + [("dp", b) for b in split]
    odd_plan = [("dp", b) for b in split] + [("shard", 2)]
    got = swap(send, "shard", 1)
    pieces = 2 ** (len(split) + 1)
    for phase, (even_dim, odd_dim) in enumerate(zip(even_plan, odd_plan)):
        def bit_of(dim):
            return (((dp if dim[0] == "dp" else shard) & dim[1]) != 0).astype(jnp.int32)

        bit = jnp.where(odd == 1, bit_of(odd_dim), bit_of(even_dim))
        rank = jnp.where((odd == 0) & (phase == 0), len(split), 0)
        j = jnp.arange(pieces // 2, dtype=jnp.int32)
        base = ((j >> rank) << (rank + 1)) | (j & ((1 << rank) - 1))
        index = jnp.concatenate([base | ((1 - bit) << rank), base | (bit << rank)]).astype(jnp.int32)
        send, keep = fold(index, keep, got, pieces, extra)
        got = exchange(send, even_dim, odd_dim)
        pieces //= 2
    total = add_low(keep, got)
    for b in dp_bits[3:]:
        total = add_low(total, swap(total, "dp", b))
    return total


def gather_dp(piece):
    split = bits_of(lax.axis_size("dp"))[:3]
    even_plan = [split[0]] + split[1:][::-1]
    odd_plan = split[::-1]
    odd = lax.axis_index("shard") % 2
    mask = jnp.zeros((1,), jnp.int32)
    for even_bit, odd_bit in zip(even_plan, odd_plan):
        piece = jnp.concatenate([piece, exchange(piece, ("dp", even_bit), ("dp", odd_bit))], axis=0)
        mask = jnp.concatenate([mask, mask | jnp.where(odd == 1, odd_bit, even_bit)])
    return piece, (lax.axis_index("dp") & (2 ** len(split) - 1)) ^ mask


def adam(master, first, second, grad, rate, decay):
    first_new = 0.5 * first + 0.5 * grad
    second_new = 0.5 * second + 0.5 * grad * grad
    correction = 1.0 - 0.5**STEP
    update = first_new / correction / (jnp.sqrt(second_new / correction) + 1e-08)
    return master - rate * (update + decay * master), first_new, second_new


def update_kernel(
    index_ref, factor_ref, early_ref, late_ref, gn_ref,
    am, af, as_, um, uf, us, dm, df, ds, nm, nf, ns,
    am2, af2, as2, um2, uf2, us2, dm2, df2, ds2, nm2, nf2, ns2, copy_ref, early, late
):
    step = pl.program_id(0)
    steps = pl.num_programs(0)
    factor = factor_ref[0]
    width = early.shape[1]
    part = late.shape[0] // 4

    @pl.when(step == 0)
    def _():
        count = index_ref.shape[0]
        for source, target in ((early_ref, early), (late_ref, late)):
            rows = target.shape[0] // count
            for j in range(count):
                place = pl.ds(pl.multiple_of(index_ref[j] * rows, rows), rows)
                target[place, :] = source[j * rows : (j + 1) * rows, :]
        new = adam(nm[...], nf[...], ns[...], gn_ref[...] * factor, 0.3, 0.0)
        nm2[...], nf2[...], ns2[...] = new
        copy_ref[copy_ref.shape[0] - SMALL :, :] = jnp.zeros((SMALL, width), BF)
        copy_ref[copy_ref.shape[0] - SMALL : copy_ref.shape[0] - SMALL + 4, 0 : nm.shape[1]] = new[0].astype(BF)

    height = part // steps

    def span(base, size):
        return pl.ds(pl.multiple_of(base + step * size, size), size)

    for m in range(5):
        source = late[span(m * part, height), :] if m < 4 else early[span(0, height), :]
        new = adam(am[m], af[m], as_[m], source.astype(F32) * factor, 0.05, 0.01)
        am2[m], af2[m], as2[m] = new
        copy_ref[span(m * part, height), :] = new[0].astype(BF)
    blocks = um.shape[1] // width
    for j in range(blocks):
        source = early[span((j + 1) * part, height), :]
        cols = slice(j * width, (j + 1) * width)
        new = adam(um[:, cols], uf[:, cols], us[:, cols], source.astype(F32) * factor, 0.05, 0.01)
        um2[:, cols], uf2[:, cols], us2[:, cols] = new
        copy_ref[span((5 + j) * part, height), :] = new[0].astype(BF)
    tall = dm.shape[0]
    source = early[(blocks + 1) * part : (blocks + 1) * part + width, span(0, tall)].astype(F32).T
    new = adam(dm[...], df[...], ds[...], source * factor, 0.05, 0.01)
    dm2[...], df2[...], ds2[...] = new
    copy_ref[span((5 + blocks) * part, tall), :] = new[0].astype(BF)


def update(index, factor, early, late, gn, attn, up, down, norm):
    steps = 4
    smem = pl.BlockSpec(memory_space=pltpu.SMEM)
    whole = lambda a: pl.BlockSpec(a.shape, lambda i: (0,) * len(a.shape))
    five, part, width = attn[0].shape
    specs = (
        [pl.BlockSpec((five, part // steps, width), lambda i: (0, i, 0))] * 3
        + [pl.BlockSpec((part // steps, up[0].shape[1]), lambda i: (i, 0))] * 3
        + [pl.BlockSpec((down[0].shape[0] // steps, width), lambda i: (i, 0))] * 3
        + [whole(norm[0])] * 3
    )
    states = tuple(attn) + tuple(up) + tuple(down) + tuple(norm)
    copy = jax.ShapeDtypeStruct((early.shape[0] + late.shape[0] + SMALL, width), BF)
    return pl.pallas_call(
        update_kernel,
        grid=(steps,),
        in_specs=[smem, smem, whole(early), whole(late), whole(gn)] + specs,
        out_specs=specs + [whole(copy)],
        out_shape=[jax.ShapeDtypeStruct(a.shape, F32) for a in states] + [copy],
        scratch_shapes=[pltpu.VMEM(early.shape, BF), pltpu.VMEM(late.shape, BF)],
        compiler_params=pltpu.CompilerParams(
            dimension_semantics=("arbitrary",), vmem_limit_bytes=VMEM_LIMIT
        ),
        name="update",
    )(index, factor, early, late, gn, *states)


def unpack_kernel(pos_ref, p0, p1, p2, p3, attn_ref, up_ref, down_ref, norm_ref):
    part = attn_ref.shape[1] // 4
    width = attn_ref.shape[2]
    blocks = up_ref.shape[1] // width
    tall = down_ref.shape[0] // 4
    for index, piece in enumerate((p0, p1, p2, p3)):
        pos = pos_ref[index]
        rows = pl.ds(pl.multiple_of(pos * part, part), part)
        for m in range(5):
            attn_ref[m, rows, :] = piece[m * part : (m + 1) * part, :]
        for j in range(blocks):
            up_ref[rows, j * width : (j + 1) * width] = piece[(5 + j) * part : (6 + j) * part, :]
        last = (5 + blocks) * part
        down_ref[pl.ds(pl.multiple_of(pos * tall, tall), tall), :] = piece[last : last + tall, :]
        norm_ref[0:4, rows] = piece[last + tall : last + tall + 4, 0:part]


def unpack(pos, pieces, width, hidden):
    whole = pl.BlockSpec(memory_space=pltpu.VMEM)
    return pl.pallas_call(
        unpack_kernel,
        in_specs=[pl.BlockSpec(memory_space=pltpu.SMEM)] + [whole] * 4,
        out_specs=[whole] * 4,
        out_shape=[
            jax.ShapeDtypeStruct((5, width, width), BF),
            jax.ShapeDtypeStruct((width, hidden), BF),
            jax.ShapeDtypeStruct((hidden, width), BF),
            jax.ShapeDtypeStruct((4, width), BF),
        ],
        compiler_params=pltpu.CompilerParams(vmem_limit_bytes=VMEM_LIMIT),
        name="unpack",
    )(pos, *pieces)


def gather_shard(own):
    across = swap(own, "shard", 2)
    return own, swap(own, "shard", 1), across, swap(across, "shard", 1)


def sum_all(values, axes):
    for axis in axes:
        for b in bits_of(lax.axis_size(axis)):
            values = values + swap(values, axis, b)
    return values


def shards(
    tokens, out_grad, domain_ids, domain_weight,
    attn_master, attn_first, attn_second,
    up_master, up_first, up_second,
    down_master, down_first, down_second,
    norm_master, norm_first, norm_second,
):
    width = tokens.shape[1]
    hidden = up_master.shape[1]
    part = width // 4
    blocks = hidden // width
    shard = lax.axis_index("shard").astype(jnp.int32)
    pos = shard ^ jnp.arange(4, dtype=jnp.int32)

    small = jnp.pad(norm_master.astype(BF), ((0, SMALL - 4), (0, width - part)))
    first = gather_shard(
        jnp.concatenate([attn_master[:4].astype(BF).reshape(4 * part, width), small])
    )
    second = gather_shard(
        jnp.concatenate(
            [attn_master[4].astype(BF)]
            + [up_master[:, j * width : (j + 1) * width].astype(BF) for j in range(blocks)]
            + [down_master.astype(BF)]
        )
    )

    domains = domain_weight.shape[0]
    onehot = (domain_ids[:, None] == jnp.arange(domains, dtype=jnp.int32)[None, :]).astype(F32)
    counts = sum_all(jnp.sum(onehot, axis=0), ("shard", "dp"))
    total_seqs = lax.axis_size("dp") * lax.axis_size("shard") * domain_ids.shape[0]
    per_domain = domain_weight * total_seqs / (domains * jnp.maximum(counts, 1.0))
    seq_weight = jnp.sum(onehot * per_domain[None, :], axis=1)

    q, k, v, n, e, eb, z, w, norm = project(pos, tokens, first)
    o, weights, scores, keys, values = mix(q, k, v, eb, z)
    y, dh, do, send, keep, dnorm = feed(pos, seq_weight, tokens, out_grad, o, norm, second)
    early = reduce_scatter(send, keep, 0)
    early, index = gather_dp(early)
    early_sq = jnp.sum(jnp.square(early.astype(F32)))
    dq, dk, dv, dc = mix_back(do, q, k, v, eb, e, z, weights, scores, keys, values)
    dx, send, keep = project_back(pos, tokens, n, dq, dk, dv, dc, dh, w, norm, dnorm)
    late = reduce_scatter(send, keep, SMALL)
    rows = late.shape[0] - SMALL
    norm_grad = lax.dynamic_slice(late[rows : rows + 4], (0, shard * part), (4, part)).astype(F32)
    late, _ = gather_dp(late[:rows])
    square = early_sq + jnp.sum(jnp.square(late.astype(F32))) + jnp.sum(jnp.square(norm_grad))
    clip_norm = jnp.sqrt(sum_all(square[None], ("shard",)))
    factor = jnp.minimum(1.0, 1.0 / (clip_norm + 1e-06))
    new = update(
        index, factor, early, late, norm_grad,
        (attn_master, attn_first, attn_second),
        (up_master, up_first, up_second),
        (down_master, down_first, down_second),
        (norm_master, norm_first, norm_second),
    )
    copies = unpack(pos, gather_shard(new[12]), width, hidden)
    return (y, dx) + tuple(new[:12]) + (clip_norm[0],) + tuple(copies)


def solution(mesh):
    rows = P(("dp", "shard"), None)
    attn = (P(None, "shard", None),) * 3
    tall = (P("shard", None),) * 6
    norm = (P(None, "shard"),) * 3
    return jax.shard_map(
        shards,
        mesh=mesh,
        in_specs=(rows, rows, P(("dp", "shard")), P()) + attn + tall + norm,
        out_specs=(rows, rows) + attn + tall + norm + (P(),) * 5,
        check_vma=False,
    )
```

```python
import functools
import jax
import jax.numpy as jnp
from jax import lax
from jax.experimental import pallas as pl
from jax.experimental.pallas import tpu as pltpu
from jax.sharding import PartitionSpec as P

BF = jnp.bfloat16
F32 = jnp.float32
VMEM_LIMIT = 56 * 1024 * 1024
VMEM_SMALL = 24 * 1024 * 1024
CHUNK = 256
SLOT = 64
GROUP = 256
LANES = 128
SMALL = 16
CHEAP = pl.CostEstimate(flops=1, bytes_accessed=1, transcendentals=0)
STEP = 10


def whole(a):
    return pl.BlockSpec(a.shape, lambda *_: (0,) * len(a.shape), pipeline_mode=pl.Buffered(1))


def dot(a, b):
    return jnp.dot(a, b, preferred_element_type=F32)


def dot_nt(a, b):
    return lax.dot_general(a, b, (((1,), (1,)), ((), ())), preferred_element_type=F32)


def dot_tn(a, b):
    return lax.dot_general(a, b, (((0,), (0,)), ((), ())), preferred_element_type=F32)


def head_of(shape, dim):
    return lax.broadcasted_iota(jnp.int32, shape, dim) // SLOT


def block_diagonal(state):
    return jnp.where(head_of(state.shape, 0) == head_of(state.shape, 1), state, 0.0).astype(BF)


def only_head(rows, head):
    return jnp.where(head_of(rows.shape, 1) == head, rows, jnp.zeros_like(rows))


def lower(square):
    row = lax.broadcasted_iota(jnp.int32, square.shape, 0)
    col = lax.broadcasted_iota(jnp.int32, square.shape, 1)
    return jnp.where(row >= col, square, 0.0).astype(BF)


def upper(square):
    row = lax.broadcasted_iota(jnp.int32, square.shape, 0)
    col = lax.broadcasted_iota(jnp.int32, square.shape, 1)
    return jnp.where(row <= col, square, 0.0).astype(BF)


def split_dot(ones, values):
    high = values.astype(BF)
    low = (values - high.astype(F32)).astype(BF)
    return dot(ones, high) + dot(ones, low)


def head_sums(values):
    ones = jnp.where(
        head_of((GROUP, GROUP), 0) == head_of((GROUP, GROUP), 1), 1.0, 0.0
    ).astype(BF)
    high = values.astype(BF)
    low = (values - high.astype(F32)).astype(BF)
    return dot(high, ones) + dot(low, ones)


def head_max(values):
    top = None
    head = head_of(values.shape, 1)
    for index in range(GROUP // SLOT):
        mine = jnp.max(jnp.where(head == index, values, -jnp.inf), axis=1, keepdims=True)
        top = mine if top is None else jnp.where(head == index, mine, top)
    return top


def normalise(values):
    centred = values - jnp.mean(values, axis=-1, keepdims=True)
    inv = lax.rsqrt(jnp.mean(centred * centred, axis=-1, keepdims=True) + 1e-05)
    return centred * inv, inv


def normalise_back(grad, unit, inv, gain):
    scaled = grad * gain
    return inv * (
        scaled
        - jnp.mean(scaled, axis=-1, keepdims=True)
        - unit * jnp.mean(scaled * unit, axis=-1, keepdims=True)
    )


def project_kernel(
    pos_ref, x_ref, p0, p1, p2, p3, q_ref, k_ref, v_ref, n_ref, e_ref, eb_ref, z_ref, w_ref, norm_ref, carry
):
    width = x_ref.shape[1]
    part = width // 4

    @pl.when(pl.program_id(0) == 0)
    def _():
        for index, piece in enumerate((p0, p1, p2, p3)):
            rows = pl.ds(pl.multiple_of(pos_ref[index] * part, part), part)
            for m in range(4):
                w_ref[m, rows, :] = piece[m * part : (m + 1) * part, :]
            norm_ref[0:4, rows] = piece[4 * part : 4 * part + 4, 0:part].astype(F32)
        carry[...] = jnp.zeros_like(carry)

    unit, _ = normalise(x_ref[...].astype(F32))
    normed = (unit * norm_ref[0:1, :] + norm_ref[1:2, :]).astype(BF)
    n_ref[...] = normed
    q_ref[...] = dot(normed, w_ref[0]).astype(BF)
    k_ref[...] = dot(normed, w_ref[1]).astype(BF)
    v_ref[...] = dot(normed, w_ref[2]).astype(BF)
    e = jnp.exp(dot(normed, w_ref[3]))
    e_ref[...] = e
    eb_ref[...] = e.astype(BF)
    rows = e.shape[0]
    ones = lower(jnp.ones((rows, rows), F32))
    z = split_dot(ones, e) + carry[0:1, :]
    z_ref[...] = z
    carry[0:1, :] = z[rows - 1 : rows, :]


def project(pos, x, pieces):
    length, width = x.shape
    steps = length // CHUNK
    rows = lambda dtype: jax.ShapeDtypeStruct((length, width), dtype)
    block = pl.BlockSpec((CHUNK, width), lambda i: (i, 0))
    return pl.pallas_call(
        project_kernel,
        grid=(steps,),
        in_specs=[pl.BlockSpec(memory_space=pltpu.SMEM), block] + [whole(p) for p in pieces],
        out_specs=[block] * 7
        + [
            whole(jax.ShapeDtypeStruct((4, width, width), BF)),
            whole(jax.ShapeDtypeStruct((8, width), F32)),
        ],
        out_shape=[rows(BF), rows(BF), rows(BF), rows(BF), rows(F32), rows(BF), rows(F32)]
        + [jax.ShapeDtypeStruct((4, width, width), BF), jax.ShapeDtypeStruct((8, width), F32)],
        scratch_shapes=[pltpu.VMEM((8, width), F32)],
        compiler_params=pltpu.CompilerParams(
            dimension_semantics=("arbitrary",), vmem_limit_bytes=VMEM_LIMIT
        ),
        name="project",
        cost_estimate=CHEAP,
    )(pos, x, *pieces)


def mix_kernel(q_ref, k_ref, v_ref, e_ref, z_ref, o_ref, w_ref, s_ref, keys_ref, values_ref, keys, values):
    @pl.when(pl.program_id(1) == 0)
    def _():
        keys[...] = jnp.zeros_like(keys)
        values[...] = jnp.zeros_like(values)

    q, k, v, e = q_ref[...], k_ref[...], v_ref[...], e_ref[...]
    inv = 1.0 / z_ref[...]
    heads = GROUP // SLOT
    es = [only_head(e, h) for h in range(heads)]
    key_state = block_diagonal(keys[...])
    value_state = block_diagonal(values[...])
    keys_ref[0, 0] = key_state
    values_ref[0, 0] = value_state
    total = dot(q, key_state)
    for h in range(heads):
        total += dot(lower(dot_nt(q, only_head(k, h))), es[h])
    scores = total * inv * 0.125
    s_ref[...] = scores
    raised = jnp.exp(scores - head_max(scores))
    weights = raised / head_sums(raised)
    w_ref[...] = weights
    ratio = (weights * inv).astype(BF)
    out = dot(ratio, value_state)
    for h in range(heads):
        out += dot(lower(dot_nt(ratio, es[h])), only_head(v, h))
    o_ref[...] = out.astype(BF)
    keys[...] += dot_tn(k, e)
    values[...] += dot_tn(e, v)


def mix(q, k, v, e, z):
    length, width = q.shape
    steps, groups = length // CHUNK, width // GROUP
    block = pl.BlockSpec((CHUNK, GROUP), lambda g, i: (i, g))
    state = pl.BlockSpec((1, 1, GROUP, GROUP), lambda g, i: (g, i, 0, 0))
    rows = lambda dtype: jax.ShapeDtypeStruct((length, width), dtype)
    states = jax.ShapeDtypeStruct((groups, steps, GROUP, GROUP), BF)
    return pl.pallas_call(
        mix_kernel,
        grid=(groups, steps),
        in_specs=[block] * 5,
        out_specs=[block] * 3 + [state] * 2,
        out_shape=[rows(BF), rows(F32), rows(F32), states, states],
        scratch_shapes=[pltpu.VMEM((GROUP, GROUP), F32)] * 2,
        compiler_params=pltpu.CompilerParams(
            dimension_semantics=("arbitrary", "arbitrary"), vmem_limit_bytes=VMEM_LIMIT
        ),
        name="mix",
        cost_estimate=CHEAP,
    )(q, k, v, e, z)


def mix_back_kernel(
    g_ref, q_ref, k_ref, v_ref, eb_ref, e_ref, z_ref, w_ref, s_ref, keys_ref, values_ref,
    dq_ref, dk_ref, dv_ref, dc_ref, later_v, later_k, carry
):
    @pl.when(pl.program_id(0) == 0)
    def _():
        later_v[...] = jnp.zeros_like(later_v)
        later_k[...] = jnp.zeros_like(later_k)
        carry[...] = jnp.zeros_like(carry)

    g, q, k, v, e = g_ref[...], q_ref[...], k_ref[...], v_ref[...], eb_ref[...]
    inv = 1.0 / z_ref[...]
    weights = w_ref[...]
    ratio = (weights * inv).astype(BF)
    heads = GROUP // SLOT
    es = [only_head(e, h) for h in range(heads)]
    state = block_diagonal(later_v[...])
    d_ratio = dot_nt(g, values_ref[0, 0])
    dv = dot(e, state)
    de = dot_nt(v, state)
    for h in range(heads):
        vh = only_head(v, h)
        d_ratio += dot(lower(dot_nt(g, vh)), es[h])
        de += dot(upper(dot_nt(vh, g)), only_head(ratio, h))
        dv += dot(upper(dot_nt(es[h], ratio)), only_head(g, h))
    dv_ref[...] = dv.astype(BF)
    d_weights = d_ratio * inv
    both = d_weights * weights
    d_scores = weights * (d_weights - head_sums(both))
    dn = (d_scores * inv * 0.125).astype(BF)
    dz = -(both + d_scores * s_ref[...]) * inv
    state = block_diagonal(later_k[...])
    dq = dot_nt(dn, keys_ref[0, 0])
    dk = dot(e, state)
    de += dot_nt(k, state)
    for h in range(heads):
        kh = only_head(k, h)
        dq += dot(lower(dot_nt(dn, es[h])), kh)
        dk += dot(upper(dot_nt(es[h], dn)), only_head(q, h))
        de += dot(upper(dot_nt(kh, q)), only_head(dn, h))
    dq_ref[...] = dq.astype(BF)
    dk_ref[...] = dk.astype(BF)
    rows = dz.shape[0]
    ones = upper(jnp.ones((rows, rows), F32))
    z_sum = split_dot(ones, dz) + carry[0:1, :]
    carry[0:1, :] = z_sum[0:1, :]
    dc_ref[...] = ((de + z_sum) * e_ref[...]).astype(BF)
    later_v[...] += dot_tn(ratio, g)
    later_k[...] += dot_tn(dn, q)


def mix_back(group, g, q, k, v, eb, e, z, w, s, keys, values):
    length, width = q.shape
    steps = length // CHUNK
    block = pl.BlockSpec((CHUNK, GROUP), lambda i: (steps - 1 - i, group))
    state = pl.BlockSpec((1, 1, GROUP, GROUP), lambda i: (group, steps - 1 - i, 0, 0))
    out = pl.BlockSpec((CHUNK, GROUP), lambda i: (steps - 1 - i, 0))
    rows = jax.ShapeDtypeStruct((length, GROUP), BF)
    return pl.pallas_call(
        mix_back_kernel,
        grid=(steps,),
        in_specs=[block] * 9 + [state] * 2,
        out_specs=[out] * 4,
        out_shape=[rows] * 4,
        scratch_shapes=[pltpu.VMEM((GROUP, GROUP), F32)] * 2 + [pltpu.VMEM((8, GROUP), F32)],
        compiler_params=pltpu.CompilerParams(
            dimension_semantics=("arbitrary",), vmem_limit_bytes=VMEM_LIMIT
        ),
        name="mix_back",
        cost_estimate=CHEAP,
    )(g, q, k, v, eb, e, z, w, s, keys, values)


def scatter_unit(place_ref, grads, first, unit, shard, target, table):
    count = place_ref.shape[1] // 2
    part = LANES
    rows = part // count
    height = target.shape[0] // (2 * count)
    for d in range(count):
        place = place_ref[table, (shard // 2) * count + d]
        where = pl.ds(pl.multiple_of(place * height + unit * rows, rows), rows)
        target[where, :] = grads[pl.ds(pl.multiple_of(first + d * rows, rows), rows), :]


def scatter_shards(pos_ref, place_ref, grads, send_ref, keep_ref, unit):
    for index in range(4):
        pos = pos_ref[index]
        target = send_ref if index % 2 else keep_ref
        scatter_unit(place_ref, grads, pos * LANES, unit, pos, target, index % 2)


def feed_kernel(
    pos_ref, place_ref, factor_ref, x_ref, g_ref, o_ref, norm_ref, p0, p1, p2, p3,
    y_ref, dh_ref, do_ref, send_ref, keep_ref, dnorm_ref,
    wo, w1, w2, branch, unit_ref, inv_ref, n2, gb, n2_t, gb_t, dn2, grads
):
    step = pl.program_id(0)
    last = pl.num_programs(0) - 1
    length, width = x_ref.shape
    part = width // 4
    block = w1.shape[2]
    tiles = length // 256

    @pl.when(step == 0)
    def _():
        for index, piece in enumerate((p0, p1, p2, p3)):
            pos = pos_ref[index]
            rows = pl.ds(pl.multiple_of(pos * part, part), part)
            wo[rows, :] = piece[0:part, :]
            for j in range(4):
                w1[j, rows, :] = piece[(j + 1) * part : (j + 2) * part, :]
            w2[pos] = piece[5 * part : 5 * part + block, :]

        def before(i, _):
            rows = pl.ds(pl.multiple_of(i * 256, 256), 256)
            h1 = x_ref[rows, :].astype(F32) + dot(o_ref[rows, :], wo[...])
            branch[rows, :] = h1
            unit, inv = normalise(h1)
            unit_ref[rows, :] = unit
            inv_ref[rows, :] = jnp.broadcast_to(inv, (256, 128))
            normed = (unit * norm_ref[2:3, :] + norm_ref[3:4, :]).astype(BF)
            n2[rows, :] = normed
            n2_t[:, rows] = normed.T
            grad = (g_ref[rows, :].astype(F32) * factor_ref[0]).astype(BF)
            gb[rows, :] = grad
            gb_t[:, rows] = grad.T
            dn2[rows, :] = jnp.zeros((256, width), F32)
            return 0

        lax.fori_loop(0, tiles, before, 0)

    up = w1[step]
    down = w2[step]
    up_grad = jnp.zeros((width, block), F32)
    down_grad = jnp.zeros((width, block), F32)
    for i in range(tiles):
        rows = slice(i * 256, (i + 1) * 256)
        a = dot(n2[rows, :], up)
        inner = 0.7978845608 * (a + 0.044715 * a * a * a)
        t = jnp.tanh(inner)
        u = (0.5 * a * (1.0 + t)).astype(BF)
        slope = 0.5 * (1.0 + t) + 0.5 * a * (1.0 - t * t) * (
            0.7978845608 + (3.0 * 0.044715 * 0.7978845608) * a * a
        )
        da = (dot_nt(gb[rows, :], down) * slope).astype(BF)
        branch[rows, :] += dot(u, down)
        dn2[rows, :] += dot_nt(da, up)
        up_grad += dot(n2_t[:, rows], da)
        down_grad += dot(gb_t[:, rows], u)
    grads[...] = up_grad.astype(BF)
    scatter_shards(pos_ref, place_ref, grads, send_ref, keep_ref, step + 1)
    grads[...] = down_grad.astype(BF)
    mine = (step ^ pos_ref[0]) & 1 == 0

    @pl.when(mine)
    def _():
        for u in range(4):
            scatter_unit(place_ref, grads, u * part, 5 + u, step, keep_ref, 0)

    @pl.when(jnp.logical_not(mine))
    def _():
        for u in range(4):
            scatter_unit(place_ref, grads, u * part, 5 + u, step, send_ref, 1)

    @pl.when(step == last)
    def _():
        gain = norm_ref[2:3, :]

        def after(i, sums):
            rows = pl.ds(pl.multiple_of(i * 256, 256), 256)
            y_ref[rows, :] = branch[rows, :].astype(BF)
            grad = dn2[rows, :]
            unit = unit_ref[rows, :]
            dh = g_ref[rows, :].astype(F32) * factor_ref[0] + normalise_back(
                grad, unit, inv_ref[rows, 0:1], gain
            )
            dh_ref[rows, :] = dh
            dh_low = dh.astype(BF)
            do_ref[rows, :] = dot_nt(dh_low, wo[...]).astype(BF)
            return (
                sums[0] + jnp.sum(grad * unit, axis=0, keepdims=True),
                sums[1] + jnp.sum(grad, axis=0, keepdims=True),
                sums[2] + dot_tn(o_ref[rows, :], dh_low),
            )

        empty = jnp.zeros((1, width), F32)
        sums = lax.fori_loop(0, tiles, after, (empty, empty, jnp.zeros((width, width), F32)))
        dnorm_ref[...] = jnp.zeros_like(dnorm_ref)
        dnorm_ref[0:1, :] = sums[0]
        dnorm_ref[1:2, :] = sums[1]
        grads[...] = sums[2].astype(BF)
        scatter_shards(pos_ref, place_ref, grads, send_ref, keep_ref, 0)


def feed(pos, place, factor, x, g, o, norm, pieces):
    length, width = x.shape
    block = width
    height = 5 * (width // 4) + block
    rows = lambda dtype: jax.ShapeDtypeStruct((length, width), dtype)
    out = [
        rows(BF), rows(F32), rows(BF),
        jax.ShapeDtypeStruct((2 * height, width), BF),
        jax.ShapeDtypeStruct((2 * height, width), BF),
        jax.ShapeDtypeStruct((8, width), F32),
    ]
    args = (x, g, o, norm) + tuple(pieces)
    return pl.pallas_call(
        feed_kernel,
        grid=(4,),
        in_specs=[pl.BlockSpec(memory_space=pltpu.SMEM)] * 3 + [whole(a) for a in args],
        out_specs=[whole(a) for a in out],
        out_shape=out,
        scratch_shapes=[
            pltpu.VMEM((width, width), BF),
            pltpu.VMEM((4, width, block), BF),
            pltpu.VMEM((4, block, width), BF),
            pltpu.VMEM((length, width), F32),
            pltpu.VMEM((length, width), F32),
            pltpu.VMEM((length, 128), F32),
            pltpu.VMEM((length, width), BF),
            pltpu.VMEM((length, width), BF),
            pltpu.VMEM((width, length), BF),
            pltpu.VMEM((width, length), BF),
            pltpu.VMEM((length, width), F32),
            pltpu.VMEM((width, block), BF),
        ],
        compiler_params=pltpu.CompilerParams(
            dimension_semantics=("arbitrary",), vmem_limit_bytes=VMEM_LIMIT
        ),
        name="feed",
        cost_estimate=CHEAP,
    )(pos, place, factor, *args)


def weight_back_kernel(pos_ref, place_ref, n_ref, *refs):
    grads_in, (send_ref, keep_ref, n_t, grads) = refs[:8], refs[8:]
    step = pl.program_id(0)

    @pl.when(step == 0)
    def _():
        n_t[...] = n_ref[...].T

    for m in range(4):
        @pl.when(step == m)
        def _():
            for half in range(2):
                cols = slice(half * GROUP, (half + 1) * GROUP)
                grads[:, cols] = dot(n_t[...], grads_in[half * 4 + m][...]).astype(BF)

    scatter_shards(pos_ref, place_ref, grads, send_ref, keep_ref, step)


def weight_back(pos, place, n, halves):
    length, width = n.shape
    out = jax.ShapeDtypeStruct((2 * width, width), BF)
    args = (n,) + tuple(halves)
    return pl.pallas_call(
        weight_back_kernel,
        grid=(4,),
        in_specs=[pl.BlockSpec(memory_space=pltpu.SMEM)] * 2 + [whole(a) for a in args],
        out_specs=[whole(out)] * 2,
        out_shape=[out] * 2,
        scratch_shapes=[pltpu.VMEM((width, length), BF), pltpu.VMEM((width, width), BF)],
        compiler_params=pltpu.CompilerParams(
            dimension_semantics=("arbitrary",), vmem_limit_bytes=VMEM_SMALL
        ),
        name="weight_back",
        cost_estimate=CHEAP,
    )(pos, place, *args)


def input_back_kernel(x_ref, dh_ref, w_ref, norm_ref, dnorm_ref, *refs):
    grads_in, (dx_ref, small_ref, sums) = refs[:8], refs[8:]
    step = pl.program_id(0)

    @pl.when(step == 0)
    def _():
        sums[...] = jnp.zeros_like(sums)

    dn = None
    for m in range(4):
        for half in range(2):
            cols = slice(half * GROUP, (half + 1) * GROUP)
            term = dot_nt(grads_in[half * 4 + m][...], w_ref[m, :, cols])
            dn = term if dn is None else dn + term
    unit, inv = normalise(x_ref[...].astype(F32))
    dx_ref[...] = dh_ref[...] + normalise_back(dn, unit, inv, norm_ref[0:1, :])
    sums[0:1, :] += jnp.sum(dn * unit, axis=0, keepdims=True)
    sums[1:2, :] += jnp.sum(dn, axis=0, keepdims=True)

    @pl.when(step == pl.num_programs(0) - 1)
    def _():
        small_ref[...] = jnp.concatenate(
            [sums[0:2, :], dnorm_ref[0:2, :], jnp.zeros((SMALL - 4, sums.shape[1]), F32)], axis=0
        ).astype(BF)


def input_back(x, dh, w, norm, dnorm, halves):
    length, width = x.shape
    tile = 256
    block = pl.BlockSpec((tile, width), lambda i: (i, 0))
    thin = pl.BlockSpec((tile, GROUP), lambda i: (i, 0))
    small = jax.ShapeDtypeStruct((SMALL, width), BF)
    return pl.pallas_call(
        input_back_kernel,
        grid=(length // tile,),
        in_specs=[block] * 2 + [whole(w), whole(norm), whole(dnorm)] + [thin] * 8,
        out_specs=[block, whole(small)],
        out_shape=[jax.ShapeDtypeStruct((length, width), F32), small],
        scratch_shapes=[pltpu.VMEM((8, width), F32)],
        compiler_params=pltpu.CompilerParams(
            dimension_semantics=("arbitrary",), vmem_limit_bytes=VMEM_SMALL
        ),
        name="input_back",
        cost_estimate=CHEAP,
    )(x, dh, w, norm, dnorm, *halves)


def bits_of(size):
    return [1 << b for b in range(size.bit_length() - 1)]


def split_bits():
    return bits_of(lax.axis_size("dp"))[:3]


def exchange(values, even, odd):
    dp, shard = lax.axis_size("dp"), lax.axis_size("shard")
    perm = []
    for d in range(dp):
        for s in range(shard):
            axis, bit = odd if s % 2 else even
            other = (d ^ bit, s) if axis == "dp" else (d, s ^ bit)
            perm.append((d * shard + s, other[0] * shard + other[1]))
    return lax.ppermute(values, ("dp", "shard"), perm)


def swap(values, axis, bit):
    return exchange(values, (axis, bit), (axis, bit))


def after(values, *others):
    return lax.optimization_barrier((values,) + others)[0]


def places():
    count = 2 ** len(split_bits())
    dp, shard = lax.axis_index("dp"), lax.axis_index("shard")
    piece = jnp.arange(2 * count, dtype=jnp.int32)
    far = (piece // count) ^ (shard // 2)
    along = (piece % count) ^ (dp % count)
    order = 0
    for b in range(len(split_bits())):
        order = order * 2 + ((along >> b) & 1)
    even, odd = far * count + order, order * 2 + far
    mine = shard % 2
    return jnp.stack(
        [jnp.where(mine == 0, even, odd), jnp.where(mine == 0, odd, even)]
    ).astype(jnp.int32)


def phases():
    split = [("dp", b) for b in split_bits()]
    return list(zip([("shard", 2)] + split, split + [("shard", 2)]))


def add_up(parts, low, high):
    total = parts[0][low:high].astype(F32)
    for part in parts[1:]:
        total = total + part[low:high].astype(F32)
    return total.astype(BF)


def add_rest(piece):
    for b in bits_of(lax.axis_size("dp"))[3:]:
        piece = add_up([piece, swap(piece, "dp", b)], 0, piece.shape[0])
    return piece


def gather_plan():
    split = split_bits()
    even = [split[0]] + split[1:][::-1]
    odd = split[::-1]
    return [(("dp", a), ("dp", b)) for a, b in zip(even, odd)]


def gather_index():
    odd = lax.axis_index("shard") % 2
    mask = jnp.zeros((1,), jnp.int32)
    for (_, even_bit), (_, odd_bit) in gather_plan():
        mask = jnp.concatenate([mask, mask | jnp.where(odd == 1, odd_bit, even_bit)])
    return (lax.axis_index("dp") % mask.shape[0]) ^ mask


def adam(master, first, second, grad, rate, decay):
    first_new = 0.5 * first + 0.5 * grad
    second_new = 0.5 * second + 0.5 * grad * grad
    correction = 1.0 - 0.5**STEP
    update = first_new / correction / (jnp.sqrt(second_new / correction) + 1e-08)
    return master - rate * (update + decay * master), first_new, second_new


def update_kernel(index_ref, factor_ref, early_ref, late_ref, gn_ref, *refs, states):
    am, af, as_, um, uf, us, dm, df, ds, nm, nf, ns = refs[:12]
    early, late = refs[-2:]
    outs = refs[12:-2]
    step = pl.program_id(0)
    factor = factor_ref[0]
    width = early.shape[1]
    part = late.shape[0] // 4
    blocks = um.shape[1] // width
    height = part // pl.num_programs(0)

    def keep(group, where, unit, size, new):
        if states:
            for target, value in zip(outs[3 * group : 3 * group + 3], new):
                target[where] = value
        else:
            rows = pl.ds(pl.multiple_of(unit * part + step * size, size), size)
            outs[0][rows, :] = new[0].astype(BF)

    @pl.when(step == 0)
    def _():
        count = index_ref.shape[0]
        rows = part // count
        for source, target in ((early_ref, early), (late_ref, late)):
            units = target.shape[0] // part
            for j in range(count):
                for u in range(units):
                    place = pl.ds(pl.multiple_of(u * part + index_ref[j] * rows, rows), rows)
                    first = (j * units + u) * rows
                    target[place, :] = source[first : first + rows, :]
        new = adam(nm[...], nf[...], ns[...], gn_ref[...] * factor, 0.3, 0.0)
        if states:
            outs[9][...], outs[10][...], outs[11][...] = new
        else:
            last = outs[0].shape[0] - SMALL
            outs[0][last:, :] = jnp.zeros((SMALL, width), BF)
            outs[0][last : last + 4, 0:part] = new[0].astype(BF)

    def span(base, size):
        return pl.ds(pl.multiple_of(base + step * size, size), size)

    for m in range(5):
        source = late[span(m * part, height), :] if m < 4 else early[span(0, height), :]
        new = adam(am[m], af[m], as_[m], source.astype(F32) * factor, 0.05, 0.01)
        keep(0, (m, slice(None), slice(None)), m, height, new)
    for j in range(blocks):
        source = early[span((j + 1) * part, height), :]
        cols = (slice(None), slice(j * width, (j + 1) * width))
        new = adam(um[cols], uf[cols], us[cols], source.astype(F32) * factor, 0.05, 0.01)
        keep(1, cols, 5 + j, height, new)
    tall = dm.shape[0]
    source = early[(blocks + 1) * part :, span(0, tall)].astype(F32).T
    new = adam(dm[...], df[...], ds[...], source * factor, 0.05, 0.01)
    keep(2, (slice(None), slice(None)), 5 + blocks, tall, new)


def update(states, index, factor, early, late, gn, attn, up, down, norm):
    steps = 4
    smem = pl.BlockSpec(memory_space=pltpu.SMEM)
    five, part, width = attn[0].shape
    specs = (
        [pl.BlockSpec((five, part // steps, width), lambda i: (0, i, 0))] * 3
        + [pl.BlockSpec((part // steps, up[0].shape[1]), lambda i: (i, 0))] * 3
        + [pl.BlockSpec((down[0].shape[0] // steps, width), lambda i: (i, 0))] * 3
        + [whole(norm[0])] * 3
    )
    arrays = tuple(attn) + tuple(up) + tuple(down) + tuple(norm)
    copy = jax.ShapeDtypeStruct((early.shape[0] + late.shape[0] + SMALL, width), BF)
    return pl.pallas_call(
        functools.partial(update_kernel, states=states),
        grid=(steps,),
        in_specs=[smem, smem, whole(early), whole(late), whole(gn)] + specs,
        out_specs=specs if states else [whole(copy)],
        out_shape=[jax.ShapeDtypeStruct(a.shape, F32) for a in arrays] if states else [copy],
        scratch_shapes=[pltpu.VMEM(early.shape, BF), pltpu.VMEM(late.shape, BF)],
        compiler_params=pltpu.CompilerParams(
            dimension_semantics=("arbitrary",), vmem_limit_bytes=VMEM_LIMIT
        ),
        name="update" if states else "renew",
        cost_estimate=CHEAP,
    )(index, factor, early, late, gn, *arrays)


def place_units(pos, piece, first, units, attn_ref, up_ref, down_ref, sems, start):
    width = attn_ref.shape[2]
    part = LANES
    blocks = up_ref.shape[1] // width
    tall = down_ref.shape[0] // 4
    found = []
    for j, unit in enumerate(units):
        source = piece.at[pl.ds(first + j * part, part), :]
        rows = pl.ds(pl.multiple_of(pos * part, part), part)
        if unit < 5:
            target = attn_ref.at[unit, rows, :]
        elif unit < 5 + blocks:
            target = up_ref.at[rows, pl.ds((unit - 5) * width, width)]
        else:
            base = pl.multiple_of(pos * tall + (unit - 5 - blocks) * part, part)
            target = down_ref.at[pl.ds(base, part), :]
        found.append(pltpu.make_async_copy(source, target, sems.at[start + j]))
    return found


def unpack_near_kernel(pos_ref, p0, p1, attn_ref, up_ref, down_ref, sems):
    units = list(range(p0.shape[0] // LANES))
    copies = place_units(pos_ref[0], p0, 0, units, attn_ref, up_ref, down_ref, sems, 0)
    copies += place_units(pos_ref[1], p1, 0, units, attn_ref, up_ref, down_ref, sems, len(units))
    for copy in copies:
        copy.start()
    for copy in copies:
        copy.wait()


def unpack_far_kernel(pos_ref, half_ref, *refs):
    pieces, (attn_ref, up_ref, down_ref, sems) = refs[:6], refs[9:]
    units = list(range((pieces[0].shape[0] * 2 + pieces[2].shape[0]) // LANES))
    low = pieces[0].shape[0] // LANES
    for side in range(2):
        @pl.when(half_ref[0] == side)
        def _():
            copies = []
            for shift in range(2):
                pos = pos_ref[2 + shift]
                group = pieces[3 * shift : 3 * shift + 3]
                for part, piece in zip((side, 1 - side), group[:2]):
                    copies += place_units(
                        pos, piece, 0, units[part * low : (part + 1) * low],
                        attn_ref, up_ref, down_ref, sems, len(copies),
                    )
                copies += place_units(
                    pos, group[2], 0, units[2 * low :],
                    attn_ref, up_ref, down_ref, sems, len(copies),
                )
            for copy in copies:
                copy.start()
            for copy in copies:
                copy.wait()


def share_copies(pos, own, other_work, width, hidden):
    units = own.shape[0] // LANES
    low = 4 * LANES
    half = (lax.axis_index("dp") % 2).astype(jnp.int32)[None]
    near = swap(own, "shard", 1)
    ours = lax.dynamic_slice(own, (half[0] * low, 0), (low, width))
    far_a = swap(ours, "shard", 2)
    far_c = swap(after(own[2 * low :], far_a), "shard", 2)
    far_b = swap(far_a, "dp", 1)
    hbm = pl.BlockSpec(memory_space=pl.ANY)
    vmem = pl.BlockSpec(memory_space=pltpu.VMEM)
    smem = pl.BlockSpec(memory_space=pltpu.SMEM)
    shapes = [
        jax.ShapeDtypeStruct((5, width, width), BF),
        jax.ShapeDtypeStruct((width, hidden), BF),
        jax.ShapeDtypeStruct((hidden, width), BF),
    ]
    params = pltpu.CompilerParams(vmem_limit_bytes=VMEM_SMALL)
    begun = list(pl.pallas_call(
        unpack_near_kernel,
        in_specs=[smem, vmem, vmem],
        out_specs=[hbm] * 3,
        out_shape=shapes,
        scratch_shapes=[pltpu.SemaphoreType.DMA((2 * units,))],
        compiler_params=params,
        name="unpack_near",
        cost_estimate=CHEAP,
    )(pos, own, near))
    far = [far_a, far_b, far_c]
    across = [swap(f, "shard", 1) for f in far[:2]]
    across.append(swap(after(far[2], other_work, *across), "shard", 1))
    done = pl.pallas_call(
        unpack_far_kernel,
        in_specs=[smem, smem] + [vmem] * 6 + [hbm] * 3,
        out_specs=[hbm] * 3,
        out_shape=shapes,
        scratch_shapes=[pltpu.SemaphoreType.DMA((2 * units,))],
        input_output_aliases={8: 0, 9: 1, 10: 2},
        compiler_params=params,
        name="unpack_far",
        cost_estimate=CHEAP,
    )(pos, half, *far, *across, *begun)
    last = units * LANES
    norms = [p[last : last + 4, :LANES] for p in (own, near)] + [
        p[p.shape[0] - SMALL : p.shape[0] - SMALL + 4, :LANES] for p in (far[2], across[2])
    ]
    low_bit, high_bit = pos[0] % 2 == 1, pos[0] // 2 == 1
    a, b, c, d = norms
    a, b, c, d = [jnp.where(low_bit, v, u) for u, v in ((a, b), (b, a), (c, d), (d, c))]
    a, b, c, d = [jnp.where(high_bit, v, u) for u, v in ((a, c), (b, d), (c, a), (d, b))]
    return tuple(done) + (jnp.concatenate([a, b, c, d], axis=1),)


def gather_shard(own):
    across = swap(own, "shard", 2)
    return own, swap(own, "shard", 1), across, swap(across, "shard", 1)


def shards(
    tokens, out_grad, domain_ids, domain_weight,
    attn_master, attn_first, attn_second,
    up_master, up_first, up_second,
    down_master, down_first, down_second,
    norm_master, norm_first, norm_second,
):
    width = tokens.shape[1]
    hidden = up_master.shape[1]
    part = width // 4
    blocks = hidden // width
    dp = lax.axis_index("dp")
    shard = lax.axis_index("shard").astype(jnp.int32)
    pos = shard ^ jnp.arange(4, dtype=jnp.int32)
    place = places()

    small = jnp.pad(norm_master.astype(BF), ((0, SMALL - 4), (0, width - part)))
    first = gather_shard(
        jnp.concatenate([attn_master[:4].astype(BF).reshape(4 * part, width), small])
    )

    domains = domain_weight.shape[0]
    onehot = (domain_ids[:, None] == jnp.arange(domains, dtype=jnp.int32)[None, :]).astype(F32)
    counts = jnp.sum(onehot, axis=0)
    for b in bits_of(lax.axis_size("dp")):
        counts = counts + swap(counts, "dp", b)
    counts_row = jnp.pad(counts.astype(BF)[None], ((0, SMALL - 1), (0, width - domains)))
    second = after(
        jnp.concatenate(
            [attn_master[4].astype(BF)]
            + [up_master[:, j * width : (j + 1) * width].astype(BF) for j in range(blocks)]
            + [down_master.astype(BF), counts_row]
        ),
        first[2],
    )
    across = swap(second, "shard", 2)
    q, k, v, n, e, eb, z, w, norm = project(pos, tokens, first)
    o, weights, scores, keys, values = mix(q, k, v, eb, z)
    second = (
        second, swap(second, "shard", 1), across, swap(after(across, o), "shard", 1)
    )
    total_seqs = lax.axis_size("dp") * lax.axis_size("shard") * domain_ids.shape[0]
    last = second[0].shape[0] - SMALL
    counts = sum(piece[last, :domains].astype(F32) for piece in second)
    per_domain = domain_weight * total_seqs / (domains * jnp.maximum(counts, 1.0))
    seq_weight = jnp.sum(onehot * per_domain[None, :], axis=1)

    y, dh, do, send, keep, dnorm = feed(pos, place, seq_weight, tokens, out_grad, o, norm, second)

    steps = phases()
    early = [keep, swap(send, "shard", 1)]
    pieces = 2 ** len(steps)
    rows = keep.shape[0] // pieces

    def forward_phase(parts, phase, rows):
        low = rows * pieces >> (phase + 1)
        return add_up(parts, low, 2 * low)

    saved = (q, k, v, eb, e, z, weights, scores, keys, values)
    back = list(mix_back(0, do, *saved))
    out = after(forward_phase(early, 0, rows), back[0])
    early.append(exchange(out, *steps[0]))
    back += mix_back(1, after(do, out), *saved)
    out = after(forward_phase(early, 1, rows), back[4])
    early.append(exchange(out, *steps[1]))
    send, keep = weight_back(pos, place, after(n, out), back)
    late = [keep, swap(send, "shard", 1)]
    out = forward_phase(early, 2, rows)
    early.append(exchange(out, *steps[2]))
    dx, small = input_back(tokens, after(dh, out), w, norm, dnorm, back)
    small = add_up([small, swap(small, "shard", 1)], 0, SMALL)
    thin = keep.shape[0] // pieces
    for phase in range(len(steps)):
        if phase >= 3:
            early.append(exchange(forward_phase(early, phase, rows), *steps[phase]))
        out = forward_phase(late, phase, thin)
        got = exchange(jnp.concatenate([out, small]), *steps[phase])
        late.append(got)
        small = add_up([small, got[out.shape[0] :]], 0, SMALL)
    early = add_rest(add_up(early, 0, rows))
    late = add_rest(jnp.concatenate([add_up(late, 0, thin), small]))
    late, small = late[:thin], late[thin:]
    norm_grad = lax.dynamic_slice(small[:4], (0, shard * part), (4, part)).astype(F32)
    for step in gather_plan():
        early = jnp.concatenate([early, exchange(early, *step)])
        late = jnp.concatenate([late, exchange(late, *step)])
    square = sum(jnp.sum(jnp.square(part.astype(F32))) for part in (early, late, norm_grad))[None]
    for b in (1, 2):
        square = square + swap(square, "shard", b)
    index = gather_index()
    clip_norm = jnp.sqrt(square)
    factor = jnp.minimum(1.0, 1.0 / (clip_norm + 1e-06))
    inputs = (
        index, factor, early, late, norm_grad,
        (attn_master, attn_first, attn_second),
        (up_master, up_first, up_second),
        (down_master, down_first, down_second),
        (norm_master, norm_first, norm_second),
    )
    (own,) = update(False, *inputs)
    new = update(True, *inputs)
    copies = share_copies(pos, own, new[0], width, hidden)
    return (y, dx) + tuple(new) + (clip_norm[0],) + tuple(copies)


def solution(mesh):
    rows = P(("dp", "shard"), None)
    attn = (P(None, "shard", None),) * 3
    tall = (P("shard", None),) * 6
    norm = (P(None, "shard"),) * 3
    return jax.shard_map(
        shards,
        mesh=mesh,
        in_specs=(rows, rows, P(("dp", "shard")), P()) + attn + tall + norm,
        out_specs=(rows, rows) + attn + tall + norm + (P(),) * 5,
        check_vma=False,
    )
```

```python
import functools
import jax
import jax.numpy as jnp
from jax import lax
from jax.experimental import pallas as pl
from jax.experimental.pallas import tpu as pltpu
from jax.sharding import PartitionSpec as P

BF = jnp.bfloat16
F32 = jnp.float32
VMEM_LIMIT = 56 * 1024 * 1024
VMEM_SMALL = 24 * 1024 * 1024
CHUNK = 256
SLOT = 64
GROUP = 256
LANES = 128
SMALL = 16
CHEAP = pl.CostEstimate(flops=1, bytes_accessed=1, transcendentals=0)
STEP = 10
TILE = 512
COUNTS = (1, 2, 1)


def whole(a):
    return pl.BlockSpec(a.shape, lambda *_: (0,) * len(a.shape), pipeline_mode=pl.Buffered(1))


def dot(a, b):
    return jnp.dot(a, b, preferred_element_type=F32)


def dot_nt(a, b):
    return lax.dot_general(a, b, (((1,), (1,)), ((), ())), preferred_element_type=F32)


def dot_tn(a, b):
    return lax.dot_general(a, b, (((0,), (0,)), ((), ())), preferred_element_type=F32)


def head_of(shape, dim):
    return lax.broadcasted_iota(jnp.int32, shape, dim) // SLOT


def block_diagonal(state):
    return jnp.where(head_of(state.shape, 0) == head_of(state.shape, 1), state, 0.0).astype(BF)


def only_head(rows, head):
    return jnp.where(head_of(rows.shape, 1) == head, rows, jnp.zeros_like(rows))


def by_head(rows):
    return jnp.concatenate([only_head(rows, h) for h in range(GROUP // SLOT)], axis=0)


def lower(square):
    size = square.shape[0]
    row = lax.broadcasted_iota(jnp.int16, (size, size), 0)
    col = lax.broadcasted_iota(jnp.int16, (size, size), 1)
    return jnp.concatenate(
        [
            jnp.where(row >= col, square[:, first : first + size].astype(BF), jnp.zeros((), BF))
            for first in range(0, square.shape[1], size)
        ],
        axis=1,
    )


def upper(square):
    size = square.shape[1]
    row = lax.broadcasted_iota(jnp.int16, (size, size), 0)
    col = lax.broadcasted_iota(jnp.int16, (size, size), 1)
    return jnp.concatenate(
        [
            jnp.where(row <= col, square[first : first + size, :].astype(BF), jnp.zeros((), BF))
            for first in range(0, square.shape[0], size)
        ],
        axis=1,
    )


def split_dot(ones, values):
    high = values.astype(BF)
    low = (values - high.astype(F32)).astype(BF)
    return dot(ones, high) + dot(ones, low)


def head_ones():
    return jnp.where(
        head_of((GROUP, GROUP), 0) == head_of((GROUP, GROUP), 1), 1.0, 0.0
    ).astype(BF)


def head_sums(values):
    ones = head_ones()
    high = values.astype(BF)
    low = (values - high.astype(F32)).astype(BF)
    return dot(high, ones) + dot(low, ones)


def head_max(values):
    top = None
    head = head_of(values.shape, 1)
    for index in range(GROUP // SLOT):
        mine = jnp.max(jnp.where(head == index, values, -jnp.inf), axis=1, keepdims=True)
        top = mine if top is None else jnp.where(head == index, mine, top)
    return top


def normalise(values):
    centred = values - jnp.mean(values, axis=-1, keepdims=True)
    inv = lax.rsqrt(jnp.mean(centred * centred, axis=-1, keepdims=True) + 1e-05)
    return centred * inv, inv


def normalise_back(grad, unit, inv, gain):
    scaled = grad * gain
    return inv * (
        scaled
        - jnp.mean(scaled, axis=-1, keepdims=True)
        - unit * jnp.mean(scaled * unit, axis=-1, keepdims=True)
    )


def attend_kernel(
    pos_ref, half_ref, x_ref, near0, near1, far0, far1, far2, far3,
    q_ref, k_ref, v_ref, n_ref, e_ref, eb_ref, z_ref, o_ref, w_ref, s_ref, keys_ref, values_ref,
    weights_ref, norm_ref, keys, values, carry
):
    width = x_ref.shape[1]
    part = width // 4

    @pl.when(pl.program_id(0) == 0)
    def _():
        low = far0.shape[0]

        def rows_of(index, first, count):
            if index < 2:
                return (near0, near1)[index][first : first + count, :]
            a, b = ((far0, far1), (far2, far3))[index - 2]
            if first >= low:
                a, b, first = b, a, first - low
            return jnp.where(half_ref[0] == 0, a[first : first + count, :], b[first : first + count, :])

        for index in range(4):
            rows = pl.ds(pl.multiple_of(pos_ref[index] * part, part), part)
            for m in range(4):
                weights_ref[m, rows, :] = rows_of(index, m * part + SMALL * (m > 1), part)
            norm_ref[:, rows] = rows_of(index, 2 * part, SMALL)[0:8, 0:part].astype(F32)
        carry[...] = jnp.zeros_like(carry)
        keys[...] = jnp.zeros_like(keys)
        values[...] = jnp.zeros_like(values)

    heads = range(GROUP // SLOT)
    groups = range(keys.shape[0])
    cols = [slice(i * GROUP, (i + 1) * GROUP) for i in groups]
    unit, _ = normalise(x_ref[...].astype(F32))
    normed = (unit * norm_ref[0:1, :] + norm_ref[1:2, :]).astype(BF)
    n_ref[...] = normed
    rows = normed.shape[0]
    ones = lower(jnp.ones((rows, rows), F32))
    q, k, v, e, inv = [], [], [], [], []
    for c in cols:
        raised = jnp.exp(dot(normed, weights_ref[3, :, c]))
        z = split_dot(ones, raised) + carry[0:1, c]
        carry[0:1, c] = z[rows - 1 : rows, :]
        e_ref[:, c] = raised
        z_ref[:, c] = z
        e.append(raised.astype(BF))
        inv.append(1.0 / z)
        for m, part_of in enumerate((q, k, v)):
            part_of.append(dot(normed, weights_ref[m, :, c]).astype(BF))
    for i in groups:
        q_ref[:, cols[i]], k_ref[:, cols[i]], v_ref[:, cols[i]] = q[i], k[i], v[i]
        eb_ref[:, cols[i]] = e[i]
    total, value_state = [], []
    for i in groups:
        state = block_diagonal(keys[i])
        keys_ref[i, 0] = state
        total.append(dot(q[i], state))
        state = block_diagonal(values[i])
        values_ref[i, 0] = state
        value_state.append(state)
    es = [by_head(e[i]) for i in groups]
    for i in groups:
        total[i] += dot(lower(dot_nt(q[i], by_head(k[i]))), es[i])
    scores = [total[i] * inv[i] * 0.125 for i in groups]
    raised = [jnp.exp(scores[i] - head_max(scores[i])) for i in groups]
    weights = [raised[i] / head_sums(raised[i]) for i in groups]
    ratio = [(weights[i] * inv[i]).astype(BF) for i in groups]
    out = [dot(ratio[i], value_state[i]) for i in groups]
    for i in groups:
        out[i] += dot(lower(dot_nt(ratio[i], es[i])), by_head(v[i]))
    for i in groups:
        s_ref[:, cols[i]] = scores[i]
        w_ref[:, cols[i]] = weights[i]
        o_ref[:, cols[i]] = out[i].astype(BF)
        keys[i] += dot_tn(k[i], e[i])
        values[i] += dot_tn(e[i], v[i])


def attend(pos, half, x, pieces):
    length, width = x.shape
    steps, groups = length // CHUNK, width // GROUP
    rows = lambda dtype: jax.ShapeDtypeStruct((length, width), dtype)
    block = pl.BlockSpec((CHUNK, width), lambda i: (i, 0))
    state = pl.BlockSpec((groups, 1, GROUP, GROUP), lambda i: (0, i, 0, 0))
    states = jax.ShapeDtypeStruct((groups, steps, GROUP, GROUP), BF)
    full = [jax.ShapeDtypeStruct((4, width, width), BF), jax.ShapeDtypeStruct((8, width), F32)]
    return pl.pallas_call(
        attend_kernel,
        grid=(steps,),
        in_specs=[pl.BlockSpec(memory_space=pltpu.SMEM)] * 2 + [block] + [whole(p) for p in pieces],
        out_specs=[block] * 10 + [state] * 2 + [whole(a) for a in full],
        out_shape=[rows(BF)] * 4
        + [rows(F32), rows(BF), rows(F32), rows(BF), rows(F32), rows(F32), states, states]
        + full,
        scratch_shapes=[pltpu.VMEM((groups, GROUP, GROUP), F32)] * 2 + [pltpu.VMEM((8, width), F32)],
        compiler_params=pltpu.CompilerParams(
            dimension_semantics=("arbitrary",), vmem_limit_bytes=VMEM_LIMIT
        ),
        name="attend",
        cost_estimate=CHEAP,
    )(pos, half, x, *pieces)


def mix_back_kernel(*refs, begun):
    g_ref, q_ref, k_ref, v_ref, eb_ref, e_ref, z_ref, w_ref, s_ref, keys_ref, values_ref = refs[:11]
    before, (dq_ref, dk_ref, dv_ref, dc_ref, later_v, later_k, carry) = refs[11:-7], refs[-7:]

    @pl.when(pl.program_id(0) == 0)
    def _():
        if begun:
            later_v[...], later_k[...], carry[...] = [ref[...] for ref in before]
        else:
            later_v[...] = jnp.zeros_like(later_v)
            later_k[...] = jnp.zeros_like(later_k)
            carry[...] = jnp.zeros_like(carry)

    heads = range(GROUP // SLOT)
    groups = range(later_v.shape[0])
    cols = [slice(i * GROUP, (i + 1) * GROUP) for i in groups]
    g, q, k, v, e = [[ref[:, c] for c in cols] for ref in (g_ref, q_ref, k_ref, v_ref, eb_ref)]
    inv = [1.0 / z_ref[:, c] for c in cols]
    weights = [w_ref[:, c] for c in cols]
    ratio = [(weights[i] * inv[i]).astype(BF) for i in groups]
    es = [by_head(e[i]) for i in groups]
    state = [block_diagonal(later_v[i]) for i in groups]
    d_ratio = [dot_nt(g[i], values_ref[i, 0]) for i in groups]
    dv = [dot(e[i], state[i]) for i in groups]
    de = [dot_nt(v[i], state[i]) for i in groups]
    for i in groups:
        vs = by_head(v[i])
        d_ratio[i] += dot(lower(dot_nt(g[i], vs)), es[i])
        de[i] += dot(upper(dot_nt(vs, g[i])), by_head(ratio[i]))
        dv[i] += dot(upper(dot_nt(es[i], ratio[i])), by_head(g[i]))
    d_weights = [d_ratio[i] * inv[i] for i in groups]
    both = [d_weights[i] * weights[i] for i in groups]
    d_scores = [weights[i] * (d_weights[i] - head_sums(both[i])) for i in groups]
    dn = [(d_scores[i] * inv[i] * 0.125).astype(BF) for i in groups]
    dz = [-(both[i] + d_scores[i] * s_ref[:, cols[i]]) * inv[i] for i in groups]
    state = [block_diagonal(later_k[i]) for i in groups]
    dq = [dot_nt(dn[i], keys_ref[i, 0]) for i in groups]
    dk = [dot(e[i], state[i]) for i in groups]
    de = [de[i] + dot_nt(k[i], state[i]) for i in groups]
    for i in groups:
        ks = by_head(k[i])
        dq[i] += dot(lower(dot_nt(dn[i], es[i])), ks)
        dk[i] += dot(upper(dot_nt(es[i], dn[i])), by_head(q[i]))
        de[i] += dot(upper(dot_nt(ks, q[i])), by_head(dn[i]))
    rows = dz[0].shape[0]
    ones = upper(jnp.ones((rows, rows), F32))
    for i in groups:
        dv_ref[:, cols[i]] = dv[i].astype(BF)
        dq_ref[:, cols[i]] = dq[i].astype(BF)
        dk_ref[:, cols[i]] = dk[i].astype(BF)
        z_sum = split_dot(ones, dz[i]) + carry[0:1, cols[i]]
        carry[0:1, cols[i]] = z_sum[0:1, :]
        dc_ref[:, cols[i]] = ((de[i] + z_sum) * e_ref[:, cols[i]]).astype(BF)
        later_v[i] += dot_tn(ratio[i], g[i])
        later_k[i] += dot_tn(dn[i], q[i])


def mix_back(last, count, before, g, q, k, v, eb, e, z, w, s, keys, values):
    length, width = q.shape
    groups = width // GROUP
    block = pl.BlockSpec((CHUNK, width), lambda i: (last - i, 0))
    state = pl.BlockSpec((groups, 1, GROUP, GROUP), lambda i: (0, last - i, 0, 0))
    out = pl.BlockSpec((CHUNK, width), lambda i: (count - 1 - i, 0))
    rows = jax.ShapeDtypeStruct((count * CHUNK, width), BF)
    sums = [jax.ShapeDtypeStruct((groups, GROUP, GROUP), F32)] * 2
    sums += [jax.ShapeDtypeStruct((8, width), F32)]
    return pl.pallas_call(
        functools.partial(mix_back_kernel, begun=bool(before)),
        grid=(count,),
        in_specs=[block] * 9 + [state] * 2 + [whole(a) for a in before],
        out_specs=[out] * 4 + [whole(a) for a in sums],
        out_shape=[rows] * 4 + sums,
        compiler_params=pltpu.CompilerParams(
            dimension_semantics=("arbitrary",), vmem_limit_bytes=VMEM_LIMIT
        ),
        name="mix_back",
        cost_estimate=CHEAP,
    )(g, q, k, v, eb, e, z, w, s, keys, values, *before)


def scatter_unit(place_ref, grads, first, unit, shard, target, table):
    count = place_ref.shape[1] // 2
    part = LANES
    rows = part // count
    height = target.shape[0] // LANES * LANES // (2 * count)
    for d in range(count):
        place = place_ref[table, (shard // 2) * count + d]
        where = pl.ds(pl.multiple_of(place * height + unit * rows, rows), rows)
        target[where, :] = grads[pl.ds(pl.multiple_of(first + d * rows, rows), rows), :]


def scatter_shards(pos_ref, place_ref, grads, send_ref, keep_ref, unit):
    for index in range(4):
        pos = pos_ref[index]
        target = send_ref if index % 2 else keep_ref
        scatter_unit(place_ref, grads, pos * LANES, unit, pos, target, index % 2)


def feed_kernel(
    pos_ref, place_ref, factor_ref, x_ref, g_ref, o_ref, norm_ref, p0, p1, p2, p3, t0, t1, t2, t3,
    y_ref, dh_ref, do_ref, send_ref, keep_ref, dnorm_ref,
    wo, w1, w2, branch, unit_ref, inv_ref, n2, gb, n2_t, gb_t, dn2, grads, u_all, da_all
):
    step = pl.program_id(0)
    last = pl.num_programs(0) - 1
    length, width = x_ref.shape
    part = width // 4
    block = w1.shape[2]
    tiles = length // 256

    @pl.when(step == 0)
    def _():
        for index, (piece, tall) in enumerate(((p0, t0), (p1, t1), (p2, t2), (p3, t3))):
            pos = pos_ref[index]
            rows = pl.ds(pl.multiple_of(pos * part, part), part)
            wo[rows, :] = piece[0:part, :]
            for j in range(4):
                w1[j, rows, :] = piece[(j + 1) * part : (j + 2) * part, :]
            w2[pos] = tall[0:block, :]

        def before(i, _):
            rows = pl.ds(pl.multiple_of(i * 256, 256), 256)
            h1 = x_ref[rows, :].astype(F32) + dot(o_ref[rows, :], wo[...])
            branch[rows, :] = h1
            unit, inv = normalise(h1)
            unit_ref[rows, :] = unit
            inv_ref[rows, :] = jnp.broadcast_to(inv, (256, 128))
            normed = (unit * norm_ref[2:3, :] + norm_ref[3:4, :]).astype(BF)
            n2[rows, :] = normed
            n2_t[:, rows] = normed.T
            grad = (g_ref[rows, :].astype(F32) * factor_ref[0]).astype(BF)
            gb[rows, :] = grad
            gb_t[:, rows] = grad.T
            dn2[rows, :] = jnp.zeros((256, width), F32)
            return 0

        lax.fori_loop(0, tiles, before, 0)

    up = w1[step]
    down = w2[step]
    tile = TILE
    for i in range(length // tile):
        rows = slice(i * tile, (i + 1) * tile)
        a = dot(n2[rows, :], up)
        square = a * a
        half = 0.5 + 0.5 * jnp.tanh(a * (0.7978845608 + (0.044715 * 0.7978845608) * square))
        u = a * half
        slope = half + u * (1.0 - half) * (
            2.0 * 0.7978845608 + (6.0 * 0.044715 * 0.7978845608) * square
        )
        u = u.astype(BF)
        da = (dot_nt(gb[rows, :], down) * slope).astype(BF)
        u_all[rows, :] = u
        da_all[rows, :] = da
        branch[rows, :] += dot(u, down)
        dn2[rows, :] += dot_nt(da, up)
    up_grad = dot(n2_t[...], da_all[...])
    down_grad = dot(gb_t[...], u_all[...])
    grads[...] = up_grad.astype(BF)
    scatter_shards(pos_ref, place_ref, grads, send_ref, keep_ref, step + 1)
    grads[...] = down_grad.astype(BF)
    mine = (step ^ pos_ref[0]) & 1 == 0

    @pl.when(mine)
    def _():
        for u in range(4):
            scatter_unit(place_ref, grads, u * part, 5 + u, step, keep_ref, 0)

    @pl.when(jnp.logical_not(mine))
    def _():
        for u in range(4):
            scatter_unit(place_ref, grads, u * part, 5 + u, step, send_ref, 1)

    @pl.when(step == last)
    def _():
        gain = norm_ref[2:3, :]

        def after(i, sums):
            rows = pl.ds(pl.multiple_of(i * 256, 256), 256)
            y_ref[rows, :] = branch[rows, :].astype(BF)
            grad = dn2[rows, :]
            unit = unit_ref[rows, :]
            dh = g_ref[rows, :].astype(F32) * factor_ref[0] + normalise_back(
                grad, unit, inv_ref[rows, 0:1], gain
            )
            dh_ref[rows, :] = dh
            dh_low = dh.astype(BF)
            do_ref[rows, :] = dot_nt(dh_low, wo[...]).astype(BF)
            return (
                sums[0] + jnp.sum(grad * unit, axis=0, keepdims=True),
                sums[1] + jnp.sum(grad, axis=0, keepdims=True),
                sums[2] + dot_tn(o_ref[rows, :], dh_low),
            )

        empty = jnp.zeros((1, width), F32)
        sums = lax.fori_loop(0, tiles, after, (empty, empty, jnp.zeros((width, width), F32)))
        dnorm_ref[...] = jnp.zeros_like(dnorm_ref)
        dnorm_ref[0:1, :] = sums[0]
        dnorm_ref[1:2, :] = sums[1]
        grads[...] = sums[2].astype(BF)
        scatter_shards(pos_ref, place_ref, grads, send_ref, keep_ref, 0)


def feed(pos, place, factor, x, g, o, norm, pieces, talls):
    length, width = x.shape
    block = width
    height = 5 * (width // 4) + block
    rows = lambda dtype: jax.ShapeDtypeStruct((length, width), dtype)
    out = [
        rows(BF), rows(F32), rows(BF),
        jax.ShapeDtypeStruct((2 * height, width), BF),
        jax.ShapeDtypeStruct((2 * height, width), BF),
        jax.ShapeDtypeStruct((8, width), F32),
    ]
    args = (x, g, o, norm) + tuple(pieces) + tuple(talls)
    return pl.pallas_call(
        feed_kernel,
        grid=(4,),
        in_specs=[pl.BlockSpec(memory_space=pltpu.SMEM)] * 3 + [whole(a) for a in args],
        out_specs=[whole(a) for a in out],
        out_shape=out,
        scratch_shapes=[
            pltpu.VMEM((width, width), BF),
            pltpu.VMEM((4, width, block), BF),
            pltpu.VMEM((4, block, width), BF),
            pltpu.VMEM((length, width), F32),
            pltpu.VMEM((length, width), F32),
            pltpu.VMEM((length, 128), F32),
            pltpu.VMEM((length, width), BF),
            pltpu.VMEM((length, width), BF),
            pltpu.VMEM((width, length), BF),
            pltpu.VMEM((width, length), BF),
            pltpu.VMEM((length, width), F32),
            pltpu.VMEM((width, block), BF),
            pltpu.VMEM((length, block), BF),
            pltpu.VMEM((length, block), BF),
        ],
        compiler_params=pltpu.CompilerParams(
            dimension_semantics=("arbitrary",), vmem_limit_bytes=VMEM_LIMIT
        ),
        name="feed",
        cost_estimate=CHEAP,
    )(pos, place, factor, *args)


def weight_back_kernel(pos_ref, place_ref, small_ref, n_ref, *refs):
    grads_in, (send_ref, keep_ref, n_t, grads) = refs[:-4], refs[-4:]
    step = pl.program_id(0)

    @pl.when(step == 0)
    def _():
        n_t[...] = n_ref[...].T
        for target in (send_ref, keep_ref):
            target[target.shape[0] - SMALL :, :] = small_ref[...]

    for m in range(4):
        @pl.when(step == m)
        def _():
            total = None
            first = 0
            for j in range(len(grads_in) // 4):
                part = grads_in[4 * j + m]
                last = first + part.shape[0]
                term = dot(n_t[:, first:last], part[...])
                total = term if total is None else total + term
                first = last
            grads[...] = total.astype(BF)

    scatter_shards(pos_ref, place_ref, grads, send_ref, keep_ref, step)


def weight_back(pos, place, small, n, halves):
    length, width = n.shape
    out = jax.ShapeDtypeStruct((2 * width + SMALL, width), BF)
    args = (small, n) + tuple(halves)
    return pl.pallas_call(
        weight_back_kernel,
        grid=(4,),
        in_specs=[pl.BlockSpec(memory_space=pltpu.SMEM)] * 2 + [whole(a) for a in args],
        out_specs=[whole(out)] * 2,
        out_shape=[out] * 2,
        scratch_shapes=[pltpu.VMEM((width, length), BF), pltpu.VMEM((width, width), BF)],
        compiler_params=pltpu.CompilerParams(
            dimension_semantics=("arbitrary",), vmem_limit_bytes=VMEM_SMALL
        ),
        name="weight_back",
        cost_estimate=CHEAP,
    )(pos, place, *args)


def input_back_kernel(x_ref, dh_ref, w_ref, norm_ref, dnorm_ref, *refs):
    grads_in, (dx_ref, small_ref, sums, dn_ref) = refs[:-4], refs[-4:]
    step = pl.program_id(0)
    tile = x_ref.shape[0]

    @pl.when(step == 0)
    def _():
        sums[...] = jnp.zeros_like(sums)

    first = 0
    for j in range(len(grads_in) // 4):
        count = grads_in[4 * j].shape[0] // tile
        begin = first

        @pl.when((step >= begin) & (step < begin + count))
        def _():
            rows = pl.ds(pl.multiple_of((step - begin) * tile, tile), tile)
            dn = None
            for m in range(4):
                term = dot_nt(grads_in[4 * j + m][rows, :], w_ref[m])
                dn = term if dn is None else dn + term
            dn_ref[...] = dn

        first += count

    dn = dn_ref[...]
    unit, inv = normalise(x_ref[...].astype(F32))
    dx_ref[...] = dh_ref[...] + normalise_back(dn, unit, inv, norm_ref[0:1, :])
    sums[0:1, :] += jnp.sum(dn * unit, axis=0, keepdims=True)
    sums[1:2, :] += jnp.sum(dn, axis=0, keepdims=True)

    @pl.when(step == pl.num_programs(0) - 1)
    def _():
        small_ref[...] = jnp.concatenate(
            [sums[0:2, :], dnorm_ref[0:2, :], jnp.zeros((SMALL - 4, sums.shape[1]), F32)], axis=0
        ).astype(BF)


def input_back(x, dh, w, norm, dnorm, halves):
    length, width = x.shape
    tile = 256
    block = pl.BlockSpec((tile, width), lambda i: (i, 0))
    small = jax.ShapeDtypeStruct((SMALL, width), BF)
    return pl.pallas_call(
        input_back_kernel,
        grid=(length // tile,),
        in_specs=[block] * 2 + [whole(w), whole(norm), whole(dnorm)] + [whole(a) for a in halves],
        out_specs=[block, whole(small)],
        out_shape=[jax.ShapeDtypeStruct((length, width), F32), small],
        scratch_shapes=[pltpu.VMEM((8, width), F32), pltpu.VMEM((tile, width), F32)],
        compiler_params=pltpu.CompilerParams(
            dimension_semantics=("arbitrary",), vmem_limit_bytes=VMEM_SMALL
        ),
        name="input_back",
        cost_estimate=CHEAP,
    )(x, dh, w, norm, dnorm, *halves)


def bits_of(size):
    return [1 << b for b in range(size.bit_length() - 1)]


def split_bits():
    return bits_of(lax.axis_size("dp"))[:3]


def exchange(values, even, odd):
    dp, shard = lax.axis_size("dp"), lax.axis_size("shard")
    perm = []
    for d in range(dp):
        for s in range(shard):
            axis, bit = odd if s % 2 else even
            other = (d ^ bit, s) if axis == "dp" else (d, s ^ bit)
            perm.append((d * shard + s, other[0] * shard + other[1]))
    return lax.ppermute(values, ("dp", "shard"), perm)


def swap(values, axis, bit):
    return exchange(values, (axis, bit), (axis, bit))


def after(values, *others):
    return lax.optimization_barrier((values,) + others)[0]


def places():
    count = 2 ** len(split_bits())
    dp, shard = lax.axis_index("dp"), lax.axis_index("shard")
    piece = jnp.arange(2 * count, dtype=jnp.int32)
    far = (piece // count) ^ (shard // 2)
    along = (piece % count) ^ (dp % count)
    order = 0
    for b in range(len(split_bits())):
        order = order * 2 + ((along >> b) & 1)
    even, odd = far * count + order, order * 2 + far
    mine = shard % 2
    return jnp.stack(
        [jnp.where(mine == 0, even, odd), jnp.where(mine == 0, odd, even)]
    ).astype(jnp.int32)


def phases():
    split = [("dp", b) for b in split_bits()]
    return list(zip([("shard", 2)] + split, split + [("shard", 2)]))


def add_up(parts, low, high):
    total = parts[0][low:high].astype(F32)
    for part in parts[1:]:
        total = total + part[low:high].astype(F32)
    return total.astype(BF)


def add_rest(piece):
    for b in bits_of(lax.axis_size("dp"))[3:]:
        piece = add_up([piece, swap(piece, "dp", b)], 0, piece.shape[0])
    return piece


def gather_plan():
    split = split_bits()
    even = [split[0]] + split[1:][::-1]
    odd = split[::-1]
    return [(("dp", a), ("dp", b)) for a, b in zip(even, odd)]


def gather_index():
    odd = lax.axis_index("shard") % 2
    mask = jnp.zeros((1,), jnp.int32)
    for (_, even_bit), (_, odd_bit) in gather_plan():
        mask = jnp.concatenate([mask, mask | jnp.where(odd == 1, odd_bit, even_bit)])
    return (lax.axis_index("dp") % mask.shape[0]) ^ mask


def adam(master, first, second, grad, rate, decay):
    first_new = 0.5 * first + 0.5 * grad
    second_new = 0.5 * second + 0.5 * grad * grad
    correction = 1.0 - 0.5**STEP
    update = first_new / correction / (jnp.sqrt(second_new / correction) + 1e-08)
    return master - rate * (update + decay * master), first_new, second_new


def gather_rows(index_ref, sources, targets):
    count = index_ref.shape[0]
    rows = LANES // count
    for source, target in zip(sources, targets):
        units = target.shape[0] // LANES
        for j in range(count):
            for u in range(units):
                place = pl.ds(pl.multiple_of(u * LANES + index_ref[j] * rows, rows), rows)
                first = (j * units + u) * rows
                target[place, :] = source[first : first + rows, :]


def renew_first_kernel(
    side_ref, index_ref, factor_ref, early_ref, late_ref, gn_ref, nm, nf, ns,
    am, af, as_, um, uf, us, copy_ref, early, late
):
    factor = factor_ref[0]
    width = early.shape[1]
    height = am.shape[1]
    gather_rows(index_ref, (early_ref, late_ref), (early, late))

    def span(unit):
        return pl.ds(pl.multiple_of(unit * LANES + side_ref[0] * height, height), height)

    for unit in range(8):
        if unit < 5:
            source = late[span(unit), :] if unit < 4 else early[span(0), :]
            state = am[unit], af[unit], as_[unit]
        else:
            source = early[span(unit - 4), :]
            cols = slice((unit - 5) * width, (unit - 4) * width)
            state = um[:, cols], uf[:, cols], us[:, cols]
        new = adam(*state, source.astype(F32) * factor, 0.05, 0.01)
        copy_ref[unit * height : (unit + 1) * height, :] = new[0].astype(BF)
    new = adam(nm[...], nf[...], ns[...], gn_ref[...] * factor, 0.3, 0.0)
    last = copy_ref.shape[0] - SMALL
    copy_ref[last:, :] = jnp.zeros((SMALL, width), BF)
    copy_ref[last : last + 4, 0:LANES] = new[0].astype(BF)


def renew_first(side, index, factor, early, late, gn, attn, up, norm):
    five, part, width = attn[0].shape
    hidden = up[0].shape[1]
    smem = pl.BlockSpec(memory_space=pltpu.SMEM)
    copy = jax.ShapeDtypeStruct((8 * part // 2 + SMALL, width), BF)
    return pl.pallas_call(
        renew_first_kernel,
        grid_spec=pltpu.PrefetchScalarGridSpec(
            num_scalar_prefetch=1,
            grid=(1,),
            in_specs=[smem, smem, whole(early), whole(late), whole(gn)]
            + [whole(a) for a in norm]
            + [pl.BlockSpec((five, part // 2, width), lambda i, side: (0, side[0], 0))] * 3
            + [pl.BlockSpec((part // 2, hidden), lambda i, side: (side[0], 0))] * 3,
            out_specs=whole(copy),
            scratch_shapes=[pltpu.VMEM(early.shape, BF), pltpu.VMEM(late.shape, BF)],
        ),
        out_shape=copy,
        compiler_params=pltpu.CompilerParams(
            dimension_semantics=("arbitrary",), vmem_limit_bytes=VMEM_LIMIT
        ),
        name="renew_first",
        cost_estimate=CHEAP,
    )(side, index, factor, early, late, gn, *norm, *attn, *up)


def update_kernel(index_ref, factor_ref, early_ref, late_ref, gn_ref, *refs):
    am, af, as_, um, uf, us, dm, df, ds, nm, nf, ns = refs[:12]
    early, late = refs[-2:]
    outs, copy_low, copy_high = refs[12:-4], refs[-4], refs[-3]
    step = pl.program_id(0)
    factor = factor_ref[0]
    width = early.shape[1]
    part = late.shape[0] // 4
    blocks = um.shape[1] // width
    height = part // pl.num_programs(0)

    def keep(group, where, unit, size, new):
        for target, value in zip(outs[3 * group : 3 * group + 3], new):
            target[where] = value
        target, unit = (copy_low, unit) if unit < 8 else (copy_high, unit - 8)
        rows = pl.ds(pl.multiple_of(unit * part + step * size, size), size)
        target[rows, :] = new[0].astype(BF)

    @pl.when(step == 0)
    def _():
        gather_rows(index_ref, (early_ref, late_ref), (early, late))
        new = adam(nm[...], nf[...], ns[...], gn_ref[...] * factor, 0.3, 0.0)
        outs[9][...], outs[10][...], outs[11][...] = new

    def span(base, size):
        return pl.ds(pl.multiple_of(base + step * size, size), size)

    for m in range(5):
        source = late[span(m * part, height), :] if m < 4 else early[span(0, height), :]
        new = adam(am[m], af[m], as_[m], source.astype(F32) * factor, 0.05, 0.01)
        keep(0, (m, slice(None), slice(None)), m, height, new)
    for j in range(blocks):
        source = early[span((j + 1) * part, height), :]
        cols = (slice(None), slice(j * width, (j + 1) * width))
        new = adam(um[cols], uf[cols], us[cols], source.astype(F32) * factor, 0.05, 0.01)
        keep(1, cols, 5 + j, height, new)
    tall = dm.shape[0]
    source = early[(blocks + 1) * part :, span(0, tall)].astype(F32).T
    new = adam(dm[...], df[...], ds[...], source * factor, 0.05, 0.01)
    keep(2, (slice(None), slice(None)), 5 + blocks, tall, new)


def update(index, factor, early, late, gn, attn, up, down, norm):
    steps = 4
    smem = pl.BlockSpec(memory_space=pltpu.SMEM)
    five, part, width = attn[0].shape
    specs = (
        [pl.BlockSpec((five, part // steps, width), lambda i: (0, i, 0))] * 3
        + [pl.BlockSpec((part // steps, up[0].shape[1]), lambda i: (i, 0))] * 3
        + [pl.BlockSpec((down[0].shape[0] // steps, width), lambda i: (i, 0))] * 3
        + [whole(norm[0])] * 3
    )
    arrays = tuple(attn) + tuple(up) + tuple(down) + tuple(norm)
    low = jax.ShapeDtypeStruct((8 * part, width), BF)
    high = jax.ShapeDtypeStruct((early.shape[0] + late.shape[0] - 8 * part, width), BF)
    return pl.pallas_call(
        update_kernel,
        grid=(steps,),
        in_specs=[smem, smem, whole(early), whole(late), whole(gn)] + specs,
        out_specs=specs + [whole(low), whole(high)],
        out_shape=[jax.ShapeDtypeStruct(a.shape, F32) for a in arrays] + [low, high],
        scratch_shapes=[pltpu.VMEM(early.shape, BF), pltpu.VMEM(late.shape, BF)],
        compiler_params=pltpu.CompilerParams(
            dimension_semantics=("arbitrary",), vmem_limit_bytes=VMEM_LIMIT
        ),
        name="update",
        cost_estimate=CHEAP,
    )(index, factor, early, late, gn, *arrays)


def place_unit(pos, source, unit, first, count, attn_ref, up_ref, down_ref, sem):
    width = attn_ref.shape[2]
    blocks = up_ref.shape[1] // width
    tall = down_ref.shape[0] // 4
    rows = pl.ds(pl.multiple_of(pos * LANES + first, count), count)
    if unit < 5:
        target = attn_ref.at[unit, rows, :]
    elif unit < 5 + blocks:
        target = up_ref.at[rows, pl.ds((unit - 5) * width, width)]
    else:
        base = pl.multiple_of(pos * tall + (unit - 5 - blocks) * LANES + first, count)
        target = down_ref.at[pl.ds(base, count), :]
    return pltpu.make_async_copy(source, target, sem)


def run_copies(copies):
    for copy in copies:
        copy.start()
    for copy in copies:
        copy.wait()


def place_whole(pos, piece, unit, outs, sems, copies):
    for j in range(piece.shape[0] // LANES):
        source = piece.at[pl.ds(j * LANES, LANES), :]
        copies.append(place_unit(pos, source, unit + j, 0, LANES, *outs, sems.at[len(copies)]))


def place_half(pos, side, piece, outs, sems, copies):
    half = LANES // 2
    for unit in range(8):
        source = piece.at[pl.ds(unit * half, half), :]
        copies.append(place_unit(pos, source, unit, half * side, half, *outs, sems.at[len(copies)]))


def unpack_near_kernel(pos_ref, side_ref, p0, p1, p2, p3, p4, p5, attn_ref, up_ref, down_ref, sems):
    copies = []
    outs = attn_ref, up_ref, down_ref
    for index, parts in enumerate(((p0, p1), (p2, p3))):
        place_whole(pos_ref[index], parts[0], 0, outs, sems, copies)
        place_whole(pos_ref[index], parts[1], 8, outs, sems, copies)
    for index, piece in enumerate((p4, p5)):
        place_half(pos_ref[2 + index], side_ref[0], piece, outs, sems, copies)
    run_copies(copies)


def unpack_far_kernel(pos_ref, side_ref, p0, p1, p2, p3, *refs):
    outs, sems = refs[3:6], refs[6]
    copies = []
    for index, piece in enumerate((p0, p1)):
        place_half(pos_ref[2 + index], side_ref[0] ^ 1, piece, outs, sems, copies)
    for index, piece in enumerate((p2, p3)):
        place_whole(pos_ref[2 + index], piece, 8, outs, sems, copies)
    run_copies(copies)


def share_copies(pos, side, low, high, first, width, hidden):
    units = (low.shape[0] + high.shape[0]) // LANES
    ours = swap(first, "shard", 2)
    other = swap(after(ours, low), "dp", 1)
    rest = swap(after(high, ours), "shard", 2)
    near = [swap(after(part, ours), "shard", 1) for part in (low, high)]
    ours_too = swap(after(ours, low), "shard", 1)
    first_too = swap(after(first[8 * LANES // 2 :], ours), "shard", 1)
    hbm = pl.BlockSpec(memory_space=pl.ANY)
    vmem = pl.BlockSpec(memory_space=pltpu.VMEM)
    smem = pl.BlockSpec(memory_space=pltpu.SMEM)
    shapes = [
        jax.ShapeDtypeStruct((5, width, width), BF),
        jax.ShapeDtypeStruct((width, hidden), BF),
        jax.ShapeDtypeStruct((hidden, width), BF),
    ]
    params = pltpu.CompilerParams(vmem_limit_bytes=VMEM_SMALL)
    begun = pl.pallas_call(
        unpack_near_kernel,
        in_specs=[smem, smem] + [vmem] * 6,
        out_specs=[hbm] * 3,
        out_shape=shapes,
        scratch_shapes=[pltpu.SemaphoreType.DMA((2 * (units + 8),))],
        compiler_params=params,
        name="unpack_near",
        cost_estimate=CHEAP,
    )(pos, side, low, high, *near, ours, ours_too)
    a, b, c, d = [
        p[p.shape[0] - SMALL : p.shape[0] - SMALL + 4, :LANES]
        for p in (first, first_too, ours, ours_too)
    ]
    low_bit, high_bit = pos[0] % 2 == 1, pos[0] // 2 == 1
    a, b, c, d = [jnp.where(low_bit, v, u) for u, v in ((a, b), (b, a), (c, d), (d, c))]
    a, b, c, d = [jnp.where(high_bit, v, u) for u, v in ((a, c), (b, d), (c, a), (d, b))]
    norms = jnp.concatenate([a, b, c, d], axis=1)
    far = [other, swap(after(other, begun[0], norms), "shard", 1)]
    far += [rest, swap(after(rest, begun[0], norms), "shard", 1)]
    done = pl.pallas_call(
        unpack_far_kernel,
        in_specs=[smem, smem] + [vmem] * 4 + [hbm] * 3,
        out_specs=[hbm] * 3,
        out_shape=shapes,
        scratch_shapes=[pltpu.SemaphoreType.DMA((2 * units,))],
        input_output_aliases={6: 0, 7: 1, 8: 2},
        compiler_params=params,
        name="unpack_far",
        cost_estimate=CHEAP,
    )(pos, side, *far, *begun)
    return tuple(done) + (norms,)


def shards(
    tokens, out_grad, domain_ids, domain_weight,
    attn_master, attn_first, attn_second,
    up_master, up_first, up_second,
    down_master, down_first, down_second,
    norm_master, norm_first, norm_second,
):
    length, width = tokens.shape
    hidden = up_master.shape[1]
    part = width // 4
    blocks = hidden // width
    dp = lax.axis_index("dp")
    shard = lax.axis_index("shard").astype(jnp.int32)
    pos = shard ^ jnp.arange(4, dtype=jnp.int32)
    half = (dp % 2).astype(jnp.int32)[None]
    place = places()

    small = jnp.pad(norm_master.astype(BF), ((0, SMALL - 4), (0, width - part)))
    rows = attn_master[:4].astype(BF).reshape(4 * part, width)
    own = jnp.concatenate([rows[: 2 * part], small, rows[2 * part :], jnp.zeros_like(small)])
    middle = own.shape[0] // 2
    near = swap(own, "shard", 1)
    ours = lax.dynamic_slice(own, (half[0] * middle, 0), (middle, width))
    far_a = swap(ours, "shard", 2)

    domains = domain_weight.shape[0]
    onehot = (domain_ids[:, None] == jnp.arange(domains, dtype=jnp.int32)[None, :]).astype(F32)
    counts = jnp.sum(onehot, axis=0)
    dp_bits = bits_of(lax.axis_size("dp"))
    for b in dp_bits[:2]:
        counts = counts + swap(counts, "dp", b)
    far_b = swap(after(far_a, counts), "dp", 1)
    second = jnp.concatenate(
        [attn_master[4].astype(BF)]
        + [up_master[:, j * width : (j + 1) * width].astype(BF) for j in range(blocks)]
    )
    second_far = swap(after(second, counts), "shard", 2)
    for b in dp_bits[2:]:
        counts = counts + after(swap(counts, "dp", b), far_b)
    counts_row = jnp.pad(counts.astype(BF)[None], ((0, SMALL - 1), (0, width - domains)))
    third = jnp.concatenate([down_master.astype(BF), counts_row])
    third_far = swap(third, "shard", 2)
    far = [far_a, far_b, swap(far_a, "shard", 1), swap(far_b, "shard", 1)]
    q, k, v, n, e, eb, z, o, weights, scores, keys, values, w, norm = attend(
        pos, half, after(tokens, third), [own, near] + far
    )
    second = [second, swap(second, "shard", 1), second_far, swap(after(second_far, o), "shard", 1)]
    third = [third, swap(third, "shard", 1), third_far, swap(after(third_far, o), "shard", 1)]
    total_seqs = lax.axis_size("dp") * lax.axis_size("shard") * domain_ids.shape[0]
    counts = sum(piece[piece.shape[0] - SMALL, :domains].astype(F32) for piece in third)
    per_domain = domain_weight * total_seqs / (domains * jnp.maximum(counts, 1.0))
    seq_weight = jnp.sum(onehot * per_domain[None, :], axis=1)
    y, dh, do, send, keep, dnorm = feed(
        pos, place, seq_weight, tokens, out_grad, o, norm, second, third
    )

    steps, plan = phases(), gather_plan()
    pieces = 2 ** len(steps)
    rows = keep.shape[0] // pieces

    def forward_phase(parts, phase, rows):
        low = rows * pieces >> (phase + 1)
        return add_up(parts, low, 2 * low)

    saved = (q, k, v, eb, e, z, weights, scores, keys, values)
    chunks = length // CHUNK
    early = [keep, swap(send, "shard", 1)]
    later = mix_back(chunks - 1, 1, (), do, *saved)
    out = after(forward_phase(early, 0, rows), later[0])
    early.append(exchange(out, *steps[0]))
    sooner = mix_back(chunks - 2, chunks - 1, later[4:], after(do, out), *saved)
    back = list(sooner[:4]) + list(later[:4])
    out = after(forward_phase(early, 1, rows), back[0])
    early.append(exchange(out, *steps[1]))
    dx, small = input_back(tokens, after(dh, out), w, norm, dnorm, back)
    send, keep = weight_back(pos, place, small, n, back)
    turn = forward_phase(early, 2, rows)
    got = exchange(turn, *steps[2])
    late = [keep, swap(after(send, turn), "shard", 1)]
    height = keep.shape[0] - SMALL
    thin = height // pieces
    small = add_up(late, height, height + SMALL)

    def late_phase(phase):
        out = jnp.concatenate([forward_phase(late, phase, thin), small])
        return out, exchange(out, *steps[phase])

    def late_sum(got):
        late.append(got)
        return add_up([small, got[got.shape[0] - SMALL :]], 0, SMALL)

    turn, late_got = late_phase(0)
    small = late_sum(late_got)
    turn, late_got = late_phase(1)
    early.append(after(got, turn))
    got = exchange(forward_phase(early, 3, rows), *steps[3])
    small = late_sum(late_got)
    turn, late_got = late_phase(2)
    early.append(after(got, turn))
    early = add_rest(add_up(early, 0, rows))
    got = exchange(early, *plan[0])
    small = late_sum(late_got)
    turn, late_got = late_phase(3)
    early = jnp.concatenate([early, after(got, turn)])
    got = exchange(early, *plan[1])
    small = late_sum(late_got)
    late = add_rest(jnp.concatenate([add_up(late, 0, thin), small]))
    late, small = late[:thin], late[thin:]
    late_got = exchange(late, *plan[0])
    norm_grad = lax.dynamic_slice(small[:4], (0, shard * part), (4, part)).astype(F32)
    late = jnp.concatenate([late, late_got])
    late = jnp.concatenate([late, exchange(late, *plan[1])])
    early = jnp.concatenate([early, after(got, late)])
    got = exchange(early, *plan[2])
    late_got = exchange(late, *plan[2])
    early = jnp.concatenate([early, after(got, late)])
    square = jnp.sum(jnp.square(norm_grad)) + jnp.sum(jnp.square(early.astype(F32)))
    late = jnp.concatenate([late, after(late_got, square)])
    square = (square + jnp.sum(jnp.square(late.astype(F32))))[None]
    for b in (1, 2):
        square = square + swap(square, "shard", b)
    index = gather_index()
    clip_norm = jnp.sqrt(square)
    factor = jnp.minimum(1.0, 1.0 / (clip_norm + 1e-06))
    attn = (attn_master, attn_first, attn_second)
    up = (up_master, up_first, up_second)
    down = (down_master, down_first, down_second)
    norms = (norm_master, norm_first, norm_second)
    leaving = renew_first(half, index, factor, early, late, norm_grad, attn, up, norms)
    *new, low, high = update(index, factor, early, after(late, leaving), norm_grad, attn, up, down, norms)
    copies = share_copies(pos, half, low, high, leaving, width, hidden)
    return (y, dx) + tuple(new) + (clip_norm[0],) + tuple(copies)


def solution(mesh):
    rows = P(("dp", "shard"), None)
    attn = (P(None, "shard", None),) * 3
    tall = (P("shard", None),) * 6
    norm = (P(None, "shard"),) * 3
    return jax.shard_map(
        shards,
        mesh=mesh,
        in_specs=(rows, rows, P(("dp", "shard")), P()) + attn + tall + norm,
        out_specs=(rows, rows) + attn + tall + norm + (P(),) * 5,
        check_vma=False,
    )
```

```python
import functools
import jax
import jax.numpy as jnp
from jax import lax
from jax.experimental import pallas as pl
from jax.experimental.pallas import tpu as pltpu
from jax.sharding import PartitionSpec as P

BF = jnp.bfloat16
F32 = jnp.float32
MIB = 1024 * 1024
VMEM_ATTEND = 40 * MIB
VMEM_MIX = 44 * MIB
VMEM_FEED = 44 * MIB
VMEM_BACK = 24 * MIB
VMEM_UPDATE = 56 * MIB
VMEM_UNPACK = 24 * MIB
CHUNK = 256
SLOT = 64
GROUP = 256
LANES = 128
SMALL = 16
CHEAP = pl.CostEstimate(flops=1, bytes_accessed=1, transcendentals=0)
STEP = 10
TILE = 512
COUNTS = (1, 2, 1)


def whole(a):
    return pl.BlockSpec(a.shape, lambda *_: (0,) * len(a.shape), pipeline_mode=pl.Buffered(1))


def dot(a, b):
    return jnp.dot(a, b, preferred_element_type=F32)


def dot_nt(a, b):
    return lax.dot_general(a, b, (((1,), (1,)), ((), ())), preferred_element_type=F32)


def dot_tn(a, b):
    return lax.dot_general(a, b, (((0,), (0,)), ((), ())), preferred_element_type=F32)


def head_of(shape, dim):
    return lax.broadcasted_iota(jnp.int32, shape, dim) // SLOT


def block_diagonal(state):
    return jnp.where(head_of(state.shape, 0) == head_of(state.shape, 1), state, 0.0).astype(BF)


def only_head(rows, head):
    return jnp.where(head_of(rows.shape, 1) == head, rows, jnp.zeros_like(rows))


def by_head(rows):
    return jnp.concatenate([only_head(rows, h) for h in range(GROUP // SLOT)], axis=0)


def lower(square):
    size = square.shape[0]
    row = lax.broadcasted_iota(jnp.int16, (size, size), 0)
    col = lax.broadcasted_iota(jnp.int16, (size, size), 1)
    return jnp.concatenate(
        [
            jnp.where(row >= col, square[:, first : first + size].astype(BF), jnp.zeros((), BF))
            for first in range(0, square.shape[1], size)
        ],
        axis=1,
    )


def upper(square):
    size = square.shape[1]
    row = lax.broadcasted_iota(jnp.int16, (size, size), 0)
    col = lax.broadcasted_iota(jnp.int16, (size, size), 1)
    return jnp.concatenate(
        [
            jnp.where(row <= col, square[first : first + size, :].astype(BF), jnp.zeros((), BF))
            for first in range(0, square.shape[0], size)
        ],
        axis=1,
    )


def split_dot(ones, values):
    high = values.astype(BF)
    low = (values - high.astype(F32)).astype(BF)
    return dot(ones, high) + dot(ones, low)


def head_ones():
    return jnp.where(
        head_of((GROUP, GROUP), 0) == head_of((GROUP, GROUP), 1), 1.0, 0.0
    ).astype(BF)


def head_sums(values):
    ones = head_ones()
    high = values.astype(BF)
    low = (values - high.astype(F32)).astype(BF)
    return dot(high, ones) + dot(low, ones)


def head_max(values):
    top = None
    head = head_of(values.shape, 1)
    for index in range(GROUP // SLOT):
        mine = jnp.max(jnp.where(head == index, values, -jnp.inf), axis=1, keepdims=True)
        top = mine if top is None else jnp.where(head == index, mine, top)
    return top


def normalise(values):
    centred = values - jnp.mean(values, axis=-1, keepdims=True)
    inv = lax.rsqrt(jnp.mean(centred * centred, axis=-1, keepdims=True) + 1e-05)
    return centred * inv, inv


def normalise_back(grad, unit, inv, gain):
    scaled = grad * gain
    return inv * (
        scaled
        - jnp.mean(scaled, axis=-1, keepdims=True)
        - unit * jnp.mean(scaled * unit, axis=-1, keepdims=True)
    )


def attend_kernel(
    pos_ref, half_ref, x_ref, near0, near1, far0, far1, far2, far3,
    q_ref, k_ref, v_ref, n_ref, e_ref, eb_ref, z_ref, o_ref, w_ref, s_ref, keys_ref, values_ref,
    weights_ref, norm_ref, keys, values, carry
):
    width = x_ref.shape[1]
    part = width // 4

    @pl.when(pl.program_id(0) == 0)
    def _():
        low = far0.shape[0]

        def rows_of(index, first, count):
            if index < 2:
                return (near0, near1)[index][first : first + count, :]
            a, b = ((far0, far1), (far2, far3))[index - 2]
            if first >= low:
                a, b, first = b, a, first - low
            return jnp.where(half_ref[0] == 0, a[first : first + count, :], b[first : first + count, :])

        for index in range(4):
            rows = pl.ds(pl.multiple_of(pos_ref[index] * part, part), part)
            for m in range(4):
                weights_ref[m, rows, :] = rows_of(index, m * part + SMALL * (m > 1), part)
            norm_ref[:, rows] = rows_of(index, 2 * part, SMALL)[0:8, 0:part].astype(F32)
        carry[...] = jnp.zeros_like(carry)
        keys[...] = jnp.zeros_like(keys)
        values[...] = jnp.zeros_like(values)

    heads = range(GROUP // SLOT)
    groups = range(keys.shape[0])
    cols = [slice(i * GROUP, (i + 1) * GROUP) for i in groups]
    unit, _ = normalise(x_ref[...].astype(F32))
    normed = (unit * norm_ref[0:1, :] + norm_ref[1:2, :]).astype(BF)
    n_ref[...] = normed
    rows = normed.shape[0]
    ones = lower(jnp.ones((rows, rows), F32))
    q, k, v, e, inv = [], [], [], [], []
    for c in cols:
        raised = jnp.exp(dot(normed, weights_ref[3, :, c]))
        z = split_dot(ones, raised) + carry[0:1, c]
        carry[0:1, c] = z[rows - 1 : rows, :]
        e_ref[:, c] = raised
        z_ref[:, c] = z
        e.append(raised.astype(BF))
        inv.append(1.0 / z)
        for m, part_of in enumerate((q, k, v)):
            part_of.append(dot(normed, weights_ref[m, :, c]).astype(BF))
    for i in groups:
        q_ref[:, cols[i]], k_ref[:, cols[i]], v_ref[:, cols[i]] = q[i], k[i], v[i]
        eb_ref[:, cols[i]] = e[i]
    total, value_state = [], []
    for i in groups:
        state = block_diagonal(keys[i])
        keys_ref[i, 0] = state
        total.append(dot(q[i], state))
        state = block_diagonal(values[i])
        values_ref[i, 0] = state
        value_state.append(state)
    es = [by_head(e[i]) for i in groups]
    for i in groups:
        total[i] += dot(lower(dot_nt(q[i], by_head(k[i]))), es[i])
    scores = [total[i] * inv[i] * 0.125 for i in groups]
    raised = [jnp.exp(scores[i] - head_max(scores[i])) for i in groups]
    weights = [raised[i] / head_sums(raised[i]) for i in groups]
    ratio = [(weights[i] * inv[i]).astype(BF) for i in groups]
    out = [dot(ratio[i], value_state[i]) for i in groups]
    for i in groups:
        out[i] += dot(lower(dot_nt(ratio[i], es[i])), by_head(v[i]))
    for i in groups:
        s_ref[:, cols[i]] = scores[i]
        w_ref[:, cols[i]] = weights[i]
        o_ref[:, cols[i]] = out[i].astype(BF)
        keys[i] += dot_tn(k[i], e[i])
        values[i] += dot_tn(e[i], v[i])


def attend(pos, half, x, pieces):
    length, width = x.shape
    steps, groups = length // CHUNK, width // GROUP
    rows = lambda dtype: jax.ShapeDtypeStruct((length, width), dtype)
    block = pl.BlockSpec((CHUNK, width), lambda i: (i, 0))
    state = pl.BlockSpec((groups, 1, GROUP, GROUP), lambda i: (0, i, 0, 0))
    states = jax.ShapeDtypeStruct((groups, steps, GROUP, GROUP), BF)
    full = [jax.ShapeDtypeStruct((4, width, width), BF), jax.ShapeDtypeStruct((8, width), F32)]
    return pl.pallas_call(
        attend_kernel,
        grid=(steps,),
        in_specs=[pl.BlockSpec(memory_space=pltpu.SMEM)] * 2 + [block] + [whole(p) for p in pieces],
        out_specs=[block] * 10 + [state] * 2 + [whole(a) for a in full],
        out_shape=[rows(BF)] * 4
        + [rows(F32), rows(BF), rows(F32), rows(BF), rows(F32), rows(F32), states, states]
        + full,
        scratch_shapes=[pltpu.VMEM((groups, GROUP, GROUP), F32)] * 2 + [pltpu.VMEM((8, width), F32)],
        compiler_params=pltpu.CompilerParams(
            dimension_semantics=("arbitrary",), vmem_limit_bytes=VMEM_ATTEND
        ),
        name="attend",
        cost_estimate=CHEAP,
    )(pos, half, x, *pieces)


def mix_back_kernel(*refs, begun):
    g_ref, q_ref, k_ref, v_ref, eb_ref, e_ref, z_ref, w_ref, s_ref, keys_ref, values_ref = refs[:11]
    before, (dq_ref, dk_ref, dv_ref, dc_ref, later_v, later_k, carry) = refs[11:-7], refs[-7:]

    @pl.when(pl.program_id(0) == 0)
    def _():
        if begun:
            later_v[...], later_k[...], carry[...] = [ref[...] for ref in before]
        else:
            later_v[...] = jnp.zeros_like(later_v)
            later_k[...] = jnp.zeros_like(later_k)
            carry[...] = jnp.zeros_like(carry)

    heads = range(GROUP // SLOT)
    groups = range(later_v.shape[0])
    cols = [slice(i * GROUP, (i + 1) * GROUP) for i in groups]
    g, q, k, v, e = [[ref[:, c] for c in cols] for ref in (g_ref, q_ref, k_ref, v_ref, eb_ref)]
    inv = [1.0 / z_ref[:, c] for c in cols]
    weights = [w_ref[:, c] for c in cols]
    ratio = [(weights[i] * inv[i]).astype(BF) for i in groups]
    es = [by_head(e[i]) for i in groups]
    state = [block_diagonal(later_v[i]) for i in groups]
    d_ratio = [dot_nt(g[i], values_ref[i, 0]) for i in groups]
    dv = [dot(e[i], state[i]) for i in groups]
    de = [dot_nt(v[i], state[i]) for i in groups]
    for i in groups:
        vs = by_head(v[i])
        d_ratio[i] += dot(lower(dot_nt(g[i], vs)), es[i])
        de[i] += dot(upper(dot_nt(vs, g[i])), by_head(ratio[i]))
        dv[i] += dot(upper(dot_nt(es[i], ratio[i])), by_head(g[i]))
    d_weights = [d_ratio[i] * inv[i] for i in groups]
    both = [d_weights[i] * weights[i] for i in groups]
    d_scores = [weights[i] * (d_weights[i] - head_sums(both[i])) for i in groups]
    dn = [(d_scores[i] * inv[i] * 0.125).astype(BF) for i in groups]
    dz = [-(both[i] + d_scores[i] * s_ref[:, cols[i]]) * inv[i] for i in groups]
    state = [block_diagonal(later_k[i]) for i in groups]
    dq = [dot_nt(dn[i], keys_ref[i, 0]) for i in groups]
    dk = [dot(e[i], state[i]) for i in groups]
    de = [de[i] + dot_nt(k[i], state[i]) for i in groups]
    for i in groups:
        ks = by_head(k[i])
        dq[i] += dot(lower(dot_nt(dn[i], es[i])), ks)
        dk[i] += dot(upper(dot_nt(es[i], dn[i])), by_head(q[i]))
        de[i] += dot(upper(dot_nt(ks, q[i])), by_head(dn[i]))
    rows = dz[0].shape[0]
    ones = upper(jnp.ones((rows, rows), F32))
    for i in groups:
        dv_ref[:, cols[i]] = dv[i].astype(BF)
        dq_ref[:, cols[i]] = dq[i].astype(BF)
        dk_ref[:, cols[i]] = dk[i].astype(BF)
        z_sum = split_dot(ones, dz[i]) + carry[0:1, cols[i]]
        carry[0:1, cols[i]] = z_sum[0:1, :]
        dc_ref[:, cols[i]] = ((de[i] + z_sum) * e_ref[:, cols[i]]).astype(BF)
        later_v[i] += dot_tn(ratio[i], g[i])
        later_k[i] += dot_tn(dn[i], q[i])


def mix_back(last, count, before, g, q, k, v, eb, e, z, w, s, keys, values):
    length, width = q.shape
    groups = width // GROUP
    block = pl.BlockSpec((CHUNK, width), lambda i: (last - i, 0))
    state = pl.BlockSpec((groups, 1, GROUP, GROUP), lambda i: (0, last - i, 0, 0))
    out = pl.BlockSpec((CHUNK, width), lambda i: (count - 1 - i, 0))
    rows = jax.ShapeDtypeStruct((count * CHUNK, width), BF)
    sums = [jax.ShapeDtypeStruct((groups, GROUP, GROUP), F32)] * 2
    sums += [jax.ShapeDtypeStruct((8, width), F32)]
    return pl.pallas_call(
        functools.partial(mix_back_kernel, begun=bool(before)),
        grid=(count,),
        in_specs=[block] * 9 + [state] * 2 + [whole(a) for a in before],
        out_specs=[out] * 4 + [whole(a) for a in sums],
        out_shape=[rows] * 4 + sums,
        compiler_params=pltpu.CompilerParams(
            dimension_semantics=("arbitrary",), vmem_limit_bytes=VMEM_MIX
        ),
        name="mix_back",
        cost_estimate=CHEAP,
    )(g, q, k, v, eb, e, z, w, s, keys, values, *before)


def scatter_unit(place_ref, grads, first, unit, shard, target, table):
    count = place_ref.shape[1] // 2
    part = LANES
    rows = part // count
    height = target.shape[0] // LANES * LANES // (2 * count)
    for d in range(count):
        place = place_ref[table, (shard // 2) * count + d]
        where = pl.ds(pl.multiple_of(place * height + unit * rows, rows), rows)
        target[where, :] = grads[pl.ds(pl.multiple_of(first + d * rows, rows), rows), :]


def scatter_shards(pos_ref, place_ref, grads, send_ref, keep_ref, unit):
    for index in range(4):
        pos = pos_ref[index]
        target = send_ref if index % 2 else keep_ref
        scatter_unit(place_ref, grads, pos * LANES, unit, pos, target, index % 2)


def feed_kernel(
    pos_ref, place_ref, domain_ref, x_ref, g_ref, o_ref, norm_ref, p0, p1, p2, p3, t0, t1, t2, t3,
    y_ref, dh_ref, do_ref, send_ref, keep_ref, dnorm_ref,
    wo, w1, w2, branch, unit_ref, inv_ref, n2, gb, n2_t, gb_t, dn2, grads, u_all, da_all, factor_ref
):
    step = pl.program_id(0)
    last = pl.num_programs(0) - 1
    length, width = x_ref.shape
    part = width // 4
    block = w1.shape[2]
    tiles = length // 256

    @pl.when(step == 0)
    def _():
        for index, (piece, tall) in enumerate(((p0, t0), (p1, t1), (p2, t2), (p3, t3))):
            pos = pos_ref[index]
            rows = pl.ds(pl.multiple_of(pos * part, part), part)
            wo[rows, :] = piece[0:part, :]
            for j in range(4):
                w1[j, rows, :] = piece[(j + 1) * part : (j + 2) * part, :]
            w2[pos] = tall[0:block, :]
        count = sum(t[block : block + SMALL, 0:LANES].astype(F32) for t in (t0, t1, t2, t3))
        share = domain_ref[0:1, :] * domain_ref[1:2, :] / jnp.maximum(count[0:1, :], 1.0)
        factor_ref[...] = jnp.broadcast_to(jnp.sum(share, axis=1, keepdims=True), factor_ref.shape)

        def before(i, _):
            rows = pl.ds(pl.multiple_of(i * 256, 256), 256)
            h1 = x_ref[rows, :].astype(F32) + dot(o_ref[rows, :], wo[...])
            branch[rows, :] = h1
            unit, inv = normalise(h1)
            unit_ref[rows, :] = unit
            inv_ref[rows, :] = jnp.broadcast_to(inv, (256, 128))
            normed = (unit * norm_ref[2:3, :] + norm_ref[3:4, :]).astype(BF)
            n2[rows, :] = normed
            n2_t[:, rows] = normed.T
            grad = (g_ref[rows, :].astype(F32) * factor_ref[0:1, 0:1]).astype(BF)
            gb[rows, :] = grad
            gb_t[:, rows] = grad.T
            dn2[rows, :] = jnp.zeros((256, width), F32)
            return 0

        lax.fori_loop(0, tiles, before, 0)

    up = w1[step]
    down = w2[step]
    tile = TILE
    for i in range(length // tile):
        rows = slice(i * tile, (i + 1) * tile)
        a = dot(n2[rows, :], up)
        square = a * a
        half = 0.5 + 0.5 * jnp.tanh(a * (0.7978845608 + (0.044715 * 0.7978845608) * square))
        u = a * half
        slope = half + u * (1.0 - half) * (
            2.0 * 0.7978845608 + (6.0 * 0.044715 * 0.7978845608) * square
        )
        u = u.astype(BF)
        da = (dot_nt(gb[rows, :], down) * slope).astype(BF)
        u_all[rows, :] = u
        da_all[rows, :] = da
        branch[rows, :] += dot(u, down)
        dn2[rows, :] += dot_nt(da, up)
    up_grad = dot(n2_t[...], da_all[...])
    down_grad = dot(gb_t[...], u_all[...])
    grads[...] = up_grad.astype(BF)
    scatter_shards(pos_ref, place_ref, grads, send_ref, keep_ref, step + 1)
    grads[...] = down_grad.astype(BF)
    mine = (step ^ pos_ref[0]) & 1 == 0

    @pl.when(mine)
    def _():
        for u in range(4):
            scatter_unit(place_ref, grads, u * part, 5 + u, step, keep_ref, 0)

    @pl.when(jnp.logical_not(mine))
    def _():
        for u in range(4):
            scatter_unit(place_ref, grads, u * part, 5 + u, step, send_ref, 1)

    @pl.when(step == last)
    def _():
        gain = norm_ref[2:3, :]

        def after(i, sums):
            rows = pl.ds(pl.multiple_of(i * 256, 256), 256)
            y_ref[rows, :] = branch[rows, :].astype(BF)
            grad = dn2[rows, :]
            unit = unit_ref[rows, :]
            dh = g_ref[rows, :].astype(F32) * factor_ref[0:1, 0:1] + normalise_back(
                grad, unit, inv_ref[rows, 0:1], gain
            )
            dh_ref[rows, :] = dh
            dh_low = dh.astype(BF)
            do_ref[rows, :] = dot_nt(dh_low, wo[...]).astype(BF)
            return (
                sums[0] + jnp.sum(grad * unit, axis=0, keepdims=True),
                sums[1] + jnp.sum(grad, axis=0, keepdims=True),
                sums[2] + dot_tn(o_ref[rows, :], dh_low),
            )

        empty = jnp.zeros((1, width), F32)
        sums = lax.fori_loop(0, tiles, after, (empty, empty, jnp.zeros((width, width), F32)))
        dnorm_ref[...] = jnp.zeros_like(dnorm_ref)
        dnorm_ref[0:1, :] = sums[0]
        dnorm_ref[1:2, :] = sums[1]
        grads[...] = sums[2].astype(BF)
        scatter_shards(pos_ref, place_ref, grads, send_ref, keep_ref, 0)


def feed(pos, place, domain_rows, x, g, o, norm, pieces, talls):
    length, width = x.shape
    block = width
    height = 5 * (width // 4) + block
    rows = lambda dtype: jax.ShapeDtypeStruct((length, width), dtype)
    out = [
        rows(BF), rows(F32), rows(BF),
        jax.ShapeDtypeStruct((2 * height, width), BF),
        jax.ShapeDtypeStruct((2 * height, width), BF),
        jax.ShapeDtypeStruct((8, width), F32),
    ]
    args = (domain_rows, x, g, o, norm) + tuple(pieces) + tuple(talls)
    return pl.pallas_call(
        feed_kernel,
        grid=(4,),
        in_specs=[pl.BlockSpec(memory_space=pltpu.SMEM)] * 2 + [whole(a) for a in args],
        out_specs=[whole(a) for a in out],
        out_shape=out,
        scratch_shapes=[
            pltpu.VMEM((width, width), BF),
            pltpu.VMEM((4, width, block), BF),
            pltpu.VMEM((4, block, width), BF),
            pltpu.VMEM((length, width), F32),
            pltpu.VMEM((length, width), F32),
            pltpu.VMEM((length, 128), F32),
            pltpu.VMEM((length, width), BF),
            pltpu.VMEM((length, width), BF),
            pltpu.VMEM((width, length), BF),
            pltpu.VMEM((width, length), BF),
            pltpu.VMEM((length, width), F32),
            pltpu.VMEM((width, block), BF),
            pltpu.VMEM((length, block), BF),
            pltpu.VMEM((length, block), BF),
            pltpu.VMEM((8, LANES), F32),
        ],
        compiler_params=pltpu.CompilerParams(
            dimension_semantics=("arbitrary",), vmem_limit_bytes=VMEM_FEED
        ),
        name="feed",
        cost_estimate=CHEAP,
    )(pos, place, *args)


def weight_back_kernel(pos_ref, place_ref, small_ref, n_ref, *refs):
    grads_in, (send_ref, keep_ref, n_t, grads) = refs[:-4], refs[-4:]
    step = pl.program_id(0)

    @pl.when(step == 0)
    def _():
        n_t[...] = n_ref[...].T
        for target in (send_ref, keep_ref):
            target[target.shape[0] - SMALL :, :] = small_ref[...]

    for m in range(4):
        @pl.when(step == m)
        def _():
            total = None
            first = 0
            for j in range(len(grads_in) // 4):
                part = grads_in[4 * j + m]
                last = first + part.shape[0]
                term = dot(n_t[:, first:last], part[...])
                total = term if total is None else total + term
                first = last
            grads[...] = total.astype(BF)

    scatter_shards(pos_ref, place_ref, grads, send_ref, keep_ref, step)


def weight_back(pos, place, small, n, halves):
    length, width = n.shape
    out = jax.ShapeDtypeStruct((2 * width + SMALL, width), BF)
    args = (small, n) + tuple(halves)
    return pl.pallas_call(
        weight_back_kernel,
        grid=(4,),
        in_specs=[pl.BlockSpec(memory_space=pltpu.SMEM)] * 2 + [whole(a) for a in args],
        out_specs=[whole(out)] * 2,
        out_shape=[out] * 2,
        scratch_shapes=[pltpu.VMEM((width, length), BF), pltpu.VMEM((width, width), BF)],
        compiler_params=pltpu.CompilerParams(
            dimension_semantics=("arbitrary",), vmem_limit_bytes=VMEM_BACK
        ),
        name="weight_back",
        cost_estimate=CHEAP,
    )(pos, place, *args)


def input_back_kernel(x_ref, dh_ref, w_ref, norm_ref, dnorm_ref, *refs):
    grads_in, (dx_ref, small_ref, sums, dn_ref) = refs[:-4], refs[-4:]
    step = pl.program_id(0)
    tile = x_ref.shape[0]

    @pl.when(step == 0)
    def _():
        sums[...] = jnp.zeros_like(sums)

    first = 0
    for j in range(len(grads_in) // 4):
        count = grads_in[4 * j].shape[0] // tile
        begin = first

        @pl.when((step >= begin) & (step < begin + count))
        def _():
            rows = pl.ds(pl.multiple_of((step - begin) * tile, tile), tile)
            dn = None
            for m in range(4):
                term = dot_nt(grads_in[4 * j + m][rows, :], w_ref[m])
                dn = term if dn is None else dn + term
            dn_ref[...] = dn

        first += count

    dn = dn_ref[...]
    unit, inv = normalise(x_ref[...].astype(F32))
    dx_ref[...] = dh_ref[...] + normalise_back(dn, unit, inv, norm_ref[0:1, :])
    sums[0:1, :] += jnp.sum(dn * unit, axis=0, keepdims=True)
    sums[1:2, :] += jnp.sum(dn, axis=0, keepdims=True)

    @pl.when(step == pl.num_programs(0) - 1)
    def _():
        small_ref[...] = jnp.concatenate(
            [sums[0:2, :], dnorm_ref[0:2, :], jnp.zeros((SMALL - 4, sums.shape[1]), F32)], axis=0
        ).astype(BF)


def input_back(x, dh, w, norm, dnorm, halves):
    length, width = x.shape
    tile = 256
    block = pl.BlockSpec((tile, width), lambda i: (i, 0))
    small = jax.ShapeDtypeStruct((SMALL, width), BF)
    return pl.pallas_call(
        input_back_kernel,
        grid=(length // tile,),
        in_specs=[block] * 2 + [whole(w), whole(norm), whole(dnorm)] + [whole(a) for a in halves],
        out_specs=[block, whole(small)],
        out_shape=[jax.ShapeDtypeStruct((length, width), F32), small],
        scratch_shapes=[pltpu.VMEM((8, width), F32), pltpu.VMEM((tile, width), F32)],
        compiler_params=pltpu.CompilerParams(
            dimension_semantics=("arbitrary",), vmem_limit_bytes=VMEM_BACK
        ),
        name="input_back",
        cost_estimate=CHEAP,
    )(x, dh, w, norm, dnorm, *halves)


def bits_of(size):
    return [1 << b for b in range(size.bit_length() - 1)]


def split_bits():
    return bits_of(lax.axis_size("dp"))[:3]


def exchange(values, even, odd):
    dp, shard = lax.axis_size("dp"), lax.axis_size("shard")
    perm = []
    for d in range(dp):
        for s in range(shard):
            axis, bit = odd if s % 2 else even
            other = (d ^ bit, s) if axis == "dp" else (d, s ^ bit)
            perm.append((d * shard + s, other[0] * shard + other[1]))
    return lax.ppermute(values, ("dp", "shard"), perm)


def swap(values, axis, bit):
    return exchange(values, (axis, bit), (axis, bit))


def after(values, *others):
    return lax.optimization_barrier((values,) + others)[0]


def places():
    count = 2 ** len(split_bits())
    dp, shard = lax.axis_index("dp"), lax.axis_index("shard")
    piece = jnp.arange(2 * count, dtype=jnp.int32)
    far = (piece // count) ^ (shard // 2)
    along = (piece % count) ^ (dp % count)
    order = 0
    for b in range(len(split_bits())):
        order = order * 2 + ((along >> b) & 1)
    even, odd = far * count + order, order * 2 + far
    mine = shard % 2
    return jnp.stack(
        [jnp.where(mine == 0, even, odd), jnp.where(mine == 0, odd, even)]
    ).astype(jnp.int32)


def phases():
    split = [("dp", b) for b in split_bits()]
    return list(zip([("shard", 2)] + split, split + [("shard", 2)]))


def add_up(parts, low, high):
    total = parts[0][low:high].astype(F32)
    for part in parts[1:]:
        total = total + part[low:high].astype(F32)
    return total.astype(BF)


def add_rest(piece):
    for b in bits_of(lax.axis_size("dp"))[3:]:
        piece = add_up([piece, swap(piece, "dp", b)], 0, piece.shape[0])
    return piece


def gather_plan():
    split = split_bits()
    even = [split[0]] + split[1:][::-1]
    odd = split[::-1]
    return [(("dp", a), ("dp", b)) for a, b in zip(even, odd)]


def gather_index():
    odd = lax.axis_index("shard") % 2
    mask = jnp.zeros((1,), jnp.int32)
    for (_, even_bit), (_, odd_bit) in gather_plan():
        mask = jnp.concatenate([mask, mask | jnp.where(odd == 1, odd_bit, even_bit)])
    return (lax.axis_index("dp") % mask.shape[0]) ^ mask


def adam(master, first, second, grad, rate, decay):
    first_new = 0.5 * first + 0.5 * grad
    second_new = 0.5 * second + 0.5 * grad * grad
    correction = 1.0 - 0.5**STEP
    update = first_new / correction / (jnp.sqrt(second_new / correction) + 1e-08)
    return master - rate * (update + decay * master), first_new, second_new


def gather_rows(index_ref, sources, targets):
    count = index_ref.shape[0]
    rows = LANES // count
    for parts, target in zip(sources, targets):
        units = target.shape[0] // LANES
        for j in range(count):
            source = parts[2 * j // count]
            for u in range(units):
                place = pl.ds(pl.multiple_of(u * LANES + index_ref[j] * rows, rows), rows)
                first = (j % (count // 2) * units + u) * rows
                target[place, :] = source[first : first + rows, :]


def squares_kernel(e0, e1, l0, l1, gn_ref, out_ref):
    total = jnp.sum(jnp.square(gn_ref[...]))
    for ref in (e0, e1, l0, l1):
        values = ref[...].astype(F32)
        total += jnp.sum(values * values)
    out_ref[...] = jnp.full(out_ref.shape, total, F32)


def squares(early, late, gn):
    vmem = pl.BlockSpec(memory_space=pltpu.VMEM)
    return pl.pallas_call(
        squares_kernel,
        in_specs=[vmem] * 5,
        out_specs=vmem,
        out_shape=jax.ShapeDtypeStruct((8, LANES), F32),
        compiler_params=pltpu.CompilerParams(vmem_limit_bytes=VMEM_UNPACK),
        name="squares",
        cost_estimate=CHEAP,
    )(*early, *late, gn)


def clip_factor(square_ref, other_ref):
    norm = jnp.sqrt(square_ref[0:1, 0:1] + other_ref[0:1, 0:1])
    return jnp.minimum(1.0, 1.0 / (norm + 1e-06))


def renew_first_kernel(
    side_ref, index_ref, square_ref, other_ref, e0, e1, l0, l1, gn_ref, nm, nf, ns,
    am, af, as_, um, uf, us, copy_ref, early, late
):
    factor = clip_factor(square_ref, other_ref)
    width = early.shape[1]
    height = am.shape[1]
    gather_rows(index_ref, ((e0, e1), (l0, l1)), (early, late))

    def span(unit):
        return pl.ds(pl.multiple_of(unit * LANES + side_ref[0] * height, height), height)

    for unit in range(8):
        if unit < 5:
            source = late[span(unit), :] if unit < 4 else early[span(0), :]
            state = am[unit], af[unit], as_[unit]
        else:
            source = early[span(unit - 4), :]
            cols = slice((unit - 5) * width, (unit - 4) * width)
            state = um[:, cols], uf[:, cols], us[:, cols]
        new = adam(*state, source.astype(F32) * factor, 0.05, 0.01)
        copy_ref[unit * height : (unit + 1) * height, :] = new[0].astype(BF)
    new = adam(nm[...], nf[...], ns[...], gn_ref[...] * factor, 0.3, 0.0)
    last = copy_ref.shape[0] - SMALL
    copy_ref[last:, :] = jnp.zeros((SMALL, width), BF)
    copy_ref[last : last + 4, 0:LANES] = new[0].astype(BF)


def renew_first(side, index, square, early, late, gn, attn, up, norm):
    five, part, width = attn[0].shape
    hidden = up[0].shape[1]
    smem = pl.BlockSpec(memory_space=pltpu.SMEM)
    copy = jax.ShapeDtypeStruct((8 * part // 2 + SMALL, width), BF)
    return pl.pallas_call(
        renew_first_kernel,
        grid_spec=pltpu.PrefetchScalarGridSpec(
            num_scalar_prefetch=1,
            grid=(1,),
            in_specs=[smem] + [whole(a) for a in (*square, *early, *late, gn, *norm)]
            + [pl.BlockSpec((five, part // 2, width), lambda i, side: (0, side[0], 0))] * 3
            + [pl.BlockSpec((part // 2, hidden), lambda i, side: (side[0], 0))] * 3,
            out_specs=whole(copy),
            scratch_shapes=[
                pltpu.VMEM((2 * early[0].shape[0], width), BF),
                pltpu.VMEM((2 * late[0].shape[0], width), BF),
            ],
        ),
        out_shape=copy,
        compiler_params=pltpu.CompilerParams(
            dimension_semantics=("arbitrary",), vmem_limit_bytes=VMEM_UPDATE
        ),
        name="renew_first",
        cost_estimate=CHEAP,
    )(side, index, *square, *early, *late, gn, *norm, *attn, *up)


def update_kernel(index_ref, square_ref, other_ref, e0, e1, l0, l1, gn_ref, *refs):
    am, af, as_, um, uf, us, dm, df, ds, nm, nf, ns = refs[:12]
    early, late = refs[-2:]
    outs, copy_low, copy_high = refs[12:-4], refs[-4], refs[-3]
    step = pl.program_id(0)
    factor = clip_factor(square_ref, other_ref)
    width = early.shape[1]
    part = late.shape[0] // 4
    blocks = um.shape[1] // width
    height = part // pl.num_programs(0)

    def keep(group, where, unit, size, new):
        for target, value in zip(outs[3 * group : 3 * group + 3], new):
            target[where] = value
        target, unit = (copy_low, unit) if unit < 8 else (copy_high, unit - 8)
        rows = pl.ds(pl.multiple_of(unit * part + step * size, size), size)
        target[rows, :] = new[0].astype(BF)

    @pl.when(step == 0)
    def _():
        gather_rows(index_ref, ((e0, e1), (l0, l1)), (early, late))
        new = adam(nm[...], nf[...], ns[...], gn_ref[...] * factor, 0.3, 0.0)
        outs[9][...], outs[10][...], outs[11][...] = new

    def span(base, size):
        return pl.ds(pl.multiple_of(base + step * size, size), size)

    for m in range(5):
        source = late[span(m * part, height), :] if m < 4 else early[span(0, height), :]
        new = adam(am[m], af[m], as_[m], source.astype(F32) * factor, 0.05, 0.01)
        keep(0, (m, slice(None), slice(None)), m, height, new)
    for j in range(blocks):
        source = early[span((j + 1) * part, height), :]
        cols = (slice(None), slice(j * width, (j + 1) * width))
        new = adam(um[cols], uf[cols], us[cols], source.astype(F32) * factor, 0.05, 0.01)
        keep(1, cols, 5 + j, height, new)
    tall = dm.shape[0]
    source = early[(blocks + 1) * part :, span(0, tall)].astype(F32).T
    new = adam(dm[...], df[...], ds[...], source * factor, 0.05, 0.01)
    keep(2, (slice(None), slice(None)), 5 + blocks, tall, new)


def update(index, square, early, late, gn, attn, up, down, norm):
    steps = 4
    smem = pl.BlockSpec(memory_space=pltpu.SMEM)
    five, part, width = attn[0].shape
    specs = (
        [pl.BlockSpec((five, part // steps, width), lambda i: (0, i, 0))] * 3
        + [pl.BlockSpec((part // steps, up[0].shape[1]), lambda i: (i, 0))] * 3
        + [pl.BlockSpec((down[0].shape[0] // steps, width), lambda i: (i, 0))] * 3
        + [whole(norm[0])] * 3
    )
    arrays = tuple(attn) + tuple(up) + tuple(down) + tuple(norm)
    low = jax.ShapeDtypeStruct((8 * part, width), BF)
    tall, short = 2 * early[0].shape[0], 2 * late[0].shape[0]
    high = jax.ShapeDtypeStruct((tall + short - 8 * part, width), BF)
    return pl.pallas_call(
        update_kernel,
        grid=(steps,),
        in_specs=[smem] + [whole(a) for a in (*square, *early, *late, gn)] + specs,
        out_specs=specs + [whole(low), whole(high)],
        out_shape=[jax.ShapeDtypeStruct(a.shape, F32) for a in arrays] + [low, high],
        scratch_shapes=[pltpu.VMEM((tall, width), BF), pltpu.VMEM((short, width), BF)],
        compiler_params=pltpu.CompilerParams(
            dimension_semantics=("arbitrary",), vmem_limit_bytes=VMEM_UPDATE
        ),
        name="update",
        cost_estimate=CHEAP,
    )(index, *square, *early, *late, gn, *arrays)


def place_unit(pos, source, unit, first, count, attn_ref, up_ref, down_ref, sem):
    width = attn_ref.shape[2]
    blocks = up_ref.shape[1] // width
    tall = down_ref.shape[0] // 4
    rows = pl.ds(pl.multiple_of(pos * LANES + first, count), count)
    if unit < 5:
        target = attn_ref.at[unit, rows, :]
    elif unit < 5 + blocks:
        target = up_ref.at[rows, pl.ds((unit - 5) * width, width)]
    else:
        base = pl.multiple_of(pos * tall + (unit - 5 - blocks) * LANES + first, count)
        target = down_ref.at[pl.ds(base, count), :]
    return pltpu.make_async_copy(source, target, sem)


def run_copies(copies):
    for copy in copies:
        copy.start()
    for copy in copies:
        copy.wait()


def place_whole(pos, piece, unit, outs, sems, copies):
    for j in range(piece.shape[0] // LANES):
        source = piece.at[pl.ds(j * LANES, LANES), :]
        copies.append(place_unit(pos, source, unit + j, 0, LANES, *outs, sems.at[len(copies)]))


def place_half(pos, side, piece, outs, sems, copies):
    half = LANES // 2
    for unit in range(8):
        source = piece.at[pl.ds(unit * half, half), :]
        copies.append(place_unit(pos, source, unit, half * side, half, *outs, sems.at[len(copies)]))


def unpack_near_kernel(pos_ref, side_ref, p0, p1, p2, p3, p4, p5, attn_ref, up_ref, down_ref, sems):
    copies = []
    outs = attn_ref, up_ref, down_ref
    for index, parts in enumerate(((p0, p1), (p2, p3))):
        place_whole(pos_ref[index], parts[0], 0, outs, sems, copies)
        place_whole(pos_ref[index], parts[1], 8, outs, sems, copies)
    for index, piece in enumerate((p4, p5)):
        place_half(pos_ref[2 + index], side_ref[0], piece, outs, sems, copies)
    run_copies(copies)


def unpack_far_kernel(pos_ref, side_ref, p0, p1, p2, p3, *refs):
    outs, sems = refs[3:6], refs[6]
    copies = []
    for index, piece in enumerate((p0, p1)):
        place_half(pos_ref[2 + index], side_ref[0] ^ 1, piece, outs, sems, copies)
    for index, piece in enumerate((p2, p3)):
        place_whole(pos_ref[2 + index], piece, 8, outs, sems, copies)
    run_copies(copies)


def share_copies(pos, side, low, high, first, width, hidden):
    units = (low.shape[0] + high.shape[0]) // LANES
    ours = swap(first, "shard", 2)
    other = swap(after(ours, low), "dp", 1)
    rest = swap(after(high, ours), "shard", 2)
    near = [swap(after(part, ours), "shard", 1) for part in (low, high)]
    ours_too = swap(after(ours, low), "shard", 1)
    first_too = swap(after(first[8 * LANES // 2 :], ours), "shard", 1)
    hbm = pl.BlockSpec(memory_space=pl.ANY)
    vmem = pl.BlockSpec(memory_space=pltpu.VMEM)
    smem = pl.BlockSpec(memory_space=pltpu.SMEM)
    shapes = [
        jax.ShapeDtypeStruct((5, width, width), BF),
        jax.ShapeDtypeStruct((width, hidden), BF),
        jax.ShapeDtypeStruct((hidden, width), BF),
    ]
    params = pltpu.CompilerParams(vmem_limit_bytes=VMEM_UNPACK)
    begun = pl.pallas_call(
        unpack_near_kernel,
        in_specs=[smem, smem] + [vmem] * 6,
        out_specs=[hbm] * 3,
        out_shape=shapes,
        scratch_shapes=[pltpu.SemaphoreType.DMA((2 * (units + 8),))],
        compiler_params=params,
        name="unpack_near",
        cost_estimate=CHEAP,
    )(pos, side, low, high, *near, ours, ours_too)
    a, b, c, d = [
        p[p.shape[0] - SMALL : p.shape[0] - SMALL + 4, :LANES]
        for p in (first, first_too, ours, ours_too)
    ]
    low_bit, high_bit = pos[0] % 2 == 1, pos[0] // 2 == 1
    a, b, c, d = [jnp.where(low_bit, v, u) for u, v in ((a, b), (b, a), (c, d), (d, c))]
    a, b, c, d = [jnp.where(high_bit, v, u) for u, v in ((a, c), (b, d), (c, a), (d, b))]
    norms = jnp.concatenate([a, b, c, d], axis=1)
    far = [other, swap(after(other, begun[0], norms), "shard", 1)]
    far += [rest, swap(after(rest, begun[0], norms), "shard", 1)]
    done = pl.pallas_call(
        unpack_far_kernel,
        in_specs=[smem, smem] + [vmem] * 4 + [hbm] * 3,
        out_specs=[hbm] * 3,
        out_shape=shapes,
        scratch_shapes=[pltpu.SemaphoreType.DMA((2 * units,))],
        input_output_aliases={6: 0, 7: 1, 8: 2},
        compiler_params=params,
        name="unpack_far",
        cost_estimate=CHEAP,
    )(pos, side, *far, *begun)
    return tuple(done) + (norms,)


def shards(
    tokens, out_grad, domain_ids, domain_weight,
    attn_master, attn_first, attn_second,
    up_master, up_first, up_second,
    down_master, down_first, down_second,
    norm_master, norm_first, norm_second,
):
    length, width = tokens.shape
    hidden = up_master.shape[1]
    part = width // 4
    blocks = hidden // width
    dp = lax.axis_index("dp")
    shard = lax.axis_index("shard").astype(jnp.int32)
    pos = shard ^ jnp.arange(4, dtype=jnp.int32)
    half = (dp % 2).astype(jnp.int32)[None]
    place = places()

    small = jnp.pad(norm_master.astype(BF), ((0, SMALL - 4), (0, width - part)))
    rows = attn_master[:4].astype(BF).reshape(4 * part, width)
    own = jnp.concatenate([rows[: 2 * part], small, rows[2 * part :], jnp.zeros_like(small)])
    middle = own.shape[0] // 2
    near = swap(own, "shard", 1)
    ours = lax.dynamic_slice(own, (half[0] * middle, 0), (middle, width))
    far_a = swap(ours, "shard", 2)

    domains = domain_weight.shape[0]
    devices = lax.axis_size("dp") * lax.axis_size("shard") * domain_ids.shape[0]
    onehot = (domain_ids[:, None] == jnp.arange(domains, dtype=jnp.int32)[None, :]).astype(F32)
    counts = jnp.sum(onehot, axis=0)
    dp_bits = bits_of(lax.axis_size("dp"))
    for b in dp_bits[:2]:
        counts = counts + swap(counts, "dp", b)
    far_b = swap(after(far_a, counts), "dp", 1)
    second = jnp.concatenate(
        [attn_master[4].astype(BF)]
        + [up_master[:, j * width : (j + 1) * width].astype(BF) for j in range(blocks)]
    )
    second_far = swap(after(second, counts), "shard", 2)
    for b in dp_bits[2:]:
        counts = counts + after(swap(counts, "dp", b), far_b)
    counts_row = jnp.pad(counts.astype(BF)[None], ((0, SMALL - 1), (0, width - domains)))
    third = jnp.concatenate([down_master.astype(BF), counts_row])
    third_far = swap(third, "shard", 2)
    second = [second, swap(second, "shard", 1), second_far]
    third = [third, swap(third, "shard", 1), third_far]
    domain_rows = jnp.pad(
        jnp.stack([onehot[0], domain_weight * devices / domains]),
        ((0, 6), (0, LANES - domains)),
    )
    far_c = swap(far_a, "shard", 1)
    far = [far_a, far_b, far_c, swap(far_b, "shard", 1)]
    q, k, v, n, e, eb, z, o, weights, scores, keys, values, w, norm = attend(
        pos, half, tokens, [own, near] + far
    )
    for pieces in (second, third):
        pieces.append(swap(after(pieces[2], o), "shard", 1))
    y, dh, do, send, keep, dnorm = feed(
        pos, place, domain_rows, tokens, out_grad, o, norm, second, third
    )

    steps, plan = phases(), gather_plan()
    pieces = 2 ** len(steps)
    rows = keep.shape[0] // pieces

    def forward_phase(parts, phase, rows):
        low = rows * pieces >> (phase + 1)
        return add_up(parts, low, 2 * low)

    saved = (q, k, v, eb, e, z, weights, scores, keys, values)
    chunks = length // CHUNK
    early = [keep, swap(send, "shard", 1)]
    later = mix_back(chunks - 1, 1, (), do, *saved)
    out = after(forward_phase(early, 0, rows), later[0])
    early.append(exchange(out, *steps[0]))
    sooner = mix_back(chunks - 2, chunks - 1, later[4:], after(do, out), *saved)
    back = list(sooner[:4]) + list(later[:4])
    out = after(forward_phase(early, 1, rows), back[0])
    early.append(exchange(out, *steps[1]))
    dx, small = input_back(tokens, after(dh, out), w, norm, dnorm, back)
    send, keep = weight_back(pos, place, small, n, back)
    turn = forward_phase(early, 2, rows)
    got = exchange(turn, *steps[2])
    late = [keep, swap(after(send, turn), "shard", 1)]
    height = keep.shape[0] - SMALL
    thin = height // pieces
    small = add_up(late, height, height + SMALL)

    def late_phase(phase):
        out = jnp.concatenate([forward_phase(late, phase, thin), small])
        return out, exchange(out, *steps[phase])

    def late_sum(got):
        late.append(got)
        return add_up([small, got[got.shape[0] - SMALL :]], 0, SMALL)

    turn, late_got = late_phase(0)
    small = late_sum(late_got)
    turn, late_got = late_phase(1)
    early.append(after(got, turn))
    got = exchange(forward_phase(early, 3, rows), *steps[3])
    small = late_sum(late_got)
    turn, late_got = late_phase(2)
    early.append(after(got, turn))
    early = add_rest(add_up(early, 0, rows))
    got = exchange(early, *plan[0])
    small = late_sum(late_got)
    turn, late_got = late_phase(3)
    early = jnp.concatenate([early, after(got, turn)])
    got = exchange(early, *plan[1])
    small = late_sum(late_got)
    late = add_rest(jnp.concatenate([add_up(late, 0, thin), small]))
    late, small = late[:thin], late[thin:]
    late_got = exchange(late, *plan[0])
    norm_grad = lax.dynamic_slice(small[:4], (0, shard * part), (4, part)).astype(F32)
    late = jnp.concatenate([late, late_got])
    late = jnp.concatenate([late, exchange(late, *plan[1])])
    early = jnp.concatenate([early, after(got, late)])
    got = exchange(early, *plan[2])
    late = (late, exchange(late, *plan[2]))
    early = (early, got)
    square = squares(early, late, norm_grad)
    square = square + swap(square, "shard", 1)
    square = (square, swap(square, "shard", 2))
    index = gather_index()
    clip_norm = jnp.sqrt(square[0][0, 0] + square[1][0, 0])
    attn = (attn_master, attn_first, attn_second)
    up = (up_master, up_first, up_second)
    down = (down_master, down_first, down_second)
    norms = (norm_master, norm_first, norm_second)
    leaving = renew_first(half, index, square, early, late, norm_grad, attn, up, norms)
    *new, low, high = update(
        index, square, early, after(late, leaving), norm_grad, attn, up, down, norms
    )
    copies = share_copies(pos, half, low, high, leaving, width, hidden)
    return (y, dx) + tuple(new) + (clip_norm,) + tuple(copies)


def solution(mesh):
    rows = P(("dp", "shard"), None)
    attn = (P(None, "shard", None),) * 3
    tall = (P("shard", None),) * 6
    norm = (P(None, "shard"),) * 3
    return jax.shard_map(
        shards,
        mesh=mesh,
        in_specs=(rows, rows, P(("dp", "shard")), P()) + attn + tall + norm,
        out_specs=(rows, rows) + attn + tall + norm + (P(),) * 5,
        check_vma=False,
    )
```

```python
import functools
import jax
import jax.numpy as jnp
from jax import lax
from jax.experimental import pallas as pl
from jax.experimental.pallas import tpu as pltpu
from jax.sharding import PartitionSpec as P

BF = jnp.bfloat16
F32 = jnp.float32
MIB = 1024 * 1024
VMEM_ATTEND = 40 * MIB
VMEM_MIX = 44 * MIB
VMEM_FEED = 44 * MIB
VMEM_BACK = 24 * MIB
VMEM_UPDATE = 56 * MIB
VMEM_UNPACK = 24 * MIB
CHUNK = 256
SLOT = 64
GROUP = 256
LANES = 128
SMALL = 16
FIRST_UNITS = 7
DIRECT_UNITS = 3
CHEAP = pl.CostEstimate(flops=1, bytes_accessed=1, transcendentals=0)
STEP = 10
TILE = 512
COUNTS = (1, 2, 1)


def whole(a):
    return pl.BlockSpec(a.shape, lambda *_: (0,) * len(a.shape), pipeline_mode=pl.Buffered(1))


def dot(a, b):
    return jnp.dot(a, b, preferred_element_type=F32)


def dot_nt(a, b):
    return lax.dot_general(a, b, (((1,), (1,)), ((), ())), preferred_element_type=F32)


def dot_tn(a, b):
    return lax.dot_general(a, b, (((0,), (0,)), ((), ())), preferred_element_type=F32)


def head_of(shape, dim):
    return lax.broadcasted_iota(jnp.int32, shape, dim) // SLOT


def block_diagonal(state):
    return jnp.where(head_of(state.shape, 0) == head_of(state.shape, 1), state, 0.0).astype(BF)


def only_head(rows, head):
    return jnp.where(head_of(rows.shape, 1) == head, rows, jnp.zeros_like(rows))


def by_head(rows):
    return jnp.concatenate([only_head(rows, h) for h in range(GROUP // SLOT)], axis=0)


def lower(square):
    size = square.shape[0]
    row = lax.broadcasted_iota(jnp.int16, (size, size), 0)
    col = lax.broadcasted_iota(jnp.int16, (size, size), 1)
    return jnp.concatenate(
        [
            jnp.where(row >= col, square[:, first : first + size].astype(BF), jnp.zeros((), BF))
            for first in range(0, square.shape[1], size)
        ],
        axis=1,
    )


def upper(square):
    size = square.shape[1]
    row = lax.broadcasted_iota(jnp.int16, (size, size), 0)
    col = lax.broadcasted_iota(jnp.int16, (size, size), 1)
    return jnp.concatenate(
        [
            jnp.where(row <= col, square[first : first + size, :].astype(BF), jnp.zeros((), BF))
            for first in range(0, square.shape[0], size)
        ],
        axis=1,
    )


def split_dot(ones, values):
    high = values.astype(BF)
    low = (values - high.astype(F32)).astype(BF)
    return dot(ones, high) + dot(ones, low)


def head_ones():
    return jnp.where(
        head_of((GROUP, GROUP), 0) == head_of((GROUP, GROUP), 1), 1.0, 0.0
    ).astype(BF)


def head_sums(values):
    ones = head_ones()
    high = values.astype(BF)
    low = (values - high.astype(F32)).astype(BF)
    return dot(high, ones) + dot(low, ones)


def head_max(values):
    top = None
    head = head_of(values.shape, 1)
    for index in range(GROUP // SLOT):
        mine = jnp.max(jnp.where(head == index, values, -jnp.inf), axis=1, keepdims=True)
        top = mine if top is None else jnp.where(head == index, mine, top)
    return top


def normalise(values):
    centred = values - jnp.mean(values, axis=-1, keepdims=True)
    inv = lax.rsqrt(jnp.mean(centred * centred, axis=-1, keepdims=True) + 1e-05)
    return centred * inv, inv


def normalise_back(grad, unit, inv, gain):
    scaled = grad * gain
    return inv * (
        scaled
        - jnp.mean(scaled, axis=-1, keepdims=True)
        - unit * jnp.mean(scaled * unit, axis=-1, keepdims=True)
    )


def attend_kernel(
    pos_ref, half_ref, x_ref, near0, near1, far0, far1, far2, far3,
    q_ref, k_ref, v_ref, n_ref, e_ref, eb_ref, z_ref, o_ref, w_ref, s_ref, keys_ref, values_ref,
    weights_ref, norm_ref, keys, values, carry
):
    width = x_ref.shape[1]
    part = width // 4

    @pl.when(pl.program_id(0) == 0)
    def _():
        low = far0.shape[0]

        def rows_of(index, first, count):
            if index < 2:
                return (near0, near1)[index][first : first + count, :]
            a, b = ((far0, far1), (far2, far3))[index - 2]
            if first >= low:
                a, b, first = b, a, first - low
            return jnp.where(half_ref[0] == 0, a[first : first + count, :], b[first : first + count, :])

        for index in range(4):
            rows = pl.ds(pl.multiple_of(pos_ref[index] * part, part), part)
            for m in range(4):
                weights_ref[m, rows, :] = rows_of(index, m * part + SMALL * (m > 1), part)
            norm_ref[:, rows] = rows_of(index, 2 * part, SMALL)[0:8, 0:part].astype(F32)
        carry[...] = jnp.zeros_like(carry)
        keys[...] = jnp.zeros_like(keys)
        values[...] = jnp.zeros_like(values)

    heads = range(GROUP // SLOT)
    groups = range(keys.shape[0])
    cols = [slice(i * GROUP, (i + 1) * GROUP) for i in groups]
    unit, _ = normalise(x_ref[...].astype(F32))
    normed = (unit * norm_ref[0:1, :] + norm_ref[1:2, :]).astype(BF)
    n_ref[...] = normed
    rows = normed.shape[0]
    ones = lower(jnp.ones((rows, rows), F32))
    q, k, v, e, inv = [], [], [], [], []
    for c in cols:
        raised = jnp.exp(dot(normed, weights_ref[3, :, c]))
        z = split_dot(ones, raised) + carry[0:1, c]
        carry[0:1, c] = z[rows - 1 : rows, :]
        e_ref[:, c] = raised
        z_ref[:, c] = z
        e.append(raised.astype(BF))
        inv.append(1.0 / z)
        for m, part_of in enumerate((q, k, v)):
            part_of.append(dot(normed, weights_ref[m, :, c]).astype(BF))
    for i in groups:
        q_ref[:, cols[i]], k_ref[:, cols[i]], v_ref[:, cols[i]] = q[i], k[i], v[i]
        eb_ref[:, cols[i]] = e[i]
    total, value_state = [], []
    for i in groups:
        state = block_diagonal(keys[i])
        keys_ref[i, 0] = state
        total.append(dot(q[i], state))
        state = block_diagonal(values[i])
        values_ref[i, 0] = state
        value_state.append(state)
    es = [by_head(e[i]) for i in groups]
    for i in groups:
        total[i] += dot(lower(dot_nt(q[i], by_head(k[i]))), es[i])
    scores = [total[i] * inv[i] * 0.125 for i in groups]
    raised = [jnp.exp(scores[i] - head_max(scores[i])) for i in groups]
    weights = [raised[i] / head_sums(raised[i]) for i in groups]
    ratio = [(weights[i] * inv[i]).astype(BF) for i in groups]
    out = [dot(ratio[i], value_state[i]) for i in groups]
    for i in groups:
        out[i] += dot(lower(dot_nt(ratio[i], es[i])), by_head(v[i]))
    for i in groups:
        s_ref[:, cols[i]] = scores[i]
        w_ref[:, cols[i]] = weights[i]
        o_ref[:, cols[i]] = out[i].astype(BF)
        keys[i] += dot_tn(k[i], e[i])
        values[i] += dot_tn(e[i], v[i])


def attend(pos, half, x, pieces):
    length, width = x.shape
    steps, groups = length // CHUNK, width // GROUP
    rows = lambda dtype: jax.ShapeDtypeStruct((length, width), dtype)
    block = pl.BlockSpec((CHUNK, width), lambda i: (i, 0))
    state = pl.BlockSpec((groups, 1, GROUP, GROUP), lambda i: (0, i, 0, 0))
    states = jax.ShapeDtypeStruct((groups, steps, GROUP, GROUP), BF)
    full = [jax.ShapeDtypeStruct((4, width, width), BF), jax.ShapeDtypeStruct((8, width), F32)]
    return pl.pallas_call(
        attend_kernel,
        grid=(steps,),
        in_specs=[pl.BlockSpec(memory_space=pltpu.SMEM)] * 2 + [block] + [whole(p) for p in pieces],
        out_specs=[block] * 10 + [state] * 2 + [whole(a) for a in full],
        out_shape=[rows(BF)] * 4
        + [rows(F32), rows(BF), rows(F32), rows(BF), rows(F32), rows(F32), states, states]
        + full,
        scratch_shapes=[pltpu.VMEM((groups, GROUP, GROUP), F32)] * 2 + [pltpu.VMEM((8, width), F32)],
        compiler_params=pltpu.CompilerParams(
            dimension_semantics=("arbitrary",), vmem_limit_bytes=VMEM_ATTEND
        ),
        name="attend",
        cost_estimate=CHEAP,
    )(pos, half, x, *pieces)


def mix_back_kernel(*refs, begun):
    g_ref, q_ref, k_ref, v_ref, eb_ref, e_ref, z_ref, w_ref, s_ref, keys_ref, values_ref = refs[:11]
    before, (dq_ref, dk_ref, dv_ref, dc_ref, later_v, later_k, carry) = refs[11:-7], refs[-7:]

    @pl.when(pl.program_id(0) == 0)
    def _():
        if begun:
            later_v[...], later_k[...], carry[...] = [ref[...] for ref in before]
        else:
            later_v[...] = jnp.zeros_like(later_v)
            later_k[...] = jnp.zeros_like(later_k)
            carry[...] = jnp.zeros_like(carry)

    heads = range(GROUP // SLOT)
    groups = range(later_v.shape[0])
    cols = [slice(i * GROUP, (i + 1) * GROUP) for i in groups]
    g, q, k, v, e = [[ref[:, c] for c in cols] for ref in (g_ref, q_ref, k_ref, v_ref, eb_ref)]
    inv = [1.0 / z_ref[:, c] for c in cols]
    weights = [w_ref[:, c] for c in cols]
    ratio = [(weights[i] * inv[i]).astype(BF) for i in groups]
    es = [by_head(e[i]) for i in groups]
    state = [block_diagonal(later_v[i]) for i in groups]
    d_ratio = [dot_nt(g[i], values_ref[i, 0]) for i in groups]
    dv = [dot(e[i], state[i]) for i in groups]
    de = [dot_nt(v[i], state[i]) for i in groups]
    for i in groups:
        vs = by_head(v[i])
        d_ratio[i] += dot(lower(dot_nt(g[i], vs)), es[i])
        de[i] += dot(upper(dot_nt(vs, g[i])), by_head(ratio[i]))
        dv[i] += dot(upper(dot_nt(es[i], ratio[i])), by_head(g[i]))
    d_weights = [d_ratio[i] * inv[i] for i in groups]
    both = [d_weights[i] * weights[i] for i in groups]
    d_scores = [weights[i] * (d_weights[i] - head_sums(both[i])) for i in groups]
    dn = [(d_scores[i] * inv[i] * 0.125).astype(BF) for i in groups]
    dz = [-(both[i] + d_scores[i] * s_ref[:, cols[i]]) * inv[i] for i in groups]
    state = [block_diagonal(later_k[i]) for i in groups]
    dq = [dot_nt(dn[i], keys_ref[i, 0]) for i in groups]
    dk = [dot(e[i], state[i]) for i in groups]
    de = [de[i] + dot_nt(k[i], state[i]) for i in groups]
    for i in groups:
        ks = by_head(k[i])
        dq[i] += dot(lower(dot_nt(dn[i], es[i])), ks)
        dk[i] += dot(upper(dot_nt(es[i], dn[i])), by_head(q[i]))
        de[i] += dot(upper(dot_nt(ks, q[i])), by_head(dn[i]))
    rows = dz[0].shape[0]
    ones = upper(jnp.ones((rows, rows), F32))
    for i in groups:
        dv_ref[:, cols[i]] = dv[i].astype(BF)
        dq_ref[:, cols[i]] = dq[i].astype(BF)
        dk_ref[:, cols[i]] = dk[i].astype(BF)
        z_sum = split_dot(ones, dz[i]) + carry[0:1, cols[i]]
        carry[0:1, cols[i]] = z_sum[0:1, :]
        dc_ref[:, cols[i]] = ((de[i] + z_sum) * e_ref[:, cols[i]]).astype(BF)
        later_v[i] += dot_tn(ratio[i], g[i])
        later_k[i] += dot_tn(dn[i], q[i])


def mix_back(last, count, before, g, q, k, v, eb, e, z, w, s, keys, values):
    length, width = q.shape
    groups = width // GROUP
    block = pl.BlockSpec((CHUNK, width), lambda i: (last - i, 0))
    state = pl.BlockSpec((groups, 1, GROUP, GROUP), lambda i: (0, last - i, 0, 0))
    out = pl.BlockSpec((CHUNK, width), lambda i: (count - 1 - i, 0))
    rows = jax.ShapeDtypeStruct((count * CHUNK, width), BF)
    sums = [jax.ShapeDtypeStruct((groups, GROUP, GROUP), F32)] * 2
    sums += [jax.ShapeDtypeStruct((8, width), F32)]
    return pl.pallas_call(
        functools.partial(mix_back_kernel, begun=bool(before)),
        grid=(count,),
        in_specs=[block] * 9 + [state] * 2 + [whole(a) for a in before],
        out_specs=[out] * 4 + [whole(a) for a in sums],
        out_shape=[rows] * 4 + sums,
        compiler_params=pltpu.CompilerParams(
            dimension_semantics=("arbitrary",), vmem_limit_bytes=VMEM_MIX
        ),
        name="mix_back",
        cost_estimate=CHEAP,
    )(g, q, k, v, eb, e, z, w, s, keys, values, *before)


def scatter_unit(place_ref, grads, first, unit, shard, target, table):
    count = place_ref.shape[1] // 2
    part = LANES
    rows = part // count
    height = target.shape[0] // LANES * LANES // (2 * count)
    for d in range(count):
        place = place_ref[table, (shard // 2) * count + d]
        where = pl.ds(pl.multiple_of(place * height + unit * rows, rows), rows)
        group = d % 2 * (count // 2) + d // 2
        target[where, :] = grads[pl.ds(pl.multiple_of(first + group * rows, rows), rows), :]


def scatter_shards(pos_ref, place_ref, grads, send_ref, keep_ref, unit):
    for index in range(4):
        pos = pos_ref[index]
        target = send_ref if index % 2 else keep_ref
        scatter_unit(place_ref, grads, pos * LANES, unit, pos, target, index % 2)


def feed_kernel(
    pos_ref, place_ref, domain_ref, x_ref, g_ref, o_ref, norm_ref, p0, p1, p2, p3, t0, t1, t2, t3,
    y_ref, dh_ref, do_ref, send_ref, keep_ref, dnorm_ref,
    wo, w1, w2, branch, unit_ref, inv_ref, n2, gb, n2_t, dn2, grads, u_all, da_all, factor_ref
):
    step = pl.program_id(0)
    last = pl.num_programs(0) - 1
    length, width = x_ref.shape
    part = width // 4
    block = w1.shape[2]
    tiles = length // 256

    @pl.when(step == 0)
    def _():
        for index, (piece, tall) in enumerate(((p0, t0), (p1, t1), (p2, t2), (p3, t3))):
            pos = pos_ref[index]
            rows = pl.ds(pl.multiple_of(pos * part, part), part)
            wo[rows, :] = piece[0:part, :]
            for j in range(4):
                w1[j, rows, :] = piece[(j + 1) * part : (j + 2) * part, :]
            w2[pos] = tall[0:block, :]
        count = sum(t[block : block + SMALL, 0:LANES].astype(F32) for t in (t0, t1, t2, t3))
        share = domain_ref[0:1, :] * domain_ref[1:2, :] / jnp.maximum(count[0:1, :], 1.0)
        factor_ref[...] = jnp.broadcast_to(jnp.sum(share, axis=1, keepdims=True), factor_ref.shape)

        def before(i, _):
            rows = pl.ds(pl.multiple_of(i * 256, 256), 256)
            h1 = x_ref[rows, :].astype(F32) + dot(o_ref[rows, :], wo[...])
            branch[rows, :] = h1
            unit, inv = normalise(h1)
            unit_ref[rows, :] = unit
            inv_ref[rows, :] = jnp.broadcast_to(inv, (256, 128))
            normed = (unit * norm_ref[2:3, :] + norm_ref[3:4, :]).astype(BF)
            n2[rows, :] = normed
            n2_t[:, rows] = normed.T
            grad = (g_ref[rows, :].astype(F32) * factor_ref[0:1, 0:1]).astype(BF)
            gb[rows, :] = grad
            dn2[rows, :] = jnp.zeros((256, width), F32)
            return 0

        lax.fori_loop(0, tiles, before, 0)

    up = w1[step]
    down = w2[step]
    tile = TILE
    for i in range(length // tile):
        rows = slice(i * tile, (i + 1) * tile)
        a = dot(n2[rows, :], up)
        square = a * a
        half = 0.5 + 0.5 * jnp.tanh(a * (0.7978845608 + (0.044715 * 0.7978845608) * square))
        u = a * half
        slope = half + u * (1.0 - half) * (
            2.0 * 0.7978845608 + (6.0 * 0.044715 * 0.7978845608) * square
        )
        u = u.astype(BF)
        da = (dot_nt(gb[rows, :], down) * slope).astype(BF)
        u_all[rows, :] = u
        da_all[rows, :] = da
        branch[rows, :] += dot(u, down)
        dn2[rows, :] += dot_nt(da, up)
    up_grad = dot(n2_t[...], da_all[...])
    down_grad = dot_tn(u_all[...], gb[...])
    grads[...] = up_grad.astype(BF)
    scatter_shards(pos_ref, place_ref, grads, send_ref, keep_ref, step + 1)
    grads[...] = down_grad.astype(BF)
    mine = (step ^ pos_ref[0]) & 1 == 0

    @pl.when(mine)
    def _():
        for u in range(4):
            scatter_unit(place_ref, grads, u * part, 5 + u, step, keep_ref, 0)

    @pl.when(jnp.logical_not(mine))
    def _():
        for u in range(4):
            scatter_unit(place_ref, grads, u * part, 5 + u, step, send_ref, 1)

    @pl.when(step == last)
    def _():
        gain = norm_ref[2:3, :]

        def after(i, sums):
            rows = pl.ds(pl.multiple_of(i * 256, 256), 256)
            y_ref[rows, :] = branch[rows, :].astype(BF)
            grad = dn2[rows, :]
            unit = unit_ref[rows, :]
            dh = g_ref[rows, :].astype(F32) * factor_ref[0:1, 0:1] + normalise_back(
                grad, unit, inv_ref[rows, 0:1], gain
            )
            dh_ref[rows, :] = dh
            dh_low = dh.astype(BF)
            do_ref[rows, :] = dot_nt(dh_low, wo[...]).astype(BF)
            return (
                sums[0] + jnp.sum(grad * unit, axis=0, keepdims=True),
                sums[1] + jnp.sum(grad, axis=0, keepdims=True),
                sums[2] + dot_tn(o_ref[rows, :], dh_low),
            )

        empty = jnp.zeros((1, width), F32)
        sums = lax.fori_loop(0, tiles, after, (empty, empty, jnp.zeros((width, width), F32)))
        dnorm_ref[...] = jnp.zeros_like(dnorm_ref)
        dnorm_ref[0:1, :] = sums[0]
        dnorm_ref[1:2, :] = sums[1]
        grads[...] = sums[2].astype(BF)
        scatter_shards(pos_ref, place_ref, grads, send_ref, keep_ref, 0)


def feed(pos, place, domain_rows, x, g, o, norm, pieces, talls):
    length, width = x.shape
    block = width
    height = 5 * (width // 4) + block
    rows = lambda dtype: jax.ShapeDtypeStruct((length, width), dtype)
    out = [
        rows(BF), rows(F32), rows(BF),
        jax.ShapeDtypeStruct((2 * height, width), BF),
        jax.ShapeDtypeStruct((2 * height, width), BF),
        jax.ShapeDtypeStruct((8, width), F32),
    ]
    args = (domain_rows, x, g, o, norm) + tuple(pieces) + tuple(talls)
    return pl.pallas_call(
        feed_kernel,
        grid=(4,),
        in_specs=[pl.BlockSpec(memory_space=pltpu.SMEM)] * 2 + [whole(a) for a in args],
        out_specs=[whole(a) for a in out],
        out_shape=out,
        scratch_shapes=[
            pltpu.VMEM((width, width), BF),
            pltpu.VMEM((4, width, block), BF),
            pltpu.VMEM((4, block, width), BF),
            pltpu.VMEM((length, width), F32),
            pltpu.VMEM((length, width), F32),
            pltpu.VMEM((length, 128), F32),
            pltpu.VMEM((length, width), BF),
            pltpu.VMEM((length, width), BF),
            pltpu.VMEM((width, length), BF),
            pltpu.VMEM((length, width), F32),
            pltpu.VMEM((width, block), BF),
            pltpu.VMEM((length, block), BF),
            pltpu.VMEM((length, block), BF),
            pltpu.VMEM((8, LANES), F32),
        ],
        compiler_params=pltpu.CompilerParams(
            dimension_semantics=("arbitrary",), vmem_limit_bytes=VMEM_FEED
        ),
        name="feed",
        cost_estimate=CHEAP,
    )(pos, place, *args)


def weight_back_kernel(pos_ref, place_ref, small_ref, n_ref, *refs):
    grads_in, (send_ref, keep_ref, n_t, grads) = refs[:-4], refs[-4:]
    step = pl.program_id(0)

    @pl.when(step == 0)
    def _():
        n_t[...] = n_ref[...].T
        for target in (send_ref, keep_ref):
            target[target.shape[0] - SMALL :, :] = small_ref[...]

    for m in range(4):
        @pl.when(step == m)
        def _():
            total = None
            first = 0
            for j in range(len(grads_in) // 4):
                part = grads_in[4 * j + m]
                last = first + part.shape[0]
                term = dot(n_t[:, first:last], part[...])
                total = term if total is None else total + term
                first = last
            grads[...] = total.astype(BF)

    scatter_shards(pos_ref, place_ref, grads, send_ref, keep_ref, step)


def weight_back(pos, place, small, n, halves):
    length, width = n.shape
    out = jax.ShapeDtypeStruct((2 * width + SMALL, width), BF)
    args = (small, n) + tuple(halves)
    return pl.pallas_call(
        weight_back_kernel,
        grid=(4,),
        in_specs=[pl.BlockSpec(memory_space=pltpu.SMEM)] * 2 + [whole(a) for a in args],
        out_specs=[whole(out)] * 2,
        out_shape=[out] * 2,
        scratch_shapes=[pltpu.VMEM((width, length), BF), pltpu.VMEM((width, width), BF)],
        compiler_params=pltpu.CompilerParams(
            dimension_semantics=("arbitrary",), vmem_limit_bytes=VMEM_BACK
        ),
        name="weight_back",
        cost_estimate=CHEAP,
    )(pos, place, *args)


def input_back_kernel(x_ref, dh_ref, w_ref, norm_ref, dnorm_ref, *refs):
    grads_in, (dx_ref, small_ref, sums, dn_ref) = refs[:-4], refs[-4:]
    step = pl.program_id(0)
    tile = x_ref.shape[0]

    @pl.when(step == 0)
    def _():
        sums[...] = jnp.zeros_like(sums)

    first = 0
    for j in range(len(grads_in) // 4):
        count = grads_in[4 * j].shape[0] // tile
        begin = first

        @pl.when((step >= begin) & (step < begin + count))
        def _():
            rows = pl.ds(pl.multiple_of((step - begin) * tile, tile), tile)
            dn = None
            for m in range(4):
                term = dot_nt(grads_in[4 * j + m][rows, :], w_ref[m])
                dn = term if dn is None else dn + term
            dn_ref[...] = dn

        first += count

    dn = dn_ref[...]
    unit, inv = normalise(x_ref[...].astype(F32))
    dx_ref[...] = dh_ref[...] + normalise_back(dn, unit, inv, norm_ref[0:1, :])
    sums[0:1, :] += jnp.sum(dn * unit, axis=0, keepdims=True)
    sums[1:2, :] += jnp.sum(dn, axis=0, keepdims=True)

    @pl.when(step == pl.num_programs(0) - 1)
    def _():
        small_ref[...] = jnp.concatenate(
            [sums[0:2, :], dnorm_ref[0:2, :], jnp.zeros((SMALL - 4, sums.shape[1]), F32)], axis=0
        ).astype(BF)


def input_back(x, dh, w, norm, dnorm, halves):
    length, width = x.shape
    tile = 256
    block = pl.BlockSpec((tile, width), lambda i: (i, 0))
    small = jax.ShapeDtypeStruct((SMALL, width), BF)
    return pl.pallas_call(
        input_back_kernel,
        grid=(length // tile,),
        in_specs=[block] * 2 + [whole(w), whole(norm), whole(dnorm)] + [whole(a) for a in halves],
        out_specs=[block, whole(small)],
        out_shape=[jax.ShapeDtypeStruct((length, width), F32), small],
        scratch_shapes=[pltpu.VMEM((8, width), F32), pltpu.VMEM((tile, width), F32)],
        compiler_params=pltpu.CompilerParams(
            dimension_semantics=("arbitrary",), vmem_limit_bytes=VMEM_BACK
        ),
        name="input_back",
        cost_estimate=CHEAP,
    )(x, dh, w, norm, dnorm, *halves)


def bits_of(size):
    return [1 << b for b in range(size.bit_length() - 1)]


def split_bits():
    return bits_of(lax.axis_size("dp"))[:3]


def exchange(values, even, odd):
    dp, shard = lax.axis_size("dp"), lax.axis_size("shard")
    perm = []
    for d in range(dp):
        for s in range(shard):
            axis, bit = odd if s % 2 else even
            other = (d ^ bit, s) if axis == "dp" else (d, s ^ bit)
            perm.append((d * shard + s, other[0] * shard + other[1]))
    return lax.ppermute(values, ("dp", "shard"), perm)


def swap(values, axis, bit):
    return exchange(values, (axis, bit), (axis, bit))


def after(values, *others):
    return lax.optimization_barrier((values,) + others)[0]


def places():
    count = 2 ** len(split_bits())
    dp, shard = lax.axis_index("dp"), lax.axis_index("shard")
    piece = jnp.arange(2 * count, dtype=jnp.int32)
    far = (piece // count) ^ (shard // 2)
    along = (piece % count) ^ (dp % count)
    order = 0
    for b in range(len(split_bits())):
        order = order * 2 + ((along >> b) & 1)
    even, odd = far * count + order, order * 2 + far
    mine = shard % 2
    return jnp.stack(
        [jnp.where(mine == 0, even, odd), jnp.where(mine == 0, odd, even)]
    ).astype(jnp.int32)


def phases():
    split = [("dp", b) for b in split_bits()]
    return list(zip([("shard", 2)] + split, split + [("shard", 2)]))


def add_up(parts, low, high):
    total = parts[0][low:high].astype(F32)
    for part in parts[1:]:
        total = total + part[low:high].astype(F32)
    return total.astype(BF)


def add_rest(piece):
    for b in bits_of(lax.axis_size("dp"))[3:]:
        piece = add_up([piece, swap(piece, "dp", b)], 0, piece.shape[0])
    return piece


def gather_plan():
    split = split_bits()
    even = split[1:] + split[:1]
    odd = split[1:][::-1] + split[:1]
    mask = jnp.zeros((1,), jnp.int32)
    for a, b in list(zip(even, odd))[:-1]:
        mask = jnp.concatenate([mask, mask | jnp.where(lax.axis_index("shard") % 2 == 1, b, a)])
    index = ((lax.axis_index("dp") % 2 ** len(split)) ^ mask) // 2
    return [(("dp", a), ("dp", b)) for a, b in zip(even, odd)], index


def adam(master, first, second, grad, rate, decay):
    first_new = 0.5 * first + 0.5 * grad
    second_new = 0.5 * second + 0.5 * grad * grad
    correction = 1.0 - 0.5**STEP
    update = first_new / correction / (jnp.sqrt(second_new / correction) + 1e-08)
    return master - rate * (update + decay * master), first_new, second_new


def gather_rows(index_ref, source, target, span, base):
    count = index_ref.shape[0]
    rows = LANES // 2 // count
    units = target.shape[0] // span
    for j in range(count):
        for u in range(units):
            place = pl.ds(pl.multiple_of(u * span + base + index_ref[j] * rows, rows), rows)
            first = (j * units + u) * rows
            target[place, :] = source[first : first + rows, :]


def squares_kernel(early_ref, late_ref, gn_ref, out_ref):
    total = 0.5 * jnp.sum(jnp.square(gn_ref[...]))
    for ref in (early_ref, late_ref):
        values = ref[...].astype(F32)
        total += jnp.sum(values * values)
    out_ref[...] = jnp.full(out_ref.shape, total, F32)


def squares(early, late, gn):
    vmem = pl.BlockSpec(memory_space=pltpu.VMEM)
    return pl.pallas_call(
        squares_kernel,
        in_specs=[vmem] * 3,
        out_specs=vmem,
        out_shape=jax.ShapeDtypeStruct((8, LANES), F32),
        compiler_params=pltpu.CompilerParams(vmem_limit_bytes=VMEM_UNPACK),
        name="squares",
        cost_estimate=CHEAP,
    )(early, late, gn)


def clip_factor(square_ref, other_ref):
    norm = jnp.sqrt(square_ref[0:1, 0:1] + other_ref[0:1, 0:1])
    return jnp.minimum(1.0, 1.0 / (norm + 1e-06))


def renew_kernel(
    side_ref, index_ref, square_ref, other_ref, early_ref, late_ref, gn_ref, nm, nf, ns,
    am, af, as_, um, uf, us, dm, df, ds, first_ref, second_ref, clip_ref, early, late
):
    factor = clip_factor(square_ref, other_ref)
    width = early.shape[1]
    half = LANES // 2
    gather_rows(index_ref, early_ref, early, half, 0)
    gather_rows(index_ref, late_ref, late, half, 0)
    blocks = um.shape[1] // width
    middle = FIRST_UNITS
    for unit in range(5 + blocks + dm.shape[0]):
        if unit < 4:
            source = late[unit * half : (unit + 1) * half, :]
        else:
            source = early[(unit - 4) * half : (unit - 3) * half, :]
        if unit < 5:
            state = am[unit], af[unit], as_[unit]
        elif unit < 5 + blocks:
            cols = slice((unit - 5) * width, (unit - 4) * width)
            state = um[:, cols], uf[:, cols], us[:, cols]
        else:
            state = [ref[unit - 5 - blocks] for ref in (dm, df, ds)]
        new = adam(*state, source.astype(F32) * factor, 0.05, 0.01)
        target, place = (first_ref, unit) if unit < middle else (second_ref, unit - middle)
        target[place * half : (place + 1) * half, :] = new[0].astype(BF)
    new = adam(nm[...], nf[...], ns[...], gn_ref[...] * factor, 0.3, 0.0)
    last = middle * half
    first_ref[last:, :] = jnp.zeros((SMALL, width), BF)
    first_ref[last : last + 4, 0:LANES] = new[0].astype(BF)
    clip_ref[0] = jnp.sqrt(square_ref[0:1, 0:1] + other_ref[0:1, 0:1])[0, 0]


def renew(side, index, square, early, late, gn, attn, up, down, norm):
    five, part, width = attn[0].shape
    hidden = up[0].shape[1]
    half = part // 2
    down = [a.reshape(a.shape[0] // part, part, width) for a in down]
    units = five + hidden // width + down[0].shape[0]
    first = jax.ShapeDtypeStruct((FIRST_UNITS * half + SMALL, width), BF)
    second = jax.ShapeDtypeStruct(((units - FIRST_UNITS) * half, width), BF)
    tall = down[0].shape[0]
    return pl.pallas_call(
        renew_kernel,
        grid_spec=pltpu.PrefetchScalarGridSpec(
            num_scalar_prefetch=1,
            grid=(1,),
            in_specs=[pl.BlockSpec(memory_space=pltpu.SMEM)]
            + [whole(a) for a in (*square, early, late, gn, *norm)]
            + [pl.BlockSpec((five, half, width), lambda i, side: (0, side[0], 0))] * 3
            + [pl.BlockSpec((half, hidden), lambda i, side: (side[0], 0))] * 3
            + [pl.BlockSpec((tall, half, width), lambda i, side: (0, side[0], 0))] * 3,
            out_specs=[whole(first), whole(second), pl.BlockSpec(memory_space=pltpu.SMEM)],
            scratch_shapes=[pltpu.VMEM(early.shape, BF), pltpu.VMEM(late.shape, BF)],
        ),
        out_shape=[first, second, jax.ShapeDtypeStruct((1,), F32)],
        compiler_params=pltpu.CompilerParams(
            dimension_semantics=("arbitrary",), vmem_limit_bytes=VMEM_UPDATE
        ),
        name="renew",
        cost_estimate=CHEAP,
    )(side, index, *square, early, late, gn, *norm, *attn, *up, *down)


def update_kernel(
    side_ref, index_ref, square_ref, other_ref, early_ref, late_ref, got_ref, gn_ref, *refs
):
    am, af, as_, um, uf, us, dm, df, ds, nm, nf, ns = refs[:12]
    early, late = refs[-2:]
    outs, copy_low, copy_high, other_half = refs[12:-5], refs[-5], refs[-4], refs[-3]
    step = pl.program_id(0)
    factor = clip_factor(square_ref, other_ref)
    width = early.shape[1]
    part = late.shape[0] // 4
    blocks = um.shape[1] // width
    height = part // pl.num_programs(0)
    half = LANES // 2

    def keep(group, where, unit, size, new):
        for target, value in zip(outs[3 * group : 3 * group + 3], new):
            target[where] = value
        target, unit = (copy_low, unit) if unit < 8 else (copy_high, unit - 8)
        rows = pl.ds(pl.multiple_of(unit * part + step * size, size), size)
        target[rows, :] = new[0].astype(BF)

    @pl.when(step == 0)
    def _():
        mine = half * side_ref[0]
        count = late_ref.shape[0]
        gather_rows(index_ref, early_ref, early, part, mine)
        gather_rows(index_ref, late_ref, late, part, mine)
        gather_rows(index_ref, got_ref.at[:count, :], late, part, half - mine)
        gather_rows(index_ref, got_ref.at[count:, :], early, part, half - mine)
        new = adam(nm[...], nf[...], ns[...], gn_ref[...] * factor, 0.3, 0.0)
        outs[9][...], outs[10][...], outs[11][...] = new

    def span(base, size):
        return pl.ds(pl.multiple_of(base + step * size, size), size)

    for m in range(5):
        source = late[span(m * part, height), :] if m < 4 else early[span(0, height), :]
        new = adam(am[m], af[m], as_[m], source.astype(F32) * factor, 0.05, 0.01)
        keep(0, (m, slice(None), slice(None)), m, height, new)
    for j in range(blocks):
        source = early[span((j + 1) * part, height), :]
        cols = (slice(None), slice(j * width, (j + 1) * width))
        new = adam(um[cols], uf[cols], us[cols], source.astype(F32) * factor, 0.05, 0.01)
        keep(1, cols, 5 + j, height, new)
    tall = dm.shape[0]
    source = early[span((blocks + 1) * part, tall), :]
    new = adam(dm[...], df[...], ds[...], source.astype(F32) * factor, 0.05, 0.01)
    keep(2, (slice(None), slice(None)), 5 + blocks, tall, new)

    @pl.when(step == pl.num_programs(0) - 1)
    def _():
        count = other_half.shape[0] // half
        base = copy_high.shape[0] - count * part
        for j in range(count):
            rows = pl.ds(pl.multiple_of(base + j * part + half - half * side_ref[0], half), half)
            other_half[j * half : (j + 1) * half, :] = copy_high[rows, :]


def update(side, index, square, early, late, got, gn, attn, up, down, norm):
    steps = 4
    smem = pl.BlockSpec(memory_space=pltpu.SMEM)
    five, part, width = attn[0].shape
    specs = (
        [pl.BlockSpec((five, part // steps, width), lambda i: (0, i, 0))] * 3
        + [pl.BlockSpec((part // steps, up[0].shape[1]), lambda i: (i, 0))] * 3
        + [pl.BlockSpec((down[0].shape[0] // steps, width), lambda i: (i, 0))] * 3
        + [whole(norm[0])] * 3
    )
    arrays = tuple(attn) + tuple(up) + tuple(down) + tuple(norm)
    low = jax.ShapeDtypeStruct((8 * part, width), BF)
    tall, short = 2 * early.shape[0], 2 * late.shape[0]
    high = jax.ShapeDtypeStruct((tall + short - 8 * part, width), BF)
    other = jax.ShapeDtypeStruct((DIRECT_UNITS * part // 2, width), BF)
    return pl.pallas_call(
        update_kernel,
        grid=(steps,),
        in_specs=[smem] * 2 + [whole(a) for a in (*square, early, late, got, gn)] + specs,
        out_specs=specs + [whole(low), whole(high), whole(other)],
        out_shape=[jax.ShapeDtypeStruct(a.shape, F32) for a in arrays] + [low, high, other],
        scratch_shapes=[pltpu.VMEM((tall, width), BF), pltpu.VMEM((short, width), BF)],
        compiler_params=pltpu.CompilerParams(
            dimension_semantics=("arbitrary",), vmem_limit_bytes=VMEM_UPDATE
        ),
        name="update",
        cost_estimate=CHEAP,
    )(side, index, *square, early, late, got, gn, *arrays)


def place_unit(pos, source, unit, first, count, attn_ref, up_ref, down_ref, sem):
    width = attn_ref.shape[2]
    blocks = up_ref.shape[1] // width
    tall = down_ref.shape[0] // 4
    rows = pl.ds(pl.multiple_of(pos * LANES + first, count), count)
    if unit < 5:
        target = attn_ref.at[unit, rows, :]
    elif unit < 5 + blocks:
        target = up_ref.at[rows, pl.ds((unit - 5) * width, width)]
    else:
        base = pl.multiple_of(pos * tall + (unit - 5 - blocks) * LANES + first, count)
        target = down_ref.at[pl.ds(base, count), :]
    return pltpu.make_async_copy(source, target, sem)


def run_copies(copies):
    for copy in copies:
        copy.start()
    for copy in copies:
        copy.wait()


def place_whole(pos, piece, unit, outs, sems, copies):
    for j in range(piece.shape[0] // LANES):
        source = piece.at[pl.ds(j * LANES, LANES), :]
        copies.append(place_unit(pos, source, unit + j, 0, LANES, *outs, sems.at[len(copies)]))


def place_half(pos, side, piece, unit, outs, sems, copies):
    half = LANES // 2
    for j in range(piece.shape[0] // half):
        source = piece.at[pl.ds(j * half, half), :]
        copies.append(
            place_unit(pos, source, unit + j, half * side, half, *outs, sems.at[len(copies)])
        )


def unpack_near_kernel(pos_ref, side_ref, p0, p1, p2, p3, p4, p5, attn_ref, up_ref, down_ref, sems):
    copies = []
    outs = attn_ref, up_ref, down_ref
    for index, parts in enumerate(((p0, p1), (p2, p3))):
        place_whole(pos_ref[index], parts[0], 0, outs, sems, copies)
        place_whole(pos_ref[index], parts[1], 8, outs, sems, copies)
    for index, piece in enumerate((p4, p5)):
        place_half(pos_ref[2 + index], side_ref[0], piece, 0, outs, sems, copies)
    run_copies(copies)


def unpack_far_kernel(pos_ref, side_ref, *refs):
    pieces, outs, sems = refs[:8], refs[11:14], refs[14]
    copies = []
    other = side_ref[0] ^ 1
    for index in range(2):
        second, first_other, second_other, direct = pieces[4 * index : 4 * index + 4]
        pos = pos_ref[2 + index]
        place_half(pos, side_ref[0], second, FIRST_UNITS, outs, sems, copies)
        place_half(pos, other, first_other, 0, outs, sems, copies)
        place_half(pos, other, second_other, FIRST_UNITS, outs, sems, copies)
        unit = FIRST_UNITS + second_other.shape[0] // (LANES // 2)
        place_half(pos, other, direct, unit, outs, sems, copies)
    run_copies(copies)


def share_copies(pos, side, first, second, low, high, direct, width, hidden):
    units = (low.shape[0] + high.shape[0]) // LANES
    half = LANES // 2
    last_rows = swap(first[FIRST_UNITS * half :], "shard", 1)
    ours, first_too, low, high, direct = lax.optimization_barrier(
        (swap(first, "shard", 2), last_rows, low, high, direct)
    )
    other = swap(ours, "dp", 1)
    second_got = swap(after(second, ours), "shard", 2)
    near = [swap(part, "shard", 1) for part in (low, high)]
    ours_too = swap(ours, "shard", 1)
    a, b, c, d = [
        p[p.shape[0] - SMALL : p.shape[0] - SMALL + 4, :LANES]
        for p in (first, first_too, ours, ours_too)
    ]
    low_bit, high_bit = pos[0] % 2 == 1, pos[0] // 2 == 1
    a, b, c, d = [jnp.where(low_bit, v, u) for u, v in ((a, b), (b, a), (c, d), (d, c))]
    a, b, c, d = [jnp.where(high_bit, v, u) for u, v in ((a, c), (b, d), (c, a), (d, b))]
    norms = jnp.concatenate([a, b, c, d], axis=1)
    hbm = pl.BlockSpec(memory_space=pl.ANY)
    vmem = pl.BlockSpec(memory_space=pltpu.VMEM)
    smem = pl.BlockSpec(memory_space=pltpu.SMEM)
    shapes = [
        jax.ShapeDtypeStruct((5, width, width), BF),
        jax.ShapeDtypeStruct((width, hidden), BF),
        jax.ShapeDtypeStruct((hidden, width), BF),
    ]
    params = pltpu.CompilerParams(vmem_limit_bytes=VMEM_UNPACK)
    begun = pl.pallas_call(
        unpack_near_kernel,
        in_specs=[smem, smem] + [vmem] * 6,
        out_specs=[hbm] * 3,
        out_shape=shapes,
        scratch_shapes=[pltpu.SemaphoreType.DMA((2 * (units + FIRST_UNITS),))],
        compiler_params=params,
        name="unpack_near",
        cost_estimate=CHEAP,
    )(pos, side, after(low, norms), high, *near, ours, ours_too)
    second = after(second_got, begun[0])
    second_other = swap(second[: -direct.shape[0]], "dp", 1)
    direct = swap(after(direct, second), "shard", 2)
    far = [second, other, second_other, direct]
    far += [swap(after(f, begun[0]), "shard", 1) for f in far]
    done = pl.pallas_call(
        unpack_far_kernel,
        in_specs=[smem, smem] + [vmem] * 8 + [hbm] * 3,
        out_specs=[hbm] * 3,
        out_shape=shapes,
        scratch_shapes=[pltpu.SemaphoreType.DMA((4 * units,))],
        input_output_aliases={10: 0, 11: 1, 12: 2},
        compiler_params=params,
        name="unpack_far",
        cost_estimate=CHEAP,
    )(pos, side, *far, *begun)
    return tuple(done) + (norms,)


def shards(
    tokens, out_grad, domain_ids, domain_weight,
    attn_master, attn_first, attn_second,
    up_master, up_first, up_second,
    down_master, down_first, down_second,
    norm_master, norm_first, norm_second,
):
    length, width = tokens.shape
    hidden = up_master.shape[1]
    part = width // 4
    blocks = hidden // width
    dp = lax.axis_index("dp")
    shard = lax.axis_index("shard").astype(jnp.int32)
    pos = shard ^ jnp.arange(4, dtype=jnp.int32)
    half = (dp % 2).astype(jnp.int32)[None]
    place = places()

    small = jnp.pad(norm_master.astype(BF), ((0, SMALL - 4), (0, width - part)))
    rows = attn_master[:4].astype(BF).reshape(4 * part, width)
    own = jnp.concatenate([rows[: 2 * part], small, rows[2 * part :], jnp.zeros_like(small)])
    middle = own.shape[0] // 2
    near = swap(own, "shard", 1)
    ours = lax.dynamic_slice(own, (half[0] * middle, 0), (middle, width))
    far_a = swap(ours, "shard", 2)

    domains = domain_weight.shape[0]
    devices = lax.axis_size("dp") * lax.axis_size("shard") * domain_ids.shape[0]
    onehot = (domain_ids[:, None] == jnp.arange(domains, dtype=jnp.int32)[None, :]).astype(F32)
    counts = jnp.sum(onehot, axis=0)
    dp_bits = bits_of(lax.axis_size("dp"))
    for b in dp_bits[:2]:
        counts = counts + swap(counts, "dp", b)
    far_b = swap(after(far_a, counts), "dp", 1)
    second = jnp.concatenate(
        [attn_master[4].astype(BF)]
        + [up_master[:, j * width : (j + 1) * width].astype(BF) for j in range(blocks)]
    )
    second_far = swap(after(second, counts), "shard", 2)
    for b in dp_bits[2:]:
        counts = counts + after(swap(counts, "dp", b), far_b)
    counts_row = jnp.pad(counts.astype(BF)[None], ((0, SMALL - 1), (0, width - domains)))
    third = jnp.concatenate([down_master.astype(BF), counts_row])
    third_far = swap(third, "shard", 2)
    second = [second, swap(second, "shard", 1), second_far]
    third = [third, swap(third, "shard", 1), third_far]
    domain_rows = jnp.pad(
        jnp.stack([onehot[0], domain_weight * devices / domains]),
        ((0, 6), (0, LANES - domains)),
    )
    far_c = swap(far_a, "shard", 1)
    far = [far_a, far_b, far_c, swap(far_b, "shard", 1)]
    q, k, v, n, e, eb, z, o, weights, scores, keys, values, w, norm = attend(
        pos, half, tokens, [own, near] + far
    )
    for pieces in (second, third):
        pieces.append(swap(after(pieces[2], o), "shard", 1))
    y, dh, do, send, keep, dnorm = feed(
        pos, place, domain_rows, tokens, out_grad, o, norm, second, third
    )

    steps = phases()
    plan, index = gather_plan()
    pieces = 2 ** len(steps)
    rows = keep.shape[0] // pieces

    def forward_phase(parts, phase, rows):
        low = rows * pieces >> (phase + 1)
        return add_up(parts, low, 2 * low)

    saved = (q, k, v, eb, e, z, weights, scores, keys, values)
    chunks = length // CHUNK
    early = [keep, swap(send, "shard", 1)]
    later = mix_back(chunks - 1, 1, (), do, *saved)
    out = after(forward_phase(early, 0, rows), later[0])
    early.append(exchange(out, *steps[0]))
    sooner = mix_back(chunks - 2, chunks - 1, later[4:], after(do, out), *saved)
    back = list(sooner[:4]) + list(later[:4])
    out = after(forward_phase(early, 1, rows), back[0])
    early.append(exchange(out, *steps[1]))
    dx, small = input_back(tokens, after(dh, out), w, norm, dnorm, back)
    send, keep = weight_back(pos, place, small, n, back)
    turn = forward_phase(early, 2, rows)
    got = exchange(turn, *steps[2])
    late = [keep, swap(after(send, turn), "shard", 1)]
    height = keep.shape[0] - SMALL
    thin = height // pieces
    small = add_up(late, height, height + SMALL)

    def late_phase(phase):
        out = jnp.concatenate([forward_phase(late, phase, thin), small])
        return out, exchange(out, *steps[phase])

    def late_sum(got):
        late.append(got)
        return add_up([small, got[got.shape[0] - SMALL :]], 0, SMALL)

    turn, late_got = late_phase(0)
    small = late_sum(late_got)
    turn, late_got = late_phase(1)
    early.append(after(got, turn))
    turn = forward_phase(early, 3, rows)
    got = exchange(turn, *steps[3])
    small = late_sum(after(late_got, turn))
    turn, late_got = late_phase(2)
    early.append(after(got, turn))
    early = add_rest(add_up(early, 0, rows))
    got = exchange(early, *plan[0])
    small = late_sum(after(late_got, early))
    turn, late_got = late_phase(3)
    early = jnp.concatenate([early, after(got, turn)])
    got = exchange(early, *plan[1])
    small = late_sum(after(late_got, early))
    late = add_rest(jnp.concatenate([add_up(late, 0, thin), small]))
    late, small = late[:thin], late[thin:]
    late_got = exchange(late, *plan[0])
    norm_grad = lax.dynamic_slice(small[:4], (0, shard * part), (4, part)).astype(F32)
    late = jnp.concatenate([late, late_got])
    late = jnp.concatenate([late, exchange(late, *plan[1])])
    early = jnp.concatenate([early, after(got, late)])
    square = squares(early, late, norm_grad)
    square = square + swap(square, "dp", 1)
    got = exchange(after(jnp.concatenate([late, early]), square), *plan[2])
    square = square + swap(square, "shard", 1)
    square = (square, swap(square, "shard", 2))
    attn = (attn_master, attn_first, attn_second)
    up = (up_master, up_first, up_second)
    down = (down_master, down_first, down_second)
    norms = (norm_master, norm_first, norm_second)
    first, second, clip_norm = renew(
        half, index, square, early, late, norm_grad, attn, up, down, norms
    )
    *new, low, high, direct = update(
        half, index, square, early, late, after(got, first), norm_grad, attn, up, down, norms
    )
    copies = share_copies(pos, half, first, second, low, high, direct, width, hidden)
    return (y, dx) + tuple(new) + (clip_norm.reshape(()),) + tuple(copies)


def solution(mesh):
    rows = P(("dp", "shard"), None)
    attn = (P(None, "shard", None),) * 3
    tall = (P("shard", None),) * 6
    norm = (P(None, "shard"),) * 3
    return jax.shard_map(
        shards,
        mesh=mesh,
        in_specs=(rows, rows, P(("dp", "shard")), P()) + attn + tall + norm,
        out_specs=(rows, rows) + attn + tall + norm + (P(),) * 5,
        check_vma=False,
    )
```

```python
import functools
import jax
import jax.numpy as jnp
from jax import lax
from jax.experimental import pallas as pl
from jax.experimental.pallas import tpu as pltpu
from jax.sharding import PartitionSpec as P

BF = jnp.bfloat16
F32 = jnp.float32
MIB = 1024 * 1024
VMEM_ATTEND = 40 * MIB
VMEM_MIX = 44 * MIB
VMEM_FEED = 44 * MIB
VMEM_BACK = 24 * MIB
VMEM_UPDATE = 56 * MIB
VMEM_UNPACK = 24 * MIB
CHUNK = 256
SLOT = 64
GROUP = 256
LANES = 128
SMALL = 16
FIRST_UNITS = 7
DIRECT_UNITS = 2
CHEAP = pl.CostEstimate(flops=1, bytes_accessed=1, transcendentals=0)
STEP = 10
TILE = 512
COUNTS = (1, 2, 1)


def whole(a):
    return pl.BlockSpec(a.shape, lambda *_: (0,) * len(a.shape), pipeline_mode=pl.Buffered(1))


def dot(a, b):
    return jnp.dot(a, b, preferred_element_type=F32)


def dot_nt(a, b):
    return lax.dot_general(a, b, (((1,), (1,)), ((), ())), preferred_element_type=F32)


def dot_tn(a, b):
    return lax.dot_general(a, b, (((0,), (0,)), ((), ())), preferred_element_type=F32)


def head_of(shape, dim):
    return lax.broadcasted_iota(jnp.int32, shape, dim) // SLOT


def block_diagonal(state):
    return jnp.where(head_of(state.shape, 0) == head_of(state.shape, 1), state, 0.0).astype(BF)


def only_head(rows, head):
    return jnp.where(head_of(rows.shape, 1) == head, rows, jnp.zeros_like(rows))


def by_head(rows):
    return jnp.concatenate([only_head(rows, h) for h in range(GROUP // SLOT)], axis=0)


def lower(square):
    size = square.shape[0]
    row = lax.broadcasted_iota(jnp.int16, (size, size), 0)
    col = lax.broadcasted_iota(jnp.int16, (size, size), 1)
    return jnp.concatenate(
        [
            jnp.where(row >= col, square[:, first : first + size].astype(BF), jnp.zeros((), BF))
            for first in range(0, square.shape[1], size)
        ],
        axis=1,
    )


def upper(square):
    size = square.shape[1]
    row = lax.broadcasted_iota(jnp.int16, (size, size), 0)
    col = lax.broadcasted_iota(jnp.int16, (size, size), 1)
    return jnp.concatenate(
        [
            jnp.where(row <= col, square[first : first + size, :].astype(BF), jnp.zeros((), BF))
            for first in range(0, square.shape[0], size)
        ],
        axis=1,
    )


def split_dot(ones, values):
    high = values.astype(BF)
    low = (values - high.astype(F32)).astype(BF)
    return dot(ones, high) + dot(ones, low)


def head_ones():
    return jnp.where(
        head_of((GROUP, GROUP), 0) == head_of((GROUP, GROUP), 1), 1.0, 0.0
    ).astype(BF)


def head_sums(values):
    ones = head_ones()
    high = values.astype(BF)
    low = (values - high.astype(F32)).astype(BF)
    return dot(high, ones) + dot(low, ones)


def head_max(values):
    top = None
    head = head_of(values.shape, 1)
    for index in range(GROUP // SLOT):
        mine = jnp.max(jnp.where(head == index, values, -jnp.inf), axis=1, keepdims=True)
        top = mine if top is None else jnp.where(head == index, mine, top)
    return top


def normalise(values):
    centred = values - jnp.mean(values, axis=-1, keepdims=True)
    inv = lax.rsqrt(jnp.mean(centred * centred, axis=-1, keepdims=True) + 1e-05)
    return centred * inv, inv


def normalise_back(grad, unit, inv, gain):
    scaled = grad * gain
    return inv * (
        scaled
        - jnp.mean(scaled, axis=-1, keepdims=True)
        - unit * jnp.mean(scaled * unit, axis=-1, keepdims=True)
    )


def attend_kernel(
    pos_ref, half_ref, x_ref, near0, near1, far0, far1, far2, far3,
    q_ref, k_ref, v_ref, n_ref, e_ref, eb_ref, z_ref, o_ref, w_ref, s_ref, keys_ref, values_ref,
    weights_ref, norm_ref, keys, values, carry
):
    width = x_ref.shape[1]
    part = width // 4

    @pl.when(pl.program_id(0) == 0)
    def _():
        low = far0.shape[0]

        def rows_of(index, first, count):
            if index < 2:
                return (near0, near1)[index][first : first + count, :]
            a, b = ((far0, far1), (far2, far3))[index - 2]
            if first >= low:
                a, b, first = b, a, first - low
            return jnp.where(half_ref[0] == 0, a[first : first + count, :], b[first : first + count, :])

        for index in range(4):
            rows = pl.ds(pl.multiple_of(pos_ref[index] * part, part), part)
            for m in range(4):
                weights_ref[m, rows, :] = rows_of(index, m * part + SMALL * (m > 1), part)
            norm_ref[:, rows] = rows_of(index, 2 * part, SMALL)[0:8, 0:part].astype(F32)
        carry[...] = jnp.zeros_like(carry)
        keys[...] = jnp.zeros_like(keys)
        values[...] = jnp.zeros_like(values)

    heads = range(GROUP // SLOT)
    groups = range(keys.shape[0])
    cols = [slice(i * GROUP, (i + 1) * GROUP) for i in groups]
    unit, _ = normalise(x_ref[...].astype(F32))
    normed = (unit * norm_ref[0:1, :] + norm_ref[1:2, :]).astype(BF)
    n_ref[...] = normed
    rows = normed.shape[0]
    ones = lower(jnp.ones((rows, rows), F32))
    q, k, v, e, inv = [], [], [], [], []
    for c in cols:
        raised = jnp.exp(dot(normed, weights_ref[3, :, c]))
        z = split_dot(ones, raised) + carry[0:1, c]
        carry[0:1, c] = z[rows - 1 : rows, :]
        e_ref[:, c] = raised
        z_ref[:, c] = z
        e.append(raised.astype(BF))
        inv.append(1.0 / z)
        for m, part_of in enumerate((q, k, v)):
            part_of.append(dot(normed, weights_ref[m, :, c]).astype(BF))
    for i in groups:
        q_ref[:, cols[i]], k_ref[:, cols[i]], v_ref[:, cols[i]] = q[i], k[i], v[i]
        eb_ref[:, cols[i]] = e[i]
    total, value_state = [], []
    for i in groups:
        state = block_diagonal(keys[i])
        keys_ref[i, 0] = state
        total.append(dot(q[i], state))
        state = block_diagonal(values[i])
        values_ref[i, 0] = state
        value_state.append(state)
    es = [by_head(e[i]) for i in groups]
    for i in groups:
        total[i] += dot(lower(dot_nt(q[i], by_head(k[i]))), es[i])
    scores = [total[i] * inv[i] * 0.125 for i in groups]
    raised = [jnp.exp(scores[i] - head_max(scores[i])) for i in groups]
    weights = [raised[i] / head_sums(raised[i]) for i in groups]
    ratio = [(weights[i] * inv[i]).astype(BF) for i in groups]
    out = [dot(ratio[i], value_state[i]) for i in groups]
    for i in groups:
        out[i] += dot(lower(dot_nt(ratio[i], es[i])), by_head(v[i]))
    for i in groups:
        s_ref[:, cols[i]] = scores[i]
        w_ref[:, cols[i]] = weights[i]
        o_ref[:, cols[i]] = out[i].astype(BF)
        keys[i] += dot_tn(k[i], e[i])
        values[i] += dot_tn(e[i], v[i])


def attend(pos, half, x, pieces):
    length, width = x.shape
    steps, groups = length // CHUNK, width // GROUP
    rows = lambda dtype: jax.ShapeDtypeStruct((length, width), dtype)
    block = pl.BlockSpec((CHUNK, width), lambda i: (i, 0))
    state = pl.BlockSpec((groups, 1, GROUP, GROUP), lambda i: (0, i, 0, 0))
    states = jax.ShapeDtypeStruct((groups, steps, GROUP, GROUP), BF)
    full = [jax.ShapeDtypeStruct((4, width, width), BF), jax.ShapeDtypeStruct((8, width), F32)]
    return pl.pallas_call(
        attend_kernel,
        grid=(steps,),
        in_specs=[pl.BlockSpec(memory_space=pltpu.SMEM)] * 2 + [block] + [whole(p) for p in pieces],
        out_specs=[block] * 10 + [state] * 2 + [whole(a) for a in full],
        out_shape=[rows(BF)] * 4
        + [rows(F32), rows(BF), rows(F32), rows(BF), rows(F32), rows(F32), states, states]
        + full,
        scratch_shapes=[pltpu.VMEM((groups, GROUP, GROUP), F32)] * 2 + [pltpu.VMEM((8, width), F32)],
        compiler_params=pltpu.CompilerParams(
            dimension_semantics=("arbitrary",), vmem_limit_bytes=VMEM_ATTEND
        ),
        name="attend",
        cost_estimate=CHEAP,
    )(pos, half, x, *pieces)


def mix_back_kernel(*refs, begun):
    g_ref, q_ref, k_ref, v_ref, eb_ref, e_ref, z_ref, w_ref, s_ref, keys_ref, values_ref = refs[:11]
    before, (dq_ref, dk_ref, dv_ref, dc_ref, later_v, later_k, carry) = refs[11:-7], refs[-7:]

    @pl.when(pl.program_id(0) == 0)
    def _():
        if begun:
            later_v[...], later_k[...], carry[...] = [ref[...] for ref in before]
        else:
            later_v[...] = jnp.zeros_like(later_v)
            later_k[...] = jnp.zeros_like(later_k)
            carry[...] = jnp.zeros_like(carry)

    heads = range(GROUP // SLOT)
    groups = range(later_v.shape[0])
    cols = [slice(i * GROUP, (i + 1) * GROUP) for i in groups]
    g, q, k, v, e = [[ref[:, c] for c in cols] for ref in (g_ref, q_ref, k_ref, v_ref, eb_ref)]
    inv = [1.0 / z_ref[:, c] for c in cols]
    weights = [w_ref[:, c] for c in cols]
    ratio = [(weights[i] * inv[i]).astype(BF) for i in groups]
    es = [by_head(e[i]) for i in groups]
    state = [block_diagonal(later_v[i]) for i in groups]
    d_ratio = [dot_nt(g[i], values_ref[i, 0]) for i in groups]
    dv = [dot(e[i], state[i]) for i in groups]
    de = [dot_nt(v[i], state[i]) for i in groups]
    for i in groups:
        vs = by_head(v[i])
        d_ratio[i] += dot(lower(dot_nt(g[i], vs)), es[i])
        de[i] += dot(upper(dot_nt(vs, g[i])), by_head(ratio[i]))
        dv[i] += dot(upper(dot_nt(es[i], ratio[i])), by_head(g[i]))
    d_weights = [d_ratio[i] * inv[i] for i in groups]
    both = [d_weights[i] * weights[i] for i in groups]
    d_scores = [weights[i] * (d_weights[i] - head_sums(both[i])) for i in groups]
    dn = [(d_scores[i] * inv[i] * 0.125).astype(BF) for i in groups]
    dz = [-(both[i] + d_scores[i] * s_ref[:, cols[i]]) * inv[i] for i in groups]
    state = [block_diagonal(later_k[i]) for i in groups]
    dq = [dot_nt(dn[i], keys_ref[i, 0]) for i in groups]
    dk = [dot(e[i], state[i]) for i in groups]
    de = [de[i] + dot_nt(k[i], state[i]) for i in groups]
    for i in groups:
        ks = by_head(k[i])
        dq[i] += dot(lower(dot_nt(dn[i], es[i])), ks)
        dk[i] += dot(upper(dot_nt(es[i], dn[i])), by_head(q[i]))
        de[i] += dot(upper(dot_nt(ks, q[i])), by_head(dn[i]))
    rows = dz[0].shape[0]
    ones = upper(jnp.ones((rows, rows), F32))
    for i in groups:
        dv_ref[:, cols[i]] = dv[i].astype(BF)
        dq_ref[:, cols[i]] = dq[i].astype(BF)
        dk_ref[:, cols[i]] = dk[i].astype(BF)
        z_sum = split_dot(ones, dz[i]) + carry[0:1, cols[i]]
        carry[0:1, cols[i]] = z_sum[0:1, :]
        dc_ref[:, cols[i]] = ((de[i] + z_sum) * e_ref[:, cols[i]]).astype(BF)
        later_v[i] += dot_tn(ratio[i], g[i])
        later_k[i] += dot_tn(dn[i], q[i])


def mix_back(last, count, before, g, q, k, v, eb, e, z, w, s, keys, values):
    length, width = q.shape
    groups = width // GROUP
    block = pl.BlockSpec((CHUNK, width), lambda i: (last - i, 0))
    state = pl.BlockSpec((groups, 1, GROUP, GROUP), lambda i: (0, last - i, 0, 0))
    out = pl.BlockSpec((CHUNK, width), lambda i: (count - 1 - i, 0))
    rows = jax.ShapeDtypeStruct((count * CHUNK, width), BF)
    sums = [jax.ShapeDtypeStruct((groups, GROUP, GROUP), F32)] * 2
    sums += [jax.ShapeDtypeStruct((8, width), F32)]
    return pl.pallas_call(
        functools.partial(mix_back_kernel, begun=bool(before)),
        grid=(count,),
        in_specs=[block] * 9 + [state] * 2 + [whole(a) for a in before],
        out_specs=[out] * 4 + [whole(a) for a in sums],
        out_shape=[rows] * 4 + sums,
        compiler_params=pltpu.CompilerParams(
            dimension_semantics=("arbitrary",), vmem_limit_bytes=VMEM_MIX
        ),
        name="mix_back",
        cost_estimate=CHEAP,
    )(g, q, k, v, eb, e, z, w, s, keys, values, *before)


def scatter_unit(place_ref, grads, first, unit, shard, target, table):
    count = place_ref.shape[1] // 2
    part = LANES
    rows = part // count
    height = target.shape[0] // LANES * LANES // (2 * count)
    for d in range(count):
        place = place_ref[table, (shard // 2) * count + d]
        where = pl.ds(pl.multiple_of(place * height + unit * rows, rows), rows)
        group = d % 2 * (count // 2) + d // 2
        target[where, :] = grads[pl.ds(pl.multiple_of(first + group * rows, rows), rows), :]


def scatter_shards(pos_ref, place_ref, grads, send_ref, keep_ref, unit):
    for index in range(4):
        pos = pos_ref[index]
        target = send_ref if index % 2 else keep_ref
        scatter_unit(place_ref, grads, pos * LANES, unit, pos, target, index % 2)


def feed_kernel(
    pos_ref, place_ref, domain_ref, x_ref, g_ref, o_ref, norm_ref, p0, p1, p2, p3, t0, t1, t2, t3,
    y_ref, dh_ref, do_ref, send_ref, keep_ref, dnorm_ref,
    wo, w1, w2, branch, unit_ref, inv_ref, n2, gb, n2_t, dn2, grads, u_all, da_all, factor_ref
):
    step = pl.program_id(0)
    last = pl.num_programs(0) - 1
    length, width = x_ref.shape
    part = width // 4
    block = w1.shape[2]
    tiles = length // 256

    @pl.when(step == 0)
    def _():
        for index, (piece, tall) in enumerate(((p0, t0), (p1, t1), (p2, t2), (p3, t3))):
            pos = pos_ref[index]
            rows = pl.ds(pl.multiple_of(pos * part, part), part)
            wo[rows, :] = piece[0:part, :]
            for j in range(4):
                w1[j, rows, :] = piece[(j + 1) * part : (j + 2) * part, :]
            w2[pos] = tall[0:block, :]
        count = sum(t[block : block + SMALL, 0:LANES].astype(F32) for t in (t0, t1, t2, t3))
        share = domain_ref[0:1, :] * domain_ref[1:2, :] / jnp.maximum(count[0:1, :], 1.0)
        factor_ref[...] = jnp.broadcast_to(jnp.sum(share, axis=1, keepdims=True), factor_ref.shape)

        def before(i, _):
            rows = pl.ds(pl.multiple_of(i * 256, 256), 256)
            h1 = x_ref[rows, :].astype(F32) + dot(o_ref[rows, :], wo[...])
            branch[rows, :] = h1
            unit, inv = normalise(h1)
            unit_ref[rows, :] = unit
            inv_ref[rows, :] = jnp.broadcast_to(inv, (256, 128))
            normed = (unit * norm_ref[2:3, :] + norm_ref[3:4, :]).astype(BF)
            n2[rows, :] = normed
            n2_t[:, rows] = normed.T
            grad = (g_ref[rows, :].astype(F32) * factor_ref[0:1, 0:1]).astype(BF)
            gb[rows, :] = grad
            dn2[rows, :] = jnp.zeros((256, width), F32)
            return 0

        lax.fori_loop(0, tiles, before, 0)

    up = w1[step]
    down = w2[step]
    tile = TILE
    for i in range(length // tile):
        rows = slice(i * tile, (i + 1) * tile)
        a = dot(n2[rows, :], up)
        square = a * a
        half = 0.5 + 0.5 * jnp.tanh(a * (0.7978845608 + (0.044715 * 0.7978845608) * square))
        u = a * half
        slope = half + u * (1.0 - half) * (
            2.0 * 0.7978845608 + (6.0 * 0.044715 * 0.7978845608) * square
        )
        u = u.astype(BF)
        da = (dot_nt(gb[rows, :], down) * slope).astype(BF)
        u_all[rows, :] = u
        da_all[rows, :] = da
        branch[rows, :] += dot(u, down)
        dn2[rows, :] += dot_nt(da, up)
    up_grad = dot(n2_t[...], da_all[...])
    down_grad = dot_tn(u_all[...], gb[...])
    grads[...] = up_grad.astype(BF)
    scatter_shards(pos_ref, place_ref, grads, send_ref, keep_ref, step + 1)
    grads[...] = down_grad.astype(BF)
    mine = (step ^ pos_ref[0]) & 1 == 0

    @pl.when(mine)
    def _():
        for u in range(4):
            scatter_unit(place_ref, grads, u * part, 5 + u, step, keep_ref, 0)

    @pl.when(jnp.logical_not(mine))
    def _():
        for u in range(4):
            scatter_unit(place_ref, grads, u * part, 5 + u, step, send_ref, 1)

    @pl.when(step == last)
    def _():
        gain = norm_ref[2:3, :]

        def after(i, sums):
            rows = pl.ds(pl.multiple_of(i * 256, 256), 256)
            y_ref[rows, :] = branch[rows, :].astype(BF)
            grad = dn2[rows, :]
            unit = unit_ref[rows, :]
            dh = g_ref[rows, :].astype(F32) * factor_ref[0:1, 0:1] + normalise_back(
                grad, unit, inv_ref[rows, 0:1], gain
            )
            dh_ref[rows, :] = dh
            dh_low = dh.astype(BF)
            do_ref[rows, :] = dot_nt(dh_low, wo[...]).astype(BF)
            return (
                sums[0] + jnp.sum(grad * unit, axis=0, keepdims=True),
                sums[1] + jnp.sum(grad, axis=0, keepdims=True),
                sums[2] + dot_tn(o_ref[rows, :], dh_low),
            )

        empty = jnp.zeros((1, width), F32)
        sums = lax.fori_loop(0, tiles, after, (empty, empty, jnp.zeros((width, width), F32)))
        dnorm_ref[...] = jnp.zeros_like(dnorm_ref)
        dnorm_ref[0:1, :] = sums[0]
        dnorm_ref[1:2, :] = sums[1]
        grads[...] = sums[2].astype(BF)
        scatter_shards(pos_ref, place_ref, grads, send_ref, keep_ref, 0)


def feed(pos, place, domain_rows, x, g, o, norm, pieces, talls):
    length, width = x.shape
    block = width
    height = 5 * (width // 4) + block
    rows = lambda dtype: jax.ShapeDtypeStruct((length, width), dtype)
    out = [
        rows(BF), rows(F32), rows(BF),
        jax.ShapeDtypeStruct((2 * height, width), BF),
        jax.ShapeDtypeStruct((2 * height, width), BF),
        jax.ShapeDtypeStruct((8, width), F32),
    ]
    args = (domain_rows, x, g, o, norm) + tuple(pieces) + tuple(talls)
    return pl.pallas_call(
        feed_kernel,
        grid=(4,),
        in_specs=[pl.BlockSpec(memory_space=pltpu.SMEM)] * 2 + [whole(a) for a in args],
        out_specs=[whole(a) for a in out],
        out_shape=out,
        scratch_shapes=[
            pltpu.VMEM((width, width), BF),
            pltpu.VMEM((4, width, block), BF),
            pltpu.VMEM((4, block, width), BF),
            pltpu.VMEM((length, width), F32),
            pltpu.VMEM((length, width), F32),
            pltpu.VMEM((length, 128), F32),
            pltpu.VMEM((length, width), BF),
            pltpu.VMEM((length, width), BF),
            pltpu.VMEM((width, length), BF),
            pltpu.VMEM((length, width), F32),
            pltpu.VMEM((width, block), BF),
            pltpu.VMEM((length, block), BF),
            pltpu.VMEM((length, block), BF),
            pltpu.VMEM((8, LANES), F32),
        ],
        compiler_params=pltpu.CompilerParams(
            dimension_semantics=("arbitrary",), vmem_limit_bytes=VMEM_FEED
        ),
        name="feed",
        cost_estimate=CHEAP,
    )(pos, place, *args)


def weight_back_kernel(pos_ref, place_ref, small_ref, n_ref, *refs):
    grads_in, (send_ref, keep_ref, n_t, grads) = refs[:-4], refs[-4:]
    step = pl.program_id(0)

    @pl.when(step == 0)
    def _():
        n_t[...] = n_ref[...].T
        for target in (send_ref, keep_ref):
            target[target.shape[0] - SMALL :, :] = small_ref[...]

    for m in range(4):
        @pl.when(step == m)
        def _():
            total = None
            first = 0
            for j in range(len(grads_in) // 4):
                part = grads_in[4 * j + m]
                last = first + part.shape[0]
                term = dot(n_t[:, first:last], part[...])
                total = term if total is None else total + term
                first = last
            grads[...] = total.astype(BF)

    scatter_shards(pos_ref, place_ref, grads, send_ref, keep_ref, step)


def weight_back(pos, place, small, n, halves):
    length, width = n.shape
    out = jax.ShapeDtypeStruct((2 * width + SMALL, width), BF)
    args = (small, n) + tuple(halves)
    return pl.pallas_call(
        weight_back_kernel,
        grid=(4,),
        in_specs=[pl.BlockSpec(memory_space=pltpu.SMEM)] * 2 + [whole(a) for a in args],
        out_specs=[whole(out)] * 2,
        out_shape=[out] * 2,
        scratch_shapes=[pltpu.VMEM((width, length), BF), pltpu.VMEM((width, width), BF)],
        compiler_params=pltpu.CompilerParams(
            dimension_semantics=("arbitrary",), vmem_limit_bytes=VMEM_BACK
        ),
        name="weight_back",
        cost_estimate=CHEAP,
    )(pos, place, *args)


def input_back_kernel(x_ref, dh_ref, w_ref, norm_ref, dnorm_ref, *refs):
    grads_in, (dx_ref, small_ref, sums, dn_ref) = refs[:-4], refs[-4:]
    step = pl.program_id(0)
    tile = x_ref.shape[0]

    @pl.when(step == 0)
    def _():
        sums[...] = jnp.zeros_like(sums)

    first = 0
    for j in range(len(grads_in) // 4):
        count = grads_in[4 * j].shape[0] // tile
        begin = first

        @pl.when((step >= begin) & (step < begin + count))
        def _():
            rows = pl.ds(pl.multiple_of((step - begin) * tile, tile), tile)
            dn = None
            for m in range(4):
                term = dot_nt(grads_in[4 * j + m][rows, :], w_ref[m])
                dn = term if dn is None else dn + term
            dn_ref[...] = dn

        first += count

    dn = dn_ref[...]
    unit, inv = normalise(x_ref[...].astype(F32))
    dx_ref[...] = dh_ref[...] + normalise_back(dn, unit, inv, norm_ref[0:1, :])
    sums[0:1, :] += jnp.sum(dn * unit, axis=0, keepdims=True)
    sums[1:2, :] += jnp.sum(dn, axis=0, keepdims=True)

    @pl.when(step == pl.num_programs(0) - 1)
    def _():
        small_ref[...] = jnp.concatenate(
            [sums[0:2, :], dnorm_ref[0:2, :], jnp.zeros((SMALL - 4, sums.shape[1]), F32)], axis=0
        ).astype(BF)


def input_back(x, dh, w, norm, dnorm, halves):
    length, width = x.shape
    tile = 256
    block = pl.BlockSpec((tile, width), lambda i: (i, 0))
    small = jax.ShapeDtypeStruct((SMALL, width), BF)
    return pl.pallas_call(
        input_back_kernel,
        grid=(length // tile,),
        in_specs=[block] * 2 + [whole(w), whole(norm), whole(dnorm)] + [whole(a) for a in halves],
        out_specs=[block, whole(small)],
        out_shape=[jax.ShapeDtypeStruct((length, width), F32), small],
        scratch_shapes=[pltpu.VMEM((8, width), F32), pltpu.VMEM((tile, width), F32)],
        compiler_params=pltpu.CompilerParams(
            dimension_semantics=("arbitrary",), vmem_limit_bytes=VMEM_BACK
        ),
        name="input_back",
        cost_estimate=CHEAP,
    )(x, dh, w, norm, dnorm, *halves)


def bits_of(size):
    return [1 << b for b in range(size.bit_length() - 1)]


def exchange(values, even, odd):
    dp, shard = lax.axis_size("dp"), lax.axis_size("shard")
    perm = []
    for d in range(dp):
        for s in range(shard):
            axis, bit = odd if s % 2 else even
            other = (d ^ bit, s) if axis == "dp" else (d, s ^ bit)
            perm.append((d * shard + s, other[0] * shard + other[1]))
    return lax.ppermute(values, ("dp", "shard"), perm)


def swap(values, axis, bit):
    return exchange(values, (axis, bit), (axis, bit))


def after(values, *others):
    return lax.optimization_barrier((values,) + others)[0]


def places():
    dp, shard = lax.axis_index("dp"), lax.axis_index("shard")
    piece = jnp.arange(16, dtype=jnp.int32)
    far = (piece // 8) ^ (shard // 2)
    along = (piece % 8) ^ (dp % 8)
    bits = [(along >> b) & 1 for b in range(3)]
    even = far * 8 + bits[0] * 4 + bits[2] * 2 + (piece >> 1 & 1)
    odd = bits[0] * 8 + bits[1] * 4 + far * 2 + (piece >> 2 & 1)
    mine = shard % 2
    return jnp.stack(
        [jnp.where(mine == 0, even, odd), jnp.where(mine == 0, odd, even)]
    ).astype(jnp.int32)


HALVINGS = [
    (("shard", 2), ("dp", 1)),
    (("dp", 1), ("dp", 2)),
    (("dp", 4), ("shard", 2)),
]
MIDDLE = (("dp", 2), ("dp", 4))
GATHERS = [(("dp", 4), ("dp", 2)), (("dp", 1), ("dp", 1))]


def quarters():
    place = lax.axis_index("dp") % 8
    j = jnp.arange(4, dtype=jnp.int32)
    even = j % 2 + 2 * ((place // 4) ^ (j // 2))
    odd = 2 * (j % 2) + ((place // 2 % 2) ^ (j // 2))
    return jnp.where(lax.axis_index("shard") % 2 == 0, even, odd).astype(jnp.int32)


def low_sum(total):
    return lax.reduce_precision(total, 8, 7).astype(BF)


def add_up(parts, low, high):
    total = parts[0][low:high].astype(F32)
    for part in parts[1:]:
        total = total + part[low:high].astype(F32)
    return low_sum(total)


def add_rest(piece):
    for b in bits_of(lax.axis_size("dp"))[3:]:
        piece = add_up([piece, swap(piece, "dp", b)], 0, piece.shape[0])
    return piece


def adam(master, first, second, grad, rate, decay):
    first_new = 0.5 * first + 0.5 * grad
    second_new = 0.5 * second + 0.5 * grad * grad
    correction = 1.0 - 0.5**STEP
    update = first_new / correction / (jnp.sqrt(second_new / correction) + 1e-08)
    return master - rate * (update + decay * master), first_new, second_new


def gather_rows(index_ref, source, target, span, base):
    count = index_ref.shape[0]
    rows = LANES // 2 // count
    units = target.shape[0] // span
    for j in range(count):
        for u in range(units):
            place = pl.ds(pl.multiple_of(u * span + base + index_ref[j] * rows, rows), rows)
            first = (j * units + u) * rows
            target[place, :] = source[first : first + rows, :]


def squares_kernel(early_ref, late_ref, gn_ref, out_ref):
    total = 0.5 * jnp.sum(jnp.square(gn_ref[...]))
    for ref in (early_ref, late_ref):
        values = ref[...].astype(F32)
        total += jnp.sum(values * values)
    out_ref[...] = jnp.full(out_ref.shape, total, F32)


def squares(early, late, gn):
    vmem = pl.BlockSpec(memory_space=pltpu.VMEM)
    return pl.pallas_call(
        squares_kernel,
        in_specs=[vmem] * 3,
        out_specs=vmem,
        out_shape=jax.ShapeDtypeStruct((8, LANES), F32),
        compiler_params=pltpu.CompilerParams(vmem_limit_bytes=VMEM_UNPACK),
        name="squares",
        cost_estimate=CHEAP,
    )(early, late, gn)


def clip_factor(square_ref, other_ref):
    norm = jnp.sqrt(square_ref[0:1, 0:1] + other_ref[0:1, 0:1])
    return jnp.minimum(1.0, 1.0 / (norm + 1e-06))


def renew_kernel(
    side_ref, index_ref, square_ref, other_ref, early_ref, late_ref, gn_ref, nm, nf, ns,
    am, af, as_, um, uf, us, dm, df, ds, first_ref, second_ref, clip_ref, early, late
):
    factor = clip_factor(square_ref, other_ref)
    width = early.shape[1]
    half = LANES // 2
    step = pl.program_id(0)
    height = am.shape[1]

    @pl.when(step == 0)
    def _():
        gather_rows(index_ref, early_ref, early, half, 0)
        gather_rows(index_ref, late_ref, late, half, 0)
        new = adam(nm[...], nf[...], ns[...], gn_ref[...] * factor, 0.3, 0.0)
        last = FIRST_UNITS * half
        first_ref[last:, :] = jnp.zeros((SMALL, width), BF)
        first_ref[last : last + 4, 0:LANES] = new[0].astype(BF)
        clip_ref[0] = jnp.sqrt(square_ref[0:1, 0:1] + other_ref[0:1, 0:1])[0, 0]

    def span(unit):
        return pl.ds(pl.multiple_of(unit * half + step * height, height), height)

    blocks = um.shape[1] // width
    middle = FIRST_UNITS
    for unit in range(5 + blocks + dm.shape[0]):
        if unit < 4:
            source = late[span(unit), :]
        else:
            source = early[span(unit - 4), :]
        if unit < 5:
            state = am[unit], af[unit], as_[unit]
        elif unit < 5 + blocks:
            cols = slice((unit - 5) * width, (unit - 4) * width)
            state = um[:, cols], uf[:, cols], us[:, cols]
        else:
            state = [ref[unit - 5 - blocks] for ref in (dm, df, ds)]
        new = adam(*state, source.astype(F32) * factor, 0.05, 0.01)
        target, place = (first_ref, unit) if unit < middle else (second_ref, unit - middle)
        target[span(place), :] = new[0].astype(BF)


def renew(side, index, square, early, late, gn, attn, up, down, norm):
    five, part, width = attn[0].shape
    hidden = up[0].shape[1]
    steps = 2
    half = part // 2
    tile = half // steps
    down = [a.reshape(a.shape[0] // part, part, width) for a in down]
    units = five + hidden // width + down[0].shape[0]
    first = jax.ShapeDtypeStruct((FIRST_UNITS * half + SMALL, width), BF)
    second = jax.ShapeDtypeStruct(((units - FIRST_UNITS) * half, width), BF)
    tall = down[0].shape[0]
    return pl.pallas_call(
        renew_kernel,
        grid_spec=pltpu.PrefetchScalarGridSpec(
            num_scalar_prefetch=1,
            grid=(steps,),
            in_specs=[pl.BlockSpec(memory_space=pltpu.SMEM)]
            + [whole(a) for a in (*square, early, late, gn, *norm)]
            + [pl.BlockSpec((five, tile, width), lambda i, side: (0, steps * side[0] + i, 0))] * 3
            + [pl.BlockSpec((tile, hidden), lambda i, side: (steps * side[0] + i, 0))] * 3
            + [pl.BlockSpec((tall, tile, width), lambda i, side: (0, steps * side[0] + i, 0))] * 3,
            out_specs=[whole(first), whole(second), pl.BlockSpec(memory_space=pltpu.SMEM)],
            scratch_shapes=[pltpu.VMEM(early.shape, BF), pltpu.VMEM(late.shape, BF)],
        ),
        out_shape=[first, second, jax.ShapeDtypeStruct((1,), F32)],
        compiler_params=pltpu.CompilerParams(
            dimension_semantics=("arbitrary",), vmem_limit_bytes=VMEM_UPDATE
        ),
        name="renew",
        cost_estimate=CHEAP,
    )(side, index, *square, early, late, gn, *norm, *attn, *up, *down)


def update_kernel(
    side_ref, index_ref, square_ref, other_ref, early_ref, late_ref, got_ref, gn_ref, *refs
):
    am, af, as_, um, uf, us, dm, df, ds, nm, nf, ns = refs[:12]
    early, late = refs[-2:]
    outs, copy_low, copy_high, other_half = refs[12:-5], refs[-5], refs[-4], refs[-3]
    step = pl.program_id(0)
    factor = clip_factor(square_ref, other_ref)
    width = early.shape[1]
    part = late.shape[0] // 4
    blocks = um.shape[1] // width
    height = part // pl.num_programs(0)
    half = LANES // 2

    def keep(group, where, unit, size, new):
        for target, value in zip(outs[3 * group : 3 * group + 3], new):
            target[where] = value
        target, unit = (copy_low, unit) if unit < 8 else (copy_high, unit - 8)
        rows = pl.ds(pl.multiple_of(unit * part + step * size, size), size)
        target[rows, :] = new[0].astype(BF)

    @pl.when(step == 0)
    def _():
        mine = half * side_ref[0]
        count = late_ref.shape[0]
        gather_rows(index_ref, early_ref, early, part, mine)
        gather_rows(index_ref, late_ref, late, part, mine)
        gather_rows(index_ref, got_ref.at[:count, :], late, part, half - mine)
        gather_rows(index_ref, got_ref.at[count:, :], early, part, half - mine)
        new = adam(nm[...], nf[...], ns[...], gn_ref[...] * factor, 0.3, 0.0)
        outs[9][...], outs[10][...], outs[11][...] = new

    def span(base, size):
        return pl.ds(pl.multiple_of(base + step * size, size), size)

    for m in range(5):
        source = late[span(m * part, height), :] if m < 4 else early[span(0, height), :]
        new = adam(am[m], af[m], as_[m], source.astype(F32) * factor, 0.05, 0.01)
        keep(0, (m, slice(None), slice(None)), m, height, new)
    for j in range(blocks):
        source = early[span((j + 1) * part, height), :]
        cols = (slice(None), slice(j * width, (j + 1) * width))
        new = adam(um[cols], uf[cols], us[cols], source.astype(F32) * factor, 0.05, 0.01)
        keep(1, cols, 5 + j, height, new)
    tall = dm.shape[0]
    source = early[span((blocks + 1) * part, tall), :]
    new = adam(dm[...], df[...], ds[...], source.astype(F32) * factor, 0.05, 0.01)
    keep(2, (slice(None), slice(None)), 5 + blocks, tall, new)

    @pl.when(step == pl.num_programs(0) - 1)
    def _():
        count = other_half.shape[0] // half
        base = copy_high.shape[0] - count * part
        for j in range(count):
            rows = pl.ds(pl.multiple_of(base + j * part + half - half * side_ref[0], half), half)
            other_half[j * half : (j + 1) * half, :] = copy_high[rows, :]


def update(side, index, square, early, late, got, gn, attn, up, down, norm):
    steps = 4
    smem = pl.BlockSpec(memory_space=pltpu.SMEM)
    five, part, width = attn[0].shape
    specs = (
        [pl.BlockSpec((five, part // steps, width), lambda i: (0, i, 0))] * 3
        + [pl.BlockSpec((part // steps, up[0].shape[1]), lambda i: (i, 0))] * 3
        + [pl.BlockSpec((down[0].shape[0] // steps, width), lambda i: (i, 0))] * 3
        + [whole(norm[0])] * 3
    )
    arrays = tuple(attn) + tuple(up) + tuple(down) + tuple(norm)
    low = jax.ShapeDtypeStruct((8 * part, width), BF)
    tall, short = 2 * early.shape[0], 2 * late.shape[0]
    high = jax.ShapeDtypeStruct((tall + short - 8 * part, width), BF)
    other = jax.ShapeDtypeStruct((DIRECT_UNITS * part // 2, width), BF)
    return pl.pallas_call(
        update_kernel,
        grid=(steps,),
        in_specs=[smem] * 2 + [whole(a) for a in (*square, early, late, got, gn)] + specs,
        out_specs=specs + [whole(low), whole(high), whole(other)],
        out_shape=[jax.ShapeDtypeStruct(a.shape, F32) for a in arrays] + [low, high, other],
        scratch_shapes=[pltpu.VMEM((tall, width), BF), pltpu.VMEM((short, width), BF)],
        compiler_params=pltpu.CompilerParams(
            dimension_semantics=("arbitrary",), vmem_limit_bytes=VMEM_UPDATE
        ),
        name="update",
        cost_estimate=CHEAP,
    )(side, index, *square, early, late, got, gn, *arrays)


def place_unit(pos, source, unit, first, count, attn_ref, up_ref, down_ref, sem):
    width = attn_ref.shape[2]
    blocks = up_ref.shape[1] // width
    tall = down_ref.shape[0] // 4
    rows = pl.ds(pl.multiple_of(pos * LANES + first, count), count)
    if unit < 5:
        target = attn_ref.at[unit, rows, :]
    elif unit < 5 + blocks:
        target = up_ref.at[rows, pl.ds((unit - 5) * width, width)]
    else:
        base = pl.multiple_of(pos * tall + (unit - 5 - blocks) * LANES + first, count)
        target = down_ref.at[pl.ds(base, count), :]
    return pltpu.make_async_copy(source, target, sem)


def run_copies(copies):
    for copy in copies:
        copy.start()
    for copy in copies:
        copy.wait()


def place_whole(pos, piece, unit, outs, sems, copies):
    for j in range(piece.shape[0] // LANES):
        source = piece.at[pl.ds(j * LANES, LANES), :]
        copies.append(place_unit(pos, source, unit + j, 0, LANES, *outs, sems.at[len(copies)]))


def place_half(pos, side, piece, unit, outs, sems, copies):
    half = LANES // 2
    for j in range(piece.shape[0] // half):
        source = piece.at[pl.ds(j * half, half), :]
        copies.append(
            place_unit(pos, source, unit + j, half * side, half, *outs, sems.at[len(copies)])
        )


def unpack_near_kernel(pos_ref, side_ref, p0, p1, p2, p3, p4, p5, attn_ref, up_ref, down_ref, sems):
    copies = []
    outs = attn_ref, up_ref, down_ref
    for index, parts in enumerate(((p0, p1), (p2, p3))):
        place_whole(pos_ref[index], parts[0], 0, outs, sems, copies)
        place_whole(pos_ref[index], parts[1], 8, outs, sems, copies)
    for index, piece in enumerate((p4, p5)):
        place_half(pos_ref[2 + index], side_ref[0], piece, 0, outs, sems, copies)
    run_copies(copies)


def unpack_far_kernel(pos_ref, side_ref, *refs):
    pieces, outs, sems = refs[:8], refs[11:14], refs[14]
    copies = []
    other = side_ref[0] ^ 1
    for index in range(2):
        second, first_other, second_other, direct = pieces[4 * index : 4 * index + 4]
        pos = pos_ref[2 + index]
        place_half(pos, side_ref[0], second, FIRST_UNITS, outs, sems, copies)
        place_half(pos, other, first_other, 0, outs, sems, copies)
        place_half(pos, other, second_other, FIRST_UNITS, outs, sems, copies)
        unit = FIRST_UNITS + second_other.shape[0] // (LANES // 2)
        place_half(pos, other, direct, unit, outs, sems, copies)
    run_copies(copies)


def share_copies(pos, side, first, second, low, high, direct, width, hidden):
    units = (low.shape[0] + high.shape[0]) // LANES
    half = LANES // 2
    last_rows = swap(first[FIRST_UNITS * half :], "shard", 1)
    ours, first_too, low, high, direct = lax.optimization_barrier(
        (swap(first, "shard", 2), last_rows, low, high, direct)
    )
    other = swap(ours, "dp", 1)
    second_got = swap(after(second, ours), "shard", 2)
    near = [swap(part, "shard", 1) for part in (low, high)]
    ours_too = swap(ours, "shard", 1)
    a, b, c, d = [
        p[p.shape[0] - SMALL : p.shape[0] - SMALL + 4, :LANES]
        for p in (first, first_too, ours, ours_too)
    ]
    low_bit, high_bit = pos[0] % 2 == 1, pos[0] // 2 == 1
    a, b, c, d = [jnp.where(low_bit, v, u) for u, v in ((a, b), (b, a), (c, d), (d, c))]
    a, b, c, d = [jnp.where(high_bit, v, u) for u, v in ((a, c), (b, d), (c, a), (d, b))]
    norms = jnp.concatenate([a, b, c, d], axis=1)
    hbm = pl.BlockSpec(memory_space=pl.ANY)
    vmem = pl.BlockSpec(memory_space=pltpu.VMEM)
    smem = pl.BlockSpec(memory_space=pltpu.SMEM)
    shapes = [
        jax.ShapeDtypeStruct((5, width, width), BF),
        jax.ShapeDtypeStruct((width, hidden), BF),
        jax.ShapeDtypeStruct((hidden, width), BF),
    ]
    params = pltpu.CompilerParams(vmem_limit_bytes=VMEM_UNPACK)
    begun = pl.pallas_call(
        unpack_near_kernel,
        in_specs=[smem, smem] + [vmem] * 6,
        out_specs=[hbm] * 3,
        out_shape=shapes,
        scratch_shapes=[pltpu.SemaphoreType.DMA((2 * (units + FIRST_UNITS),))],
        compiler_params=params,
        name="unpack_near",
        cost_estimate=CHEAP,
    )(pos, side, after(low, norms), high, *near, ours, ours_too)
    second = after(second_got, begun[0])
    second_other = swap(second[: -direct.shape[0]], "dp", 1)
    direct = swap(after(direct, second), "shard", 2)
    far = [second, other, second_other, direct]
    far += [swap(after(f, begun[0]), "shard", 1) for f in far]
    done = pl.pallas_call(
        unpack_far_kernel,
        in_specs=[smem, smem] + [vmem] * 8 + [hbm] * 3,
        out_specs=[hbm] * 3,
        out_shape=shapes,
        scratch_shapes=[pltpu.SemaphoreType.DMA((4 * units,))],
        input_output_aliases={10: 0, 11: 1, 12: 2},
        compiler_params=params,
        name="unpack_far",
        cost_estimate=CHEAP,
    )(pos, side, *far, *begun)
    return tuple(done) + (norms,)


def shards(
    tokens, out_grad, domain_ids, domain_weight,
    attn_master, attn_first, attn_second,
    up_master, up_first, up_second,
    down_master, down_first, down_second,
    norm_master, norm_first, norm_second,
):
    length, width = tokens.shape
    hidden = up_master.shape[1]
    part = width // 4
    blocks = hidden // width
    dp = lax.axis_index("dp")
    shard = lax.axis_index("shard").astype(jnp.int32)
    pos = shard ^ jnp.arange(4, dtype=jnp.int32)
    half = (dp % 2).astype(jnp.int32)[None]
    place = places()

    small = jnp.pad(norm_master.astype(BF), ((0, SMALL - 4), (0, width - part)))
    rows = attn_master[:4].astype(BF).reshape(4 * part, width)
    own = jnp.concatenate([rows[: 2 * part], small, rows[2 * part :], jnp.zeros_like(small)])
    middle = own.shape[0] // 2
    near = swap(own, "shard", 1)
    ours = lax.dynamic_slice(own, (half[0] * middle, 0), (middle, width))
    far_a = swap(ours, "shard", 2)

    domains = domain_weight.shape[0]
    devices = lax.axis_size("dp") * lax.axis_size("shard") * domain_ids.shape[0]
    onehot = (domain_ids[:, None] == jnp.arange(domains, dtype=jnp.int32)[None, :]).astype(F32)
    counts = jnp.sum(onehot, axis=0)
    dp_bits = bits_of(lax.axis_size("dp"))
    for b in dp_bits[:2]:
        counts = counts + swap(counts, "dp", b)
    far_b = swap(after(far_a, counts), "dp", 1)
    second = jnp.concatenate(
        [attn_master[4].astype(BF)]
        + [up_master[:, j * width : (j + 1) * width].astype(BF) for j in range(blocks)]
    )
    second_far = swap(after(second, counts), "shard", 2)
    for b in dp_bits[2:]:
        counts = counts + after(swap(counts, "dp", b), far_b)
    counts_row = jnp.pad(counts.astype(BF)[None], ((0, SMALL - 1), (0, width - domains)))
    third = jnp.concatenate([down_master.astype(BF), counts_row])
    third_far = swap(third, "shard", 2)
    second = [second, swap(second, "shard", 1), second_far]
    third = [third, swap(third, "shard", 1), third_far]
    domain_rows = jnp.pad(
        jnp.stack([onehot[0], domain_weight * devices / domains]),
        ((0, 6), (0, LANES - domains)),
    )
    far_c = swap(far_a, "shard", 1)
    far = [far_a, far_b, far_c, swap(far_b, "shard", 1)]
    q, k, v, n, e, eb, z, o, weights, scores, keys, values, w, norm = attend(
        pos, half, tokens, [own, near] + far
    )
    for pieces in (second, third):
        pieces.append(swap(after(pieces[2], o), "shard", 1))
    y, dh, do, send, keep, dnorm = feed(
        pos, place, domain_rows, tokens, out_grad, o, norm, second, third
    )

    steps, plan, index = HALVINGS + [MIDDLE], GATHERS, quarters()
    pieces = 16
    rows = keep.shape[0] // pieces

    def forward_phase(parts, phase, rows):
        low = rows * pieces >> (phase + 1)
        return add_up(parts, low, 2 * low)

    saved = (q, k, v, eb, e, z, weights, scores, keys, values)
    chunks = length // CHUNK
    early = [keep, swap(send, "shard", 1)]
    later = mix_back(chunks - 1, 1, (), do, *saved)
    out = after(forward_phase(early, 0, rows), later[0])
    early.append(exchange(out, *steps[0]))
    sooner = mix_back(chunks - 2, chunks - 1, later[4:], after(do, out), *saved)
    back = list(sooner[:4]) + list(later[:4])
    out = after(forward_phase(early, 1, rows), back[0])
    early.append(exchange(out, *steps[1]))
    dx, small = input_back(tokens, after(dh, out), w, norm, dnorm, back)
    send, keep = weight_back(pos, place, small, n, back)
    turn = forward_phase(early, 2, rows)
    got = exchange(turn, *steps[2])
    late = [keep, swap(after(send, turn), "shard", 1)]
    height = keep.shape[0] - SMALL
    thin = height // pieces
    small = add_up(late, height, height + SMALL)

    def late_phase(phase):
        out = jnp.concatenate([forward_phase(late, phase, thin), small])
        return out, exchange(out, *steps[phase])

    def late_sum(got):
        late.append(got)
        return add_up([small, got[got.shape[0] - SMALL :]], 0, SMALL)

    turn, late_got = late_phase(0)
    small = late_sum(late_got)
    turn, late_got = late_phase(1)
    early.append(after(got, turn))
    turn = add_up(early, 0, 2 * rows)
    got = exchange(turn, *steps[3])
    small = late_sum(after(late_got, turn))
    early = turn
    turn, late_got = late_phase(2)
    early = add_rest(add_up([early, after(got, turn)], 0, 2 * rows))
    got = exchange(early, *plan[0])
    small = late_sum(after(late_got, early))
    out = jnp.concatenate([add_up(late, 0, 2 * thin), small])
    late_got = exchange(out, *steps[3])
    late = add_rest(add_up([out, late_got], 0, 2 * thin + SMALL))
    late, small = late[: 2 * thin], late[2 * thin :]
    late_got = exchange(late, *plan[0])
    norm_grad = lax.dynamic_slice(small[:4], (0, shard * part), (4, part)).astype(F32)
    early = jnp.concatenate([early, after(got, late)])
    late = jnp.concatenate([late, after(late_got, early)])
    square = squares(early, late, norm_grad)
    square = square + swap(square, "dp", 1)
    got = exchange(after(jnp.concatenate([late, early]), square), *plan[1])
    square = square + swap(square, "shard", 1)
    square = (square, swap(square, "shard", 2))
    attn = (attn_master, attn_first, attn_second)
    up = (up_master, up_first, up_second)
    down = (down_master, down_first, down_second)
    norms = (norm_master, norm_first, norm_second)
    first, second, clip_norm = renew(
        half, index, square, early, late, norm_grad, attn, up, down, norms
    )
    *new, low, high, direct = update(
        half, index, square, early, late, after(got, first), norm_grad, attn, up, down, norms
    )
    copies = share_copies(pos, half, first, second, low, high, direct, width, hidden)
    return (y, dx) + tuple(new) + (clip_norm.reshape(()),) + tuple(copies)


def solution(mesh):
    rows = P(("dp", "shard"), None)
    attn = (P(None, "shard", None),) * 3
    tall = (P("shard", None),) * 6
    norm = (P(None, "shard"),) * 3
    return jax.shard_map(
        shards,
        mesh=mesh,
        in_specs=(rows, rows, P(("dp", "shard")), P()) + attn + tall + norm,
        out_specs=(rows, rows) + attn + tall + norm + (P(),) * 5,
        check_vma=False,
    )
```

```python
import functools
import jax
import jax.numpy as jnp
from jax import lax
from jax.experimental import pallas as pl
from jax.experimental.pallas import tpu as pltpu
from jax.sharding import PartitionSpec as P

BF = jnp.bfloat16
F32 = jnp.float32
MIB = 1024 * 1024
VMEM_ATTEND = 40 * MIB
VMEM_MIX = 44 * MIB
VMEM_FEED = 44 * MIB
VMEM_BACK = 24 * MIB
VMEM_UPDATE = 56 * MIB
VMEM_UNPACK = 24 * MIB
CHUNK = 256
SLOT = 64
GROUP = 256
LANES = 128
SMALL = 16
FIRST_UNITS = 7
DIRECT_UNITS = 2
CHEAP = pl.CostEstimate(flops=1, bytes_accessed=1, transcendentals=0)
STEP = 10
TILE = 512
COUNTS = (1, 2, 1)


def whole(a):
    return pl.BlockSpec(a.shape, lambda *_: (0,) * len(a.shape), pipeline_mode=pl.Buffered(1))


def dot(a, b):
    return jnp.dot(a, b, preferred_element_type=F32)


def dot_nt(a, b):
    return lax.dot_general(a, b, (((1,), (1,)), ((), ())), preferred_element_type=F32)


def dot_tn(a, b):
    return lax.dot_general(a, b, (((0,), (0,)), ((), ())), preferred_element_type=F32)


def head_of(shape, dim):
    return lax.broadcasted_iota(jnp.int32, shape, dim) // SLOT


def block_diagonal(state):
    return jnp.where(head_of(state.shape, 0) == head_of(state.shape, 1), state, 0.0).astype(BF)


def only_head(rows, head):
    return jnp.where(head_of(rows.shape, 1) == head, rows, jnp.zeros_like(rows))


def by_head(rows):
    return jnp.concatenate([only_head(rows, h) for h in range(GROUP // SLOT)], axis=0)


def lower(square):
    size = square.shape[0]
    row = lax.broadcasted_iota(jnp.int16, (size, size), 0)
    col = lax.broadcasted_iota(jnp.int16, (size, size), 1)
    return jnp.concatenate(
        [
            jnp.where(row >= col, square[:, first : first + size].astype(BF), jnp.zeros((), BF))
            for first in range(0, square.shape[1], size)
        ],
        axis=1,
    )


def upper(square):
    size = square.shape[1]
    row = lax.broadcasted_iota(jnp.int16, (size, size), 0)
    col = lax.broadcasted_iota(jnp.int16, (size, size), 1)
    return jnp.concatenate(
        [
            jnp.where(row <= col, square[first : first + size, :].astype(BF), jnp.zeros((), BF))
            for first in range(0, square.shape[0], size)
        ],
        axis=1,
    )


def split_dot(ones, values):
    high = values.astype(BF)
    low = (values - high.astype(F32)).astype(BF)
    return dot(ones, high) + dot(ones, low)


def head_ones():
    return jnp.where(
        head_of((GROUP, GROUP), 0) == head_of((GROUP, GROUP), 1), 1.0, 0.0
    ).astype(BF)


def head_sums(values):
    ones = head_ones()
    high = values.astype(BF)
    low = (values - high.astype(F32)).astype(BF)
    return dot(high, ones) + dot(low, ones)


def head_max(values):
    top = None
    head = head_of(values.shape, 1)
    for index in range(GROUP // SLOT):
        mine = jnp.max(jnp.where(head == index, values, -jnp.inf), axis=1, keepdims=True)
        top = mine if top is None else jnp.where(head == index, mine, top)
    return top


def normalise(values):
    centred = values - jnp.mean(values, axis=-1, keepdims=True)
    inv = lax.rsqrt(jnp.mean(centred * centred, axis=-1, keepdims=True) + 1e-05)
    return centred * inv, inv


def normalise_back(grad, unit, inv, gain):
    scaled = grad * gain
    return inv * (
        scaled
        - jnp.mean(scaled, axis=-1, keepdims=True)
        - unit * jnp.mean(scaled * unit, axis=-1, keepdims=True)
    )


def attend_kernel(
    pos_ref, half_ref, x_ref, near0, near1, far0, far1, far2, far3,
    q_ref, k_ref, v_ref, n_ref, e_ref, eb_ref, z_ref, o_ref, w_ref, s_ref, keys_ref, values_ref,
    weights_ref, norm_ref, keys, values, carry
):
    width = x_ref.shape[1]
    part = width // 4

    @pl.when(pl.program_id(0) == 0)
    def _():
        low = far0.shape[0]

        def rows_of(index, first, count):
            if index < 2:
                return (near0, near1)[index][first : first + count, :]
            a, b = ((far0, far1), (far2, far3))[index - 2]
            if first >= low:
                a, b, first = b, a, first - low
            return jnp.where(half_ref[0] == 0, a[first : first + count, :], b[first : first + count, :])

        for index in range(4):
            rows = pl.ds(pl.multiple_of(pos_ref[index] * part, part), part)
            for m in range(4):
                weights_ref[m, rows, :] = rows_of(index, m * part + SMALL * (m > 1), part)
            norm_ref[:, rows] = rows_of(index, 2 * part, SMALL)[0:8, 0:part].astype(F32)
        carry[...] = jnp.zeros_like(carry)
        keys[...] = jnp.zeros_like(keys)
        values[...] = jnp.zeros_like(values)

    heads = range(GROUP // SLOT)
    groups = range(keys.shape[0])
    cols = [slice(i * GROUP, (i + 1) * GROUP) for i in groups]
    unit, _ = normalise(x_ref[...].astype(F32))
    normed = (unit * norm_ref[0:1, :] + norm_ref[1:2, :]).astype(BF)
    n_ref[...] = normed
    rows = normed.shape[0]
    ones = lower(jnp.ones((rows, rows), F32))
    q, k, v, e, inv = [], [], [], [], []
    for c in cols:
        raised = jnp.exp(dot(normed, weights_ref[3, :, c]))
        z = split_dot(ones, raised) + carry[0:1, c]
        carry[0:1, c] = z[rows - 1 : rows, :]
        e_ref[:, c] = raised
        z_ref[:, c] = z
        e.append(raised.astype(BF))
        inv.append(1.0 / z)
        for m, part_of in enumerate((q, k, v)):
            part_of.append(dot(normed, weights_ref[m, :, c]).astype(BF))
    for i in groups:
        q_ref[:, cols[i]], k_ref[:, cols[i]], v_ref[:, cols[i]] = q[i], k[i], v[i]
        eb_ref[:, cols[i]] = e[i]
    total, value_state = [], []
    for i in groups:
        state = block_diagonal(keys[i])
        keys_ref[i, 0] = state
        total.append(dot(q[i], state))
        state = block_diagonal(values[i])
        values_ref[i, 0] = state
        value_state.append(state)
    es = [by_head(e[i]) for i in groups]
    for i in groups:
        total[i] += dot(lower(dot_nt(q[i], by_head(k[i]))), es[i])
    scores = [total[i] * inv[i] * 0.125 for i in groups]
    raised = [jnp.exp(scores[i] - head_max(scores[i])) for i in groups]
    weights = [raised[i] / head_sums(raised[i]) for i in groups]
    ratio = [(weights[i] * inv[i]).astype(BF) for i in groups]
    out = [dot(ratio[i], value_state[i]) for i in groups]
    for i in groups:
        out[i] += dot(lower(dot_nt(ratio[i], es[i])), by_head(v[i]))
    for i in groups:
        s_ref[:, cols[i]] = scores[i]
        w_ref[:, cols[i]] = weights[i]
        o_ref[:, cols[i]] = out[i].astype(BF)
        keys[i] += dot_tn(k[i], e[i])
        values[i] += dot_tn(e[i], v[i])


def attend(pos, half, x, pieces):
    length, width = x.shape
    steps, groups = length // CHUNK, width // GROUP
    rows = lambda dtype: jax.ShapeDtypeStruct((length, width), dtype)
    block = pl.BlockSpec((CHUNK, width), lambda i: (i, 0))
    state = pl.BlockSpec((groups, 1, GROUP, GROUP), lambda i: (0, i, 0, 0))
    states = jax.ShapeDtypeStruct((groups, steps, GROUP, GROUP), BF)
    full = [jax.ShapeDtypeStruct((4, width, width), BF), jax.ShapeDtypeStruct((8, width), F32)]
    return pl.pallas_call(
        attend_kernel,
        grid=(steps,),
        in_specs=[pl.BlockSpec(memory_space=pltpu.SMEM)] * 2 + [block] + [whole(p) for p in pieces],
        out_specs=[block] * 10 + [state] * 2 + [whole(a) for a in full],
        out_shape=[rows(BF)] * 4
        + [rows(F32), rows(BF), rows(F32), rows(BF), rows(F32), rows(F32), states, states]
        + full,
        scratch_shapes=[pltpu.VMEM((groups, GROUP, GROUP), F32)] * 2 + [pltpu.VMEM((8, width), F32)],
        compiler_params=pltpu.CompilerParams(
            dimension_semantics=("arbitrary",), vmem_limit_bytes=VMEM_ATTEND
        ),
        name="attend",
        cost_estimate=CHEAP,
    )(pos, half, x, *pieces)


def mix_back_kernel(*refs, begun):
    g_ref, q_ref, k_ref, v_ref, eb_ref, e_ref, z_ref, w_ref, s_ref, keys_ref, values_ref = refs[:11]
    before, (dq_ref, dk_ref, dv_ref, dc_ref, later_v, later_k, carry) = refs[11:-7], refs[-7:]

    @pl.when(pl.program_id(0) == 0)
    def _():
        if begun:
            later_v[...], later_k[...], carry[...] = [ref[...] for ref in before]
        else:
            later_v[...] = jnp.zeros_like(later_v)
            later_k[...] = jnp.zeros_like(later_k)
            carry[...] = jnp.zeros_like(carry)

    heads = range(GROUP // SLOT)
    groups = range(later_v.shape[0])
    cols = [slice(i * GROUP, (i + 1) * GROUP) for i in groups]
    g, q, k, v, e = [[ref[:, c] for c in cols] for ref in (g_ref, q_ref, k_ref, v_ref, eb_ref)]
    inv = [1.0 / z_ref[:, c] for c in cols]
    weights = [w_ref[:, c] for c in cols]
    ratio = [(weights[i] * inv[i]).astype(BF) for i in groups]
    es = [by_head(e[i]) for i in groups]
    state = [block_diagonal(later_v[i]) for i in groups]
    d_ratio = [dot_nt(g[i], values_ref[i, 0]) for i in groups]
    dv = [dot(e[i], state[i]) for i in groups]
    de = [dot_nt(v[i], state[i]) for i in groups]
    for i in groups:
        vs = by_head(v[i])
        d_ratio[i] += dot(lower(dot_nt(g[i], vs)), es[i])
        de[i] += dot(upper(dot_nt(vs, g[i])), by_head(ratio[i]))
        dv[i] += dot(upper(dot_nt(es[i], ratio[i])), by_head(g[i]))
    d_weights = [d_ratio[i] * inv[i] for i in groups]
    both = [d_weights[i] * weights[i] for i in groups]
    d_scores = [weights[i] * (d_weights[i] - head_sums(both[i])) for i in groups]
    dn = [(d_scores[i] * inv[i] * 0.125).astype(BF) for i in groups]
    dz = [-(both[i] + d_scores[i] * s_ref[:, cols[i]]) * inv[i] for i in groups]
    state = [block_diagonal(later_k[i]) for i in groups]
    dq = [dot_nt(dn[i], keys_ref[i, 0]) for i in groups]
    dk = [dot(e[i], state[i]) for i in groups]
    de = [de[i] + dot_nt(k[i], state[i]) for i in groups]
    for i in groups:
        ks = by_head(k[i])
        dq[i] += dot(lower(dot_nt(dn[i], es[i])), ks)
        dk[i] += dot(upper(dot_nt(es[i], dn[i])), by_head(q[i]))
        de[i] += dot(upper(dot_nt(ks, q[i])), by_head(dn[i]))
    rows = dz[0].shape[0]
    ones = upper(jnp.ones((rows, rows), F32))
    for i in groups:
        dv_ref[:, cols[i]] = dv[i].astype(BF)
        dq_ref[:, cols[i]] = dq[i].astype(BF)
        dk_ref[:, cols[i]] = dk[i].astype(BF)
        z_sum = split_dot(ones, dz[i]) + carry[0:1, cols[i]]
        carry[0:1, cols[i]] = z_sum[0:1, :]
        dc_ref[:, cols[i]] = ((de[i] + z_sum) * e_ref[:, cols[i]]).astype(BF)
        later_v[i] += dot_tn(ratio[i], g[i])
        later_k[i] += dot_tn(dn[i], q[i])


def mix_back(last, count, before, g, q, k, v, eb, e, z, w, s, keys, values):
    length, width = q.shape
    groups = width // GROUP
    block = pl.BlockSpec((CHUNK, width), lambda i: (last - i, 0))
    state = pl.BlockSpec((groups, 1, GROUP, GROUP), lambda i: (0, last - i, 0, 0))
    out = pl.BlockSpec((CHUNK, width), lambda i: (count - 1 - i, 0))
    rows = jax.ShapeDtypeStruct((count * CHUNK, width), BF)
    sums = [jax.ShapeDtypeStruct((groups, GROUP, GROUP), F32)] * 2
    sums += [jax.ShapeDtypeStruct((8, width), F32)]
    return pl.pallas_call(
        functools.partial(mix_back_kernel, begun=bool(before)),
        grid=(count,),
        in_specs=[block] * 9 + [state] * 2 + [whole(a) for a in before],
        out_specs=[out] * 4 + [whole(a) for a in sums],
        out_shape=[rows] * 4 + sums,
        compiler_params=pltpu.CompilerParams(
            dimension_semantics=("arbitrary",), vmem_limit_bytes=VMEM_MIX
        ),
        name="mix_back",
        cost_estimate=CHEAP,
    )(g, q, k, v, eb, e, z, w, s, keys, values, *before)


def scatter_unit(place_ref, grads, first, unit, shard, target, table):
    count = place_ref.shape[1] // 2
    part = LANES
    rows = part // count
    height = target.shape[0] // LANES * LANES // (2 * count)
    for d in range(count):
        place = place_ref[table, (shard // 2) * count + d]
        where = pl.ds(pl.multiple_of(place * height + unit * rows, rows), rows)
        group = d % 2 * (count // 2) + d // 2
        target[where, :] = grads[pl.ds(pl.multiple_of(first + group * rows, rows), rows), :]


def scatter_shards(pos_ref, place_ref, grads, send_ref, keep_ref, unit):
    for index in range(4):
        pos = pos_ref[index]
        target = send_ref if index % 2 else keep_ref
        scatter_unit(place_ref, grads, pos * LANES, unit, pos, target, index % 2)


def feed_kernel(
    pos_ref, place_ref, domain_ref, x_ref, g_ref, o_ref, norm_ref, p0, p1, p2, p3, t0, t1, t2, t3,
    y_ref, dh_ref, do_ref, send_ref, keep_ref, dnorm_ref,
    wo, w1, w2, branch, unit_ref, inv_ref, n2, gb, n2_t, dn2, grads, u_all, da_all, factor_ref
):
    step = pl.program_id(0)
    last = pl.num_programs(0) - 1
    length, width = x_ref.shape
    part = width // 4
    block = w1.shape[2]
    tiles = length // 256

    @pl.when(step == 0)
    def _():
        for index, (piece, tall) in enumerate(((p0, t0), (p1, t1), (p2, t2), (p3, t3))):
            pos = pos_ref[index]
            rows = pl.ds(pl.multiple_of(pos * part, part), part)
            wo[rows, :] = piece[0:part, :]
            for j in range(4):
                w1[j, rows, :] = piece[(j + 1) * part : (j + 2) * part, :]
            w2[pos] = tall[0:block, :]
        count = sum(t[block : block + SMALL, 0:LANES].astype(F32) for t in (t0, t1, t2, t3))
        share = domain_ref[0:1, :] * domain_ref[1:2, :] / jnp.maximum(count[0:1, :], 1.0)
        factor_ref[...] = jnp.broadcast_to(jnp.sum(share, axis=1, keepdims=True), factor_ref.shape)

        def before(i, _):
            rows = slice(i * 256, (i + 1) * 256)
            h1 = x_ref[rows, :].astype(F32) + dot(o_ref[rows, :], wo[...])
            branch[rows, :] = h1
            unit, inv = normalise(h1)
            unit_ref[rows, :] = unit
            inv_ref[rows, :] = jnp.broadcast_to(inv, (256, 128))
            normed = (unit * norm_ref[2:3, :] + norm_ref[3:4, :]).astype(BF)
            n2[rows, :] = normed
            n2_t[:, rows] = normed.T
            grad = (g_ref[rows, :].astype(F32) * factor_ref[0:1, 0:1]).astype(BF)
            gb[rows, :] = grad
            dn2[rows, :] = jnp.zeros((256, width), F32)
            return 0

        for i in range(tiles):
            before(i, 0)

    up = w1[step]
    down = w2[step]
    tile = TILE
    for i in range(length // tile):
        rows = slice(i * tile, (i + 1) * tile)
        a = dot(n2[rows, :], up)
        square = a * a
        half = 0.5 + 0.5 * jnp.tanh(a * (0.7978845608 + (0.044715 * 0.7978845608) * square))
        u = a * half
        slope = half + u * (1.0 - half) * (
            2.0 * 0.7978845608 + (6.0 * 0.044715 * 0.7978845608) * square
        )
        u = u.astype(BF)
        da = (dot_nt(gb[rows, :], down) * slope).astype(BF)
        u_all[rows, :] = u
        da_all[rows, :] = da
        branch[rows, :] += dot(u, down)
        dn2[rows, :] += dot_nt(da, up)
    up_grad = dot(n2_t[...], da_all[...])
    down_grad = dot_tn(u_all[...], gb[...])
    grads[...] = up_grad.astype(BF)
    scatter_shards(pos_ref, place_ref, grads, send_ref, keep_ref, step + 1)
    grads[...] = down_grad.astype(BF)
    mine = (step ^ pos_ref[0]) & 1 == 0

    @pl.when(mine)
    def _():
        for u in range(4):
            scatter_unit(place_ref, grads, u * part, 5 + u, step, keep_ref, 0)

    @pl.when(jnp.logical_not(mine))
    def _():
        for u in range(4):
            scatter_unit(place_ref, grads, u * part, 5 + u, step, send_ref, 1)

    @pl.when(step == last)
    def _():
        gain = norm_ref[2:3, :]

        def after(i, sums):
            rows = slice(i * 256, (i + 1) * 256)
            y_ref[rows, :] = branch[rows, :].astype(BF)
            grad = dn2[rows, :]
            unit = unit_ref[rows, :]
            dh = g_ref[rows, :].astype(F32) * factor_ref[0:1, 0:1] + normalise_back(
                grad, unit, inv_ref[rows, 0:1], gain
            )
            dh_ref[rows, :] = dh
            dh_low = dh.astype(BF)
            do_ref[rows, :] = dot_nt(dh_low, wo[...]).astype(BF)
            return (
                sums[0] + jnp.sum(grad * unit, axis=0, keepdims=True),
                sums[1] + jnp.sum(grad, axis=0, keepdims=True),
                sums[2] + dot_tn(o_ref[rows, :], dh_low),
            )

        empty = jnp.zeros((1, width), F32)
        sums = (empty, empty, jnp.zeros((width, width), F32))
        for i in range(tiles):
            sums = after(i, sums)
        dnorm_ref[...] = jnp.zeros_like(dnorm_ref)
        dnorm_ref[0:1, :] = sums[0]
        dnorm_ref[1:2, :] = sums[1]
        grads[...] = sums[2].astype(BF)
        scatter_shards(pos_ref, place_ref, grads, send_ref, keep_ref, 0)


def feed(pos, place, domain_rows, x, g, o, norm, pieces, talls):
    length, width = x.shape
    block = width
    height = 5 * (width // 4) + block
    rows = lambda dtype: jax.ShapeDtypeStruct((length, width), dtype)
    out = [
        rows(BF), rows(F32), rows(BF),
        jax.ShapeDtypeStruct((2 * height, width), BF),
        jax.ShapeDtypeStruct((2 * height, width), BF),
        jax.ShapeDtypeStruct((8, width), F32),
    ]
    args = (domain_rows, x, g, o, norm) + tuple(pieces) + tuple(talls)
    return pl.pallas_call(
        feed_kernel,
        grid=(4,),
        in_specs=[pl.BlockSpec(memory_space=pltpu.SMEM)] * 2 + [whole(a) for a in args],
        out_specs=[whole(a) for a in out],
        out_shape=out,
        scratch_shapes=[
            pltpu.VMEM((width, width), BF),
            pltpu.VMEM((4, width, block), BF),
            pltpu.VMEM((4, block, width), BF),
            pltpu.VMEM((length, width), F32),
            pltpu.VMEM((length, width), F32),
            pltpu.VMEM((length, 128), F32),
            pltpu.VMEM((length, width), BF),
            pltpu.VMEM((length, width), BF),
            pltpu.VMEM((width, length), BF),
            pltpu.VMEM((length, width), F32),
            pltpu.VMEM((width, block), BF),
            pltpu.VMEM((length, block), BF),
            pltpu.VMEM((length, block), BF),
            pltpu.VMEM((8, LANES), F32),
        ],
        compiler_params=pltpu.CompilerParams(
            dimension_semantics=("arbitrary",), vmem_limit_bytes=VMEM_FEED
        ),
        name="feed",
        cost_estimate=CHEAP,
    )(pos, place, *args)


def weight_back_kernel(pos_ref, place_ref, small_ref, n_ref, *refs):
    grads_in, (send_ref, keep_ref, n_t, grads) = refs[:-4], refs[-4:]
    n_t[...] = n_ref[...].T
    for target in (send_ref, keep_ref):
        target[target.shape[0] - SMALL :, :] = small_ref[...]
    for m in range(4):
        total = None
        first = 0
        for j in range(len(grads_in) // 4):
            part = grads_in[4 * j + m]
            last = first + part.shape[0]
            term = dot(n_t[:, first:last], part[...])
            total = term if total is None else total + term
            first = last
        grads[m] = total.astype(BF)
    for m in range(4):
        scatter_shards(pos_ref, place_ref, grads.at[m], send_ref, keep_ref, m)


def weight_back(pos, place, small, n, halves):
    length, width = n.shape
    out = jax.ShapeDtypeStruct((2 * width + SMALL, width), BF)
    args = (small, n) + tuple(halves)
    return pl.pallas_call(
        weight_back_kernel,
        grid=(1,),
        in_specs=[pl.BlockSpec(memory_space=pltpu.SMEM)] * 2 + [whole(a) for a in args],
        out_specs=[whole(out)] * 2,
        out_shape=[out] * 2,
        scratch_shapes=[pltpu.VMEM((width, length), BF), pltpu.VMEM((4, width, width), BF)],
        compiler_params=pltpu.CompilerParams(
            dimension_semantics=("arbitrary",), vmem_limit_bytes=VMEM_BACK
        ),
        name="weight_back",
        cost_estimate=CHEAP,
    )(pos, place, *args)


def input_back_kernel(x_ref, dh_ref, w_ref, norm_ref, dnorm_ref, *refs):
    grads_in, (dx_ref, small_ref, sums, dn_ref) = refs[:-4], refs[-4:]
    step = pl.program_id(0)
    tile = x_ref.shape[0]

    @pl.when(step == 0)
    def _():
        sums[...] = jnp.zeros_like(sums)

    first = 0
    for j in range(len(grads_in) // 4):
        count = grads_in[4 * j].shape[0] // tile
        begin = first

        @pl.when((step >= begin) & (step < begin + count))
        def _():
            rows = pl.ds(pl.multiple_of((step - begin) * tile, tile), tile)
            dn = None
            for m in range(4):
                term = dot_nt(grads_in[4 * j + m][rows, :], w_ref[m])
                dn = term if dn is None else dn + term
            dn_ref[...] = dn

        first += count

    dn = dn_ref[...]
    unit, inv = normalise(x_ref[...].astype(F32))
    dx_ref[...] = dh_ref[...] + normalise_back(dn, unit, inv, norm_ref[0:1, :])
    sums[0:1, :] += jnp.sum(dn * unit, axis=0, keepdims=True)
    sums[1:2, :] += jnp.sum(dn, axis=0, keepdims=True)

    @pl.when(step == pl.num_programs(0) - 1)
    def _():
        small_ref[...] = jnp.concatenate(
            [sums[0:2, :], dnorm_ref[0:2, :], jnp.zeros((SMALL - 4, sums.shape[1]), F32)], axis=0
        ).astype(BF)


def input_back(x, dh, w, norm, dnorm, halves):
    length, width = x.shape
    tile = 256
    block = pl.BlockSpec((tile, width), lambda i: (i, 0))
    small = jax.ShapeDtypeStruct((SMALL, width), BF)
    return pl.pallas_call(
        input_back_kernel,
        grid=(length // tile,),
        in_specs=[block] * 2 + [whole(w), whole(norm), whole(dnorm)] + [whole(a) for a in halves],
        out_specs=[block, whole(small)],
        out_shape=[jax.ShapeDtypeStruct((length, width), F32), small],
        scratch_shapes=[pltpu.VMEM((8, width), F32), pltpu.VMEM((tile, width), F32)],
        compiler_params=pltpu.CompilerParams(
            dimension_semantics=("arbitrary",), vmem_limit_bytes=VMEM_BACK
        ),
        name="input_back",
        cost_estimate=CHEAP,
    )(x, dh, w, norm, dnorm, *halves)


def bits_of(size):
    return [1 << b for b in range(size.bit_length() - 1)]


def exchange(values, even, odd):
    dp, shard = lax.axis_size("dp"), lax.axis_size("shard")
    perm = []
    for d in range(dp):
        for s in range(shard):
            axis, bit = odd if s % 2 else even
            other = (d ^ bit, s) if axis == "dp" else (d, s ^ bit)
            perm.append((d * shard + s, other[0] * shard + other[1]))
    return lax.ppermute(values, ("dp", "shard"), perm)


def swap(values, axis, bit):
    return exchange(values, (axis, bit), (axis, bit))


def after(values, *others):
    return lax.optimization_barrier((values,) + others)[0]


def places():
    dp, shard = lax.axis_index("dp"), lax.axis_index("shard")
    piece = jnp.arange(16, dtype=jnp.int32)
    far = (piece // 8) ^ (shard // 2)
    along = (piece % 8) ^ (dp % 8)
    bits = [(along >> b) & 1 for b in range(3)]
    even = far * 8 + bits[0] * 4 + bits[2] * 2 + (piece >> 1 & 1)
    odd = bits[0] * 8 + bits[1] * 4 + far * 2 + (piece >> 2 & 1)
    mine = shard % 2
    return jnp.stack(
        [jnp.where(mine == 0, even, odd), jnp.where(mine == 0, odd, even)]
    ).astype(jnp.int32)


HALVINGS = [
    (("shard", 2), ("dp", 1)),
    (("dp", 1), ("dp", 2)),
    (("dp", 4), ("shard", 2)),
]
MIDDLE = (("dp", 2), ("dp", 4))
GATHERS = [(("dp", 4), ("dp", 2)), (("dp", 1), ("dp", 1))]


def quarters():
    place = lax.axis_index("dp") % 8
    j = jnp.arange(4, dtype=jnp.int32)
    even = j % 2 + 2 * ((place // 4) ^ (j // 2))
    odd = 2 * (j % 2) + ((place // 2 % 2) ^ (j // 2))
    return jnp.where(lax.axis_index("shard") % 2 == 0, even, odd).astype(jnp.int32)


def low_sum(total):
    return lax.reduce_precision(total, 8, 7).astype(BF)


def add_up(parts, low, high):
    total = parts[0][low:high].astype(F32)
    for part in parts[1:]:
        total = total + part[low:high].astype(F32)
    return low_sum(total)


def add_rest(piece):
    for b in bits_of(lax.axis_size("dp"))[3:]:
        piece = add_up([piece, swap(piece, "dp", b)], 0, piece.shape[0])
    return piece


def adam(master, first, second, grad, rate, decay):
    first_new = 0.5 * first + 0.5 * grad
    second_new = 0.5 * second + 0.5 * grad * grad
    correction = 1.0 - 0.5**STEP
    update = first_new / correction / (jnp.sqrt(second_new / correction) + 1e-08)
    return master - rate * (update + decay * master), first_new, second_new


def gather_rows(index_ref, source, target, span, base):
    count = index_ref.shape[0]
    rows = LANES // 2 // count
    units = target.shape[0] // span
    for j in range(count):
        for u in range(units):
            place = pl.ds(pl.multiple_of(u * span + base + index_ref[j] * rows, rows), rows)
            first = (j * units + u) * rows
            target[place, :] = source[first : first + rows, :]


def squares_kernel(early_ref, late_ref, gn_ref, out_ref):
    total = 0.5 * jnp.sum(jnp.square(gn_ref[...]))
    for ref in (early_ref, late_ref):
        values = ref[...].astype(F32)
        total += jnp.sum(values * values)
    out_ref[...] = jnp.full(out_ref.shape, total, F32)


def squares(early, late, gn):
    vmem = pl.BlockSpec(memory_space=pltpu.VMEM)
    return pl.pallas_call(
        squares_kernel,
        in_specs=[vmem] * 3,
        out_specs=vmem,
        out_shape=jax.ShapeDtypeStruct((8, LANES), F32),
        compiler_params=pltpu.CompilerParams(vmem_limit_bytes=VMEM_UNPACK),
        name="squares",
        cost_estimate=CHEAP,
    )(early, late, gn)


def clip_factor(square_ref, other_ref):
    norm = jnp.sqrt(square_ref[0:1, 0:1] + other_ref[0:1, 0:1])
    return jnp.minimum(1.0, 1.0 / (norm + 1e-06))


def renew_kernel(
    side_ref, index_ref, square_ref, other_ref, early_ref, late_ref, gn_ref, nm, nf, ns,
    am, af, as_, um, uf, us, dm, df, ds, first_ref, second_ref, clip_ref, early, late
):
    factor = clip_factor(square_ref, other_ref)
    width = early.shape[1]
    half = LANES // 2
    step = pl.program_id(0)
    height = am.shape[1]

    @pl.when(step == 0)
    def _():
        gather_rows(index_ref, early_ref, early, half, 0)
        gather_rows(index_ref, late_ref, late, half, 0)
        new = adam(nm[...], nf[...], ns[...], gn_ref[...] * factor, 0.3, 0.0)
        last = FIRST_UNITS * half
        first_ref[last:, :] = jnp.zeros((SMALL, width), BF)
        first_ref[last : last + 4, 0:LANES] = new[0].astype(BF)
        clip_ref[0] = jnp.sqrt(square_ref[0:1, 0:1] + other_ref[0:1, 0:1])[0, 0]

    def span(unit):
        return pl.ds(pl.multiple_of(unit * half + step * height, height), height)

    blocks = um.shape[1] // width
    middle = FIRST_UNITS
    for unit in range(5 + blocks + dm.shape[0]):
        if unit < 4:
            source = late[span(unit), :]
        else:
            source = early[span(unit - 4), :]
        if unit < 5:
            state = am[unit], af[unit], as_[unit]
        elif unit < 5 + blocks:
            cols = slice((unit - 5) * width, (unit - 4) * width)
            state = um[:, cols], uf[:, cols], us[:, cols]
        else:
            state = [ref[unit - 5 - blocks] for ref in (dm, df, ds)]
        new = adam(*state, source.astype(F32) * factor, 0.05, 0.01)
        target, place = (first_ref, unit) if unit < middle else (second_ref, unit - middle)
        target[span(place), :] = new[0].astype(BF)


def renew(side, index, square, early, late, gn, attn, up, down, norm):
    five, part, width = attn[0].shape
    hidden = up[0].shape[1]
    steps = 2
    half = part // 2
    tile = half // steps
    down = [a.reshape(a.shape[0] // part, part, width) for a in down]
    units = five + hidden // width + down[0].shape[0]
    first = jax.ShapeDtypeStruct((FIRST_UNITS * half + SMALL, width), BF)
    second = jax.ShapeDtypeStruct(((units - FIRST_UNITS) * half, width), BF)
    tall = down[0].shape[0]
    return pl.pallas_call(
        renew_kernel,
        grid_spec=pltpu.PrefetchScalarGridSpec(
            num_scalar_prefetch=1,
            grid=(steps,),
            in_specs=[pl.BlockSpec(memory_space=pltpu.SMEM)]
            + [whole(a) for a in (*square, early, late, gn, *norm)]
            + [pl.BlockSpec((five, tile, width), lambda i, side: (0, steps * side[0] + i, 0))] * 3
            + [pl.BlockSpec((tile, hidden), lambda i, side: (steps * side[0] + i, 0))] * 3
            + [pl.BlockSpec((tall, tile, width), lambda i, side: (0, steps * side[0] + i, 0))] * 3,
            out_specs=[whole(first), whole(second), pl.BlockSpec(memory_space=pltpu.SMEM)],
            scratch_shapes=[pltpu.VMEM(early.shape, BF), pltpu.VMEM(late.shape, BF)],
        ),
        out_shape=[first, second, jax.ShapeDtypeStruct((1,), F32)],
        compiler_params=pltpu.CompilerParams(
            dimension_semantics=("arbitrary",), vmem_limit_bytes=VMEM_UPDATE
        ),
        name="renew",
        cost_estimate=CHEAP,
    )(side, index, *square, early, late, gn, *norm, *attn, *up, *down)


def update_kernel(
    side_ref, index_ref, square_ref, other_ref, early_ref, late_ref, got_ref, gn_ref, *refs
):
    am, af, as_, um, uf, us, dm, df, ds, nm, nf, ns = refs[:12]
    early, late = refs[-2:]
    outs, copy_low, copy_high, other_half = refs[12:-5], refs[-5], refs[-4], refs[-3]
    step = pl.program_id(0)
    factor = clip_factor(square_ref, other_ref)
    width = early.shape[1]
    part = late.shape[0] // 4
    blocks = um.shape[1] // width
    height = part // pl.num_programs(0)
    half = LANES // 2

    def keep(group, where, unit, size, new):
        for target, value in zip(outs[3 * group : 3 * group + 3], new):
            target[where] = value
        target, unit = (copy_low, unit) if unit < 8 else (copy_high, unit - 8)
        rows = pl.ds(pl.multiple_of(unit * part + step * size, size), size)
        target[rows, :] = new[0].astype(BF)

    @pl.when(step == 0)
    def _():
        mine = half * side_ref[0]
        count = late_ref.shape[0]
        gather_rows(index_ref, early_ref, early, part, mine)
        gather_rows(index_ref, late_ref, late, part, mine)
        gather_rows(index_ref, got_ref.at[:count, :], late, part, half - mine)
        gather_rows(index_ref, got_ref.at[count:, :], early, part, half - mine)
        new = adam(nm[...], nf[...], ns[...], gn_ref[...] * factor, 0.3, 0.0)
        outs[9][...], outs[10][...], outs[11][...] = new

    def span(base, size):
        return pl.ds(pl.multiple_of(base + step * size, size), size)

    for m in range(5):
        source = late[span(m * part, height), :] if m < 4 else early[span(0, height), :]
        new = adam(am[m], af[m], as_[m], source.astype(F32) * factor, 0.05, 0.01)
        keep(0, (m, slice(None), slice(None)), m, height, new)
    for j in range(blocks):
        source = early[span((j + 1) * part, height), :]
        cols = (slice(None), slice(j * width, (j + 1) * width))
        new = adam(um[cols], uf[cols], us[cols], source.astype(F32) * factor, 0.05, 0.01)
        keep(1, cols, 5 + j, height, new)
    tall = dm.shape[0]
    source = early[span((blocks + 1) * part, tall), :]
    new = adam(dm[...], df[...], ds[...], source.astype(F32) * factor, 0.05, 0.01)
    keep(2, (slice(None), slice(None)), 5 + blocks, tall, new)

    @pl.when(step == pl.num_programs(0) - 1)
    def _():
        count = other_half.shape[0] // half
        base = copy_high.shape[0] - count * part
        for j in range(count):
            rows = pl.ds(pl.multiple_of(base + j * part + half - half * side_ref[0], half), half)
            other_half[j * half : (j + 1) * half, :] = copy_high[rows, :]


def update(side, index, square, early, late, got, gn, attn, up, down, norm):
    steps = 4
    smem = pl.BlockSpec(memory_space=pltpu.SMEM)
    five, part, width = attn[0].shape
    specs = (
        [pl.BlockSpec((five, part // steps, width), lambda i: (0, i, 0))] * 3
        + [pl.BlockSpec((part // steps, up[0].shape[1]), lambda i: (i, 0))] * 3
        + [pl.BlockSpec((down[0].shape[0] // steps, width), lambda i: (i, 0))] * 3
        + [whole(norm[0])] * 3
    )
    arrays = tuple(attn) + tuple(up) + tuple(down) + tuple(norm)
    low = jax.ShapeDtypeStruct((8 * part, width), BF)
    tall, short = 2 * early.shape[0], 2 * late.shape[0]
    high = jax.ShapeDtypeStruct((tall + short - 8 * part, width), BF)
    other = jax.ShapeDtypeStruct((DIRECT_UNITS * part // 2, width), BF)
    return pl.pallas_call(
        update_kernel,
        grid=(steps,),
        in_specs=[smem] * 2 + [whole(a) for a in (*square, early, late, got, gn)] + specs,
        out_specs=specs + [whole(low), whole(high), whole(other)],
        out_shape=[jax.ShapeDtypeStruct(a.shape, F32) for a in arrays] + [low, high, other],
        scratch_shapes=[pltpu.VMEM((tall, width), BF), pltpu.VMEM((short, width), BF)],
        compiler_params=pltpu.CompilerParams(
            dimension_semantics=("arbitrary",), vmem_limit_bytes=VMEM_UPDATE
        ),
        name="update",
        cost_estimate=CHEAP,
    )(side, index, *square, early, late, got, gn, *arrays)


def place_unit(pos, source, unit, first, count, attn_ref, up_ref, down_ref, sem):
    width = attn_ref.shape[2]
    blocks = up_ref.shape[1] // width
    tall = down_ref.shape[0] // 4
    rows = pl.ds(pl.multiple_of(pos * LANES + first, count), count)
    if unit < 5:
        target = attn_ref.at[unit, rows, :]
    elif unit < 5 + blocks:
        target = up_ref.at[rows, pl.ds((unit - 5) * width, width)]
    else:
        base = pl.multiple_of(pos * tall + (unit - 5 - blocks) * LANES + first, count)
        target = down_ref.at[pl.ds(base, count), :]
    return pltpu.make_async_copy(source, target, sem)


def run_copies(copies):
    for copy in copies:
        copy.start()
    for copy in copies:
        copy.wait()


def place_whole(pos, piece, unit, outs, sems, copies):
    for j in range(piece.shape[0] // LANES):
        source = piece.at[pl.ds(j * LANES, LANES), :]
        copies.append(place_unit(pos, source, unit + j, 0, LANES, *outs, sems.at[len(copies)]))


def place_half(pos, side, piece, unit, outs, sems, copies):
    half = LANES // 2
    for j in range(piece.shape[0] // half):
        source = piece.at[pl.ds(j * half, half), :]
        copies.append(
            place_unit(pos, source, unit + j, half * side, half, *outs, sems.at[len(copies)])
        )


def unpack_near_kernel(pos_ref, side_ref, p0, p1, p2, p3, p4, p5, attn_ref, up_ref, down_ref, sems):
    copies = []
    outs = attn_ref, up_ref, down_ref
    for index, parts in enumerate(((p0, p1), (p2, p3))):
        place_whole(pos_ref[index], parts[0], 0, outs, sems, copies)
        place_whole(pos_ref[index], parts[1], 8, outs, sems, copies)
    for index, piece in enumerate((p4, p5)):
        place_half(pos_ref[2 + index], side_ref[0], piece, 0, outs, sems, copies)
    run_copies(copies)


def unpack_far_kernel(pos_ref, side_ref, *refs):
    pieces, outs, sems = refs[:8], refs[11:14], refs[14]
    copies = []
    other = side_ref[0] ^ 1
    for index in range(2):
        second, first_other, second_other, direct = pieces[4 * index : 4 * index + 4]
        pos = pos_ref[2 + index]
        place_half(pos, side_ref[0], second, FIRST_UNITS, outs, sems, copies)
        place_half(pos, other, first_other, 0, outs, sems, copies)
        place_half(pos, other, second_other, FIRST_UNITS, outs, sems, copies)
        unit = FIRST_UNITS + second_other.shape[0] // (LANES // 2)
        place_half(pos, other, direct, unit, outs, sems, copies)
    run_copies(copies)


def share_copies(pos, side, first, second, low, high, direct, width, hidden):
    units = (low.shape[0] + high.shape[0]) // LANES
    half = LANES // 2
    last_rows = swap(first[FIRST_UNITS * half :], "shard", 1)
    ours, first_too, low, high, direct = lax.optimization_barrier(
        (swap(first, "shard", 2), last_rows, low, high, direct)
    )
    other = swap(ours, "dp", 1)
    second_got = swap(after(second, ours), "shard", 2)
    near = [swap(part, "shard", 1) for part in (low, high)]
    ours_too = swap(ours, "shard", 1)
    a, b, c, d = [
        p[p.shape[0] - SMALL : p.shape[0] - SMALL + 4, :LANES]
        for p in (first, first_too, ours, ours_too)
    ]
    low_bit, high_bit = pos[0] % 2 == 1, pos[0] // 2 == 1
    a, b, c, d = [jnp.where(low_bit, v, u) for u, v in ((a, b), (b, a), (c, d), (d, c))]
    a, b, c, d = [jnp.where(high_bit, v, u) for u, v in ((a, c), (b, d), (c, a), (d, b))]
    norms = jnp.concatenate([a, b, c, d], axis=1)
    hbm = pl.BlockSpec(memory_space=pl.ANY)
    vmem = pl.BlockSpec(memory_space=pltpu.VMEM)
    smem = pl.BlockSpec(memory_space=pltpu.SMEM)
    shapes = [
        jax.ShapeDtypeStruct((5, width, width), BF),
        jax.ShapeDtypeStruct((width, hidden), BF),
        jax.ShapeDtypeStruct((hidden, width), BF),
    ]
    params = pltpu.CompilerParams(vmem_limit_bytes=VMEM_UNPACK)
    begun = pl.pallas_call(
        unpack_near_kernel,
        in_specs=[smem, smem] + [vmem] * 6,
        out_specs=[hbm] * 3,
        out_shape=shapes,
        scratch_shapes=[pltpu.SemaphoreType.DMA((2 * (units + FIRST_UNITS),))],
        compiler_params=params,
        name="unpack_near",
        cost_estimate=CHEAP,
    )(pos, side, after(low, norms), high, *near, ours, ours_too)
    second = after(second_got, begun[0])
    second_other = swap(second[: -direct.shape[0]], "dp", 1)
    direct = swap(after(direct, second), "shard", 2)
    far = [second, other, second_other, direct]
    far += [swap(after(f, begun[0]), "shard", 1) for f in far]
    done = pl.pallas_call(
        unpack_far_kernel,
        in_specs=[smem, smem] + [vmem] * 8 + [hbm] * 3,
        out_specs=[hbm] * 3,
        out_shape=shapes,
        scratch_shapes=[pltpu.SemaphoreType.DMA((4 * units,))],
        input_output_aliases={10: 0, 11: 1, 12: 2},
        compiler_params=params,
        name="unpack_far",
        cost_estimate=CHEAP,
    )(pos, side, *far, *begun)
    return tuple(done) + (norms,)


def shards(
    tokens, out_grad, domain_ids, domain_weight,
    attn_master, attn_first, attn_second,
    up_master, up_first, up_second,
    down_master, down_first, down_second,
    norm_master, norm_first, norm_second,
):
    length, width = tokens.shape
    hidden = up_master.shape[1]
    part = width // 4
    blocks = hidden // width
    dp = lax.axis_index("dp")
    shard = lax.axis_index("shard").astype(jnp.int32)
    pos = shard ^ jnp.arange(4, dtype=jnp.int32)
    half = (dp % 2).astype(jnp.int32)[None]
    place = places()

    small = jnp.pad(norm_master.astype(BF), ((0, SMALL - 4), (0, width - part)))
    rows = attn_master[:4].astype(BF).reshape(4 * part, width)
    own = jnp.concatenate([rows[: 2 * part], small, rows[2 * part :], jnp.zeros_like(small)])
    middle = own.shape[0] // 2
    near = swap(own, "shard", 1)
    ours = lax.dynamic_slice(own, (half[0] * middle, 0), (middle, width))
    far_a = swap(ours, "shard", 2)

    domains = domain_weight.shape[0]
    devices = lax.axis_size("dp") * lax.axis_size("shard") * domain_ids.shape[0]
    onehot = (domain_ids[:, None] == jnp.arange(domains, dtype=jnp.int32)[None, :]).astype(F32)
    counts = jnp.sum(onehot, axis=0)
    dp_bits = bits_of(lax.axis_size("dp"))
    for b in dp_bits[:2]:
        counts = counts + swap(counts, "dp", b)
    far_b = swap(after(far_a, counts), "dp", 1)
    second = jnp.concatenate(
        [attn_master[4].astype(BF)]
        + [up_master[:, j * width : (j + 1) * width].astype(BF) for j in range(blocks)]
    )
    second_far = swap(after(second, counts), "shard", 2)
    for b in dp_bits[2:]:
        counts = counts + after(swap(counts, "dp", b), far_b)
    counts_row = jnp.pad(counts.astype(BF)[None], ((0, SMALL - 1), (0, width - domains)))
    third = jnp.concatenate([down_master.astype(BF), counts_row])
    third_far = swap(third, "shard", 2)
    second = [second, swap(second, "shard", 1), second_far]
    third = [third, swap(third, "shard", 1), third_far]
    domain_rows = jnp.pad(
        jnp.stack([onehot[0], domain_weight * devices / domains]),
        ((0, 6), (0, LANES - domains)),
    )
    far_c = swap(far_a, "shard", 1)
    far = [far_a, far_b, far_c, swap(far_b, "shard", 1)]
    q, k, v, n, e, eb, z, o, weights, scores, keys, values, w, norm = attend(
        pos, half, tokens, [own, near] + far
    )
    for pieces in (second, third):
        pieces.append(swap(after(pieces[2], o), "shard", 1))
    y, dh, do, send, keep, dnorm = feed(
        pos, place, domain_rows, tokens, out_grad, o, norm, second, third
    )

    steps, plan, index = HALVINGS + [MIDDLE], GATHERS, quarters()
    pieces = 16
    rows = keep.shape[0] // pieces

    def forward_phase(parts, phase, rows):
        low = rows * pieces >> (phase + 1)
        return add_up(parts, low, 2 * low)

    saved = (q, k, v, eb, e, z, weights, scores, keys, values)
    chunks = length // CHUNK
    early = [keep, swap(send, "shard", 1)]
    later = mix_back(chunks - 1, 1, (), do, *saved)
    out = after(forward_phase(early, 0, rows), later[0])
    early.append(exchange(out, *steps[0]))
    sooner = mix_back(chunks - 2, chunks - 1, later[4:], after(do, out), *saved)
    back = list(sooner[:4]) + list(later[:4])
    out = after(forward_phase(early, 1, rows), back[0])
    early.append(exchange(out, *steps[1]))
    dx, small = input_back(tokens, after(dh, out), w, norm, dnorm, back)
    send, keep = weight_back(pos, place, small, n, back)
    turn = forward_phase(early, 2, rows)
    got = exchange(turn, *steps[2])
    late = [keep, swap(after(send, turn), "shard", 1)]
    height = keep.shape[0] - SMALL
    thin = height // pieces
    small = add_up(late, height, height + SMALL)

    def late_phase(phase):
        out = jnp.concatenate([forward_phase(late, phase, thin), small])
        return out, exchange(out, *steps[phase])

    def late_sum(got):
        late.append(got)
        return add_up([small, got[got.shape[0] - SMALL :]], 0, SMALL)

    turn, late_got = late_phase(0)
    small = late_sum(late_got)
    turn, late_got = late_phase(1)
    early.append(after(got, turn))
    turn = add_up(early, 0, 2 * rows)
    got = exchange(turn, *steps[3])
    small = late_sum(after(late_got, turn))
    early = turn
    turn, late_got = late_phase(2)
    early = add_rest(add_up([early, after(got, turn)], 0, 2 * rows))
    got = exchange(early, *plan[0])
    small = late_sum(after(late_got, early))
    out = jnp.concatenate([add_up(late, 0, 2 * thin), small])
    late_got = exchange(out, *steps[3])
    late = add_rest(add_up([out, late_got], 0, 2 * thin + SMALL))
    late, small = late[: 2 * thin], late[2 * thin :]
    late_got = exchange(late, *plan[0])
    norm_grad = lax.dynamic_slice(small[:4], (0, shard * part), (4, part)).astype(F32)
    early = jnp.concatenate([early, after(got, late)])
    late = jnp.concatenate([late, after(late_got, early)])
    square = squares(early, late, norm_grad)
    square = square + swap(square, "dp", 1)
    got = exchange(after(jnp.concatenate([late, early]), square), *plan[1])
    square = square + swap(square, "shard", 1)
    square = (square, swap(square, "shard", 2))
    attn = (attn_master, attn_first, attn_second)
    up = (up_master, up_first, up_second)
    down = (down_master, down_first, down_second)
    norms = (norm_master, norm_first, norm_second)
    first, second, clip_norm = renew(
        half, index, square, early, late, norm_grad, attn, up, down, norms
    )
    *new, low, high, direct = update(
        half, index, square, early, late, after(got, first), norm_grad, attn, up, down, norms
    )
    copies = share_copies(pos, half, first, second, low, high, direct, width, hidden)
    return (y, dx) + tuple(new) + (clip_norm.reshape(()),) + tuple(copies)


def solution(mesh):
    rows = P(("dp", "shard"), None)
    attn = (P(None, "shard", None),) * 3
    tall = (P("shard", None),) * 6
    norm = (P(None, "shard"),) * 3
    return jax.shard_map(
        shards,
        mesh=mesh,
        in_specs=(rows, rows, P(("dp", "shard")), P()) + attn + tall + norm,
        out_specs=(rows, rows) + attn + tall + norm + (P(),) * 5,
        check_vma=False,
    )
```

```python
import functools
import jax
import jax.numpy as jnp
from jax import lax
from jax.experimental import pallas as pl
from jax.experimental.pallas import tpu as pltpu
from jax.sharding import PartitionSpec as P

BF = jnp.bfloat16
F32 = jnp.float32
MIB = 1024 * 1024
VMEM_ATTEND = 48 * MIB
VMEM_MIX = 44 * MIB
VMEM_FEED = 44 * MIB
VMEM_BACK = 24 * MIB
VMEM_UPDATE = 56 * MIB
VMEM_UNPACK = 24 * MIB
CHUNK = 256
SLOT = 64
GROUP = 256
LANES = 128
SMALL = 16
FIRST_UNITS = 7
DIRECT_UNITS = 2
CHEAP = pl.CostEstimate(flops=1, bytes_accessed=1, transcendentals=0)
STEP = 10
TILE = 512
COUNTS = (1, 2, 1)


def whole(a):
    return pl.BlockSpec(a.shape, lambda *_: (0,) * len(a.shape), pipeline_mode=pl.Buffered(1))


def dot(a, b):
    return jnp.dot(a, b, preferred_element_type=F32)


def dot_nt(a, b):
    return lax.dot_general(a, b, (((1,), (1,)), ((), ())), preferred_element_type=F32)


def dot_tn(a, b):
    return lax.dot_general(a, b, (((0,), (0,)), ((), ())), preferred_element_type=F32)


def head_of(shape, dim):
    return lax.broadcasted_iota(jnp.int32, shape, dim) // SLOT


def block_diagonal(state):
    return jnp.where(head_of(state.shape, 0) == head_of(state.shape, 1), state, 0.0).astype(BF)


def only_head(rows, head):
    return jnp.where(head_of(rows.shape, 1) == head, rows, jnp.zeros_like(rows))


def by_head(rows):
    return jnp.concatenate([only_head(rows, h) for h in range(GROUP // SLOT)], axis=0)


def lower(square):
    size = square.shape[0]
    row = lax.broadcasted_iota(jnp.int16, (size, size), 0)
    col = lax.broadcasted_iota(jnp.int16, (size, size), 1)
    return jnp.concatenate(
        [
            jnp.where(row >= col, square[:, first : first + size].astype(BF), jnp.zeros((), BF))
            for first in range(0, square.shape[1], size)
        ],
        axis=1,
    )


def upper(square):
    size = square.shape[1]
    row = lax.broadcasted_iota(jnp.int16, (size, size), 0)
    col = lax.broadcasted_iota(jnp.int16, (size, size), 1)
    return jnp.concatenate(
        [
            jnp.where(row <= col, square[first : first + size, :].astype(BF), jnp.zeros((), BF))
            for first in range(0, square.shape[0], size)
        ],
        axis=1,
    )


def split_dot(ones, values):
    high = values.astype(BF)
    low = (values - high.astype(F32)).astype(BF)
    return dot(ones, high) + dot(ones, low)


def head_ones():
    return jnp.where(
        head_of((GROUP, GROUP), 0) == head_of((GROUP, GROUP), 1), 1.0, 0.0
    ).astype(BF)


def head_sums(values):
    ones = head_ones()
    high = values.astype(BF)
    low = (values - high.astype(F32)).astype(BF)
    return dot(high, ones) + dot(low, ones)


def head_max(values):
    top = None
    head = head_of(values.shape, 1)
    for index in range(GROUP // SLOT):
        mine = jnp.max(jnp.where(head == index, values, -jnp.inf), axis=1, keepdims=True)
        top = mine if top is None else jnp.where(head == index, mine, top)
    return top


def normalise(values):
    centred = values - jnp.mean(values, axis=-1, keepdims=True)
    inv = lax.rsqrt(jnp.mean(centred * centred, axis=-1, keepdims=True) + 1e-05)
    return centred * inv, inv


def normalise_back(grad, unit, inv, gain):
    scaled = grad * gain
    return inv * (
        scaled
        - jnp.mean(scaled, axis=-1, keepdims=True)
        - unit * jnp.mean(scaled * unit, axis=-1, keepdims=True)
    )


def attend_kernel(
    pos_ref, half_ref, x_ref, near0, near1, far0, far1, far2, far3,
    q_ref, k_ref, v_ref, n_ref, e_ref, eb_ref, z_ref, o_ref, w_ref, s_ref, keys_ref, values_ref,
    weights_ref, norm_ref, keys, values, carry
):
    width = x_ref.shape[1]
    part = width // 4

    @pl.when(pl.program_id(0) == 0)
    def _():
        low = far0.shape[0]

        def rows_of(index, first, count):
            if index < 2:
                return (near0, near1)[index][first : first + count, :]
            a, b = ((far0, far1), (far2, far3))[index - 2]
            if first >= low:
                a, b, first = b, a, first - low
            return jnp.where(half_ref[0] == 0, a[first : first + count, :], b[first : first + count, :])

        for index in range(4):
            rows = pl.ds(pl.multiple_of(pos_ref[index] * part, part), part)
            for m in range(4):
                weights_ref[m, rows, :] = rows_of(index, m * part + SMALL * (m > 1), part)
            norm_ref[:, rows] = rows_of(index, 2 * part, SMALL)[0:8, 0:part].astype(F32)
        carry[...] = jnp.zeros_like(carry)
        keys[...] = jnp.zeros_like(keys)
        values[...] = jnp.zeros_like(values)

    heads = range(GROUP // SLOT)
    groups = range(keys.shape[0])
    cols = [slice(i * GROUP, (i + 1) * GROUP) for i in groups]
    unit, _ = normalise(x_ref[...].astype(F32))
    normed = (unit * norm_ref[0:1, :] + norm_ref[1:2, :]).astype(BF)
    n_ref[...] = normed
    rows = normed.shape[0]
    ones = lower(jnp.ones((rows, rows), F32))
    q, k, v, e, inv = [], [], [], [], []
    for c in cols:
        raised = jnp.exp(dot(normed, weights_ref[3, :, c]))
        z = split_dot(ones, raised) + carry[0:1, c]
        carry[0:1, c] = z[rows - 1 : rows, :]
        e_ref[:, c] = raised
        z_ref[:, c] = z
        e.append(raised.astype(BF))
        inv.append(1.0 / z)
        for m, part_of in enumerate((q, k, v)):
            part_of.append(dot(normed, weights_ref[m, :, c]).astype(BF))
    for i in groups:
        q_ref[:, cols[i]], k_ref[:, cols[i]], v_ref[:, cols[i]] = q[i], k[i], v[i]
        eb_ref[:, cols[i]] = e[i]
    total, value_state = [], []
    for i in groups:
        state = block_diagonal(keys[i])
        keys_ref[i, 0] = state
        total.append(dot(q[i], state))
        state = block_diagonal(values[i])
        values_ref[i, 0] = state
        value_state.append(state)
    es = [by_head(e[i]) for i in groups]
    for i in groups:
        total[i] += dot(lower(dot_nt(q[i], by_head(k[i]))), es[i])
    scores = [total[i] * inv[i] * 0.125 for i in groups]
    raised = [jnp.exp(scores[i] - head_max(scores[i])) for i in groups]
    weights = [raised[i] / head_sums(raised[i]) for i in groups]
    ratio = [(weights[i] * inv[i]).astype(BF) for i in groups]
    out = [dot(ratio[i], value_state[i]) for i in groups]
    for i in groups:
        out[i] += dot(lower(dot_nt(ratio[i], es[i])), by_head(v[i]))
    for i in groups:
        s_ref[:, cols[i]] = scores[i]
        w_ref[:, cols[i]] = weights[i]
        o_ref[:, cols[i]] = out[i].astype(BF)
        keys[i] += dot_tn(k[i], e[i])
        values[i] += dot_tn(e[i], v[i])


def attend(pos, half, x, pieces):
    length, width = x.shape
    steps, groups = length // CHUNK, width // GROUP
    rows = lambda dtype: jax.ShapeDtypeStruct((length, width), dtype)
    block = pl.BlockSpec((CHUNK, width), lambda i: (i, 0))
    state = pl.BlockSpec((groups, 1, GROUP, GROUP), lambda i: (0, i, 0, 0))
    states = jax.ShapeDtypeStruct((groups, steps, GROUP, GROUP), BF)
    full = [jax.ShapeDtypeStruct((4, width, width), BF), jax.ShapeDtypeStruct((8, width), F32)]
    return pl.pallas_call(
        attend_kernel,
        grid=(steps,),
        in_specs=[pl.BlockSpec(memory_space=pltpu.SMEM)] * 2 + [block] + [whole(p) for p in pieces],
        out_specs=[block] * 10 + [state] * 2 + [whole(a) for a in full],
        out_shape=[rows(BF)] * 4
        + [rows(F32), rows(BF), rows(F32), rows(BF), rows(F32), rows(F32), states, states]
        + full,
        scratch_shapes=[pltpu.VMEM((groups, GROUP, GROUP), F32)] * 2 + [pltpu.VMEM((8, width), F32)],
        compiler_params=pltpu.CompilerParams(
            dimension_semantics=("arbitrary",), vmem_limit_bytes=VMEM_ATTEND
        ),
        name="attend",
        cost_estimate=CHEAP,
    )(pos, half, x, *pieces)


def mix_back_kernel(*refs, begun):
    g_ref, q_ref, k_ref, v_ref, eb_ref, e_ref, z_ref, w_ref, s_ref, keys_ref, values_ref = refs[:11]
    before, (dq_ref, dk_ref, dv_ref, dc_ref, later_v, later_k, carry) = refs[11:-7], refs[-7:]

    @pl.when(pl.program_id(0) == 0)
    def _():
        if begun:
            later_v[...], later_k[...], carry[...] = [ref[...] for ref in before]
        else:
            later_v[...] = jnp.zeros_like(later_v)
            later_k[...] = jnp.zeros_like(later_k)
            carry[...] = jnp.zeros_like(carry)

    heads = range(GROUP // SLOT)
    groups = range(later_v.shape[0])
    cols = [slice(i * GROUP, (i + 1) * GROUP) for i in groups]
    g, q, k, v, e = [[ref[:, c] for c in cols] for ref in (g_ref, q_ref, k_ref, v_ref, eb_ref)]
    inv = [1.0 / z_ref[:, c] for c in cols]
    weights = [w_ref[:, c] for c in cols]
    ratio = [(weights[i] * inv[i]).astype(BF) for i in groups]
    es = [by_head(e[i]) for i in groups]
    state = [block_diagonal(later_v[i]) for i in groups]
    d_ratio = [dot_nt(g[i], values_ref[i, 0]) for i in groups]
    dv = [dot(e[i], state[i]) for i in groups]
    de = [dot_nt(v[i], state[i]) for i in groups]
    for i in groups:
        vs = by_head(v[i])
        d_ratio[i] += dot(lower(dot_nt(g[i], vs)), es[i])
        de[i] += dot(upper(dot_nt(vs, g[i])), by_head(ratio[i]))
        dv[i] += dot(upper(dot_nt(es[i], ratio[i])), by_head(g[i]))
    d_weights = [d_ratio[i] * inv[i] for i in groups]
    both = [d_weights[i] * weights[i] for i in groups]
    d_scores = [weights[i] * (d_weights[i] - head_sums(both[i])) for i in groups]
    dn = [(d_scores[i] * inv[i] * 0.125).astype(BF) for i in groups]
    dz = [-(both[i] + d_scores[i] * s_ref[:, cols[i]]) * inv[i] for i in groups]
    state = [block_diagonal(later_k[i]) for i in groups]
    dq = [dot_nt(dn[i], keys_ref[i, 0]) for i in groups]
    dk = [dot(e[i], state[i]) for i in groups]
    de = [de[i] + dot_nt(k[i], state[i]) for i in groups]
    for i in groups:
        ks = by_head(k[i])
        dq[i] += dot(lower(dot_nt(dn[i], es[i])), ks)
        dk[i] += dot(upper(dot_nt(es[i], dn[i])), by_head(q[i]))
        de[i] += dot(upper(dot_nt(ks, q[i])), by_head(dn[i]))
    rows = dz[0].shape[0]
    ones = upper(jnp.ones((rows, rows), F32))
    for i in groups:
        dv_ref[:, cols[i]] = dv[i].astype(BF)
        dq_ref[:, cols[i]] = dq[i].astype(BF)
        dk_ref[:, cols[i]] = dk[i].astype(BF)
        z_sum = split_dot(ones, dz[i]) + carry[0:1, cols[i]]
        carry[0:1, cols[i]] = z_sum[0:1, :]
        dc_ref[:, cols[i]] = ((de[i] + z_sum) * e_ref[:, cols[i]]).astype(BF)
        later_v[i] += dot_tn(ratio[i], g[i])
        later_k[i] += dot_tn(dn[i], q[i])


def mix_back(last, count, before, g, q, k, v, eb, e, z, w, s, keys, values):
    length, width = q.shape
    groups = width // GROUP
    block = pl.BlockSpec((CHUNK, width), lambda i: (last - i, 0))
    state = pl.BlockSpec((groups, 1, GROUP, GROUP), lambda i: (0, last - i, 0, 0))
    out = pl.BlockSpec((CHUNK, width), lambda i: (count - 1 - i, 0))
    rows = jax.ShapeDtypeStruct((count * CHUNK, width), BF)
    sums = [jax.ShapeDtypeStruct((groups, GROUP, GROUP), F32)] * 2
    sums += [jax.ShapeDtypeStruct((8, width), F32)]
    return pl.pallas_call(
        functools.partial(mix_back_kernel, begun=bool(before)),
        grid=(count,),
        in_specs=[block] * 9 + [state] * 2 + [whole(a) for a in before],
        out_specs=[out] * 4 + [whole(a) for a in sums],
        out_shape=[rows] * 4 + sums,
        compiler_params=pltpu.CompilerParams(
            dimension_semantics=("arbitrary",), vmem_limit_bytes=VMEM_MIX
        ),
        name="mix_back",
        cost_estimate=CHEAP,
    )(g, q, k, v, eb, e, z, w, s, keys, values, *before)


def scatter_unit(place_ref, grads, first, unit, shard, target, table):
    count = place_ref.shape[1] // 2
    part = LANES
    rows = part // count
    height = target.shape[0] // LANES * LANES // (2 * count)
    for d in range(count):
        place = place_ref[table, (shard // 2) * count + d]
        where = pl.ds(pl.multiple_of(place * height + unit * rows, rows), rows)
        group = d % 2 * (count // 2) + d // 2
        target[where, :] = grads[pl.ds(pl.multiple_of(first + group * rows, rows), rows), :]


def scatter_shards(pos_ref, place_ref, grads, send_ref, keep_ref, unit):
    for index in range(4):
        pos = pos_ref[index]
        target = send_ref if index % 2 else keep_ref
        scatter_unit(place_ref, grads, pos * LANES, unit, pos, target, index % 2)


def feed_kernel(
    pos_ref, place_ref, domain_ref, x_ref, g_ref, o_ref, norm_ref, p0, p1, p2, p3, t0, t1, t2, t3,
    y_ref, dh_ref, do_ref, send_ref, keep_ref, dnorm_ref,
    wo, w1, w2, branch, unit_ref, inv_ref, n2, gb, n2_t, dn2, grads, u_all, da_all, factor_ref
):
    step = pl.program_id(0)
    last = pl.num_programs(0) - 1
    length, width = x_ref.shape
    part = width // 4
    block = w1.shape[2]
    tiles = length // 256

    @pl.when(step == 0)
    def _():
        for index, (piece, tall) in enumerate(((p0, t0), (p1, t1), (p2, t2), (p3, t3))):
            pos = pos_ref[index]
            rows = pl.ds(pl.multiple_of(pos * part, part), part)
            wo[rows, :] = piece[0:part, :]
            for j in range(4):
                w1[j, rows, :] = piece[(j + 1) * part : (j + 2) * part, :]
            w2[pos] = tall[0:block, :]
        count = sum(t[block : block + SMALL, 0:LANES].astype(F32) for t in (t0, t1, t2, t3))
        share = domain_ref[0:1, :] * domain_ref[1:2, :] / jnp.maximum(count[0:1, :], 1.0)
        factor_ref[...] = jnp.broadcast_to(jnp.sum(share, axis=1, keepdims=True), factor_ref.shape)

        def before(i, _):
            rows = slice(i * 256, (i + 1) * 256)
            h1 = x_ref[rows, :].astype(F32) + dot(o_ref[rows, :], wo[...])
            branch[rows, :] = h1
            unit, inv = normalise(h1)
            unit_ref[rows, :] = unit
            inv_ref[rows, :] = jnp.broadcast_to(inv, (256, 128))
            normed = (unit * norm_ref[2:3, :] + norm_ref[3:4, :]).astype(BF)
            n2[rows, :] = normed
            n2_t[:, rows] = normed.T
            grad = (g_ref[rows, :].astype(F32) * factor_ref[0:1, 0:1]).astype(BF)
            gb[rows, :] = grad
            dn2[rows, :] = jnp.zeros((256, width), F32)
            return 0

        for i in range(tiles):
            before(i, 0)

    up = w1[step]
    down = w2[step]
    tile = TILE
    for i in range(length // tile):
        rows = slice(i * tile, (i + 1) * tile)
        a = dot(n2[rows, :], up)
        square = a * a
        half = 0.5 + 0.5 * jnp.tanh(a * (0.7978845608 + (0.044715 * 0.7978845608) * square))
        u = a * half
        slope = half + u * (1.0 - half) * (
            2.0 * 0.7978845608 + (6.0 * 0.044715 * 0.7978845608) * square
        )
        u = u.astype(BF)
        da = (dot_nt(gb[rows, :], down) * slope).astype(BF)
        u_all[rows, :] = u
        da_all[rows, :] = da
        branch[rows, :] += dot(u, down)
        dn2[rows, :] += dot_nt(da, up)
    up_grad = dot(n2_t[...], da_all[...])
    down_grad = dot_tn(u_all[...], gb[...])
    grads[...] = up_grad.astype(BF)
    scatter_shards(pos_ref, place_ref, grads, send_ref, keep_ref, step + 1)
    grads[...] = down_grad.astype(BF)
    mine = (step ^ pos_ref[0]) & 1 == 0

    @pl.when(mine)
    def _():
        for u in range(4):
            scatter_unit(place_ref, grads, u * part, 5 + u, step, keep_ref, 0)

    @pl.when(jnp.logical_not(mine))
    def _():
        for u in range(4):
            scatter_unit(place_ref, grads, u * part, 5 + u, step, send_ref, 1)

    @pl.when(step == last)
    def _():
        gain = norm_ref[2:3, :]

        def after(i, sums):
            rows = slice(i * 256, (i + 1) * 256)
            y_ref[rows, :] = branch[rows, :].astype(BF)
            grad = dn2[rows, :]
            unit = unit_ref[rows, :]
            dh = g_ref[rows, :].astype(F32) * factor_ref[0:1, 0:1] + normalise_back(
                grad, unit, inv_ref[rows, 0:1], gain
            )
            dh_ref[rows, :] = dh
            dh_low = dh.astype(BF)
            do_ref[rows, :] = dot_nt(dh_low, wo[...]).astype(BF)
            return (
                sums[0] + jnp.sum(grad * unit, axis=0, keepdims=True),
                sums[1] + jnp.sum(grad, axis=0, keepdims=True),
                sums[2] + dot_tn(o_ref[rows, :], dh_low),
            )

        empty = jnp.zeros((1, width), F32)
        sums = (empty, empty, jnp.zeros((width, width), F32))
        for i in range(tiles):
            sums = after(i, sums)
        dnorm_ref[...] = jnp.zeros_like(dnorm_ref)
        dnorm_ref[0:1, :] = sums[0]
        dnorm_ref[1:2, :] = sums[1]
        grads[...] = sums[2].astype(BF)
        scatter_shards(pos_ref, place_ref, grads, send_ref, keep_ref, 0)


def feed(pos, place, domain_rows, x, g, o, norm, pieces, talls):
    length, width = x.shape
    block = width
    height = 5 * (width // 4) + block
    rows = lambda dtype: jax.ShapeDtypeStruct((length, width), dtype)
    out = [
        rows(BF), rows(F32), rows(BF),
        jax.ShapeDtypeStruct((2 * height, width), BF),
        jax.ShapeDtypeStruct((2 * height, width), BF),
        jax.ShapeDtypeStruct((8, width), F32),
    ]
    args = (domain_rows, x, g, o, norm) + tuple(pieces) + tuple(talls)
    return pl.pallas_call(
        feed_kernel,
        grid=(4,),
        in_specs=[pl.BlockSpec(memory_space=pltpu.SMEM)] * 2 + [whole(a) for a in args],
        out_specs=[whole(a) for a in out],
        out_shape=out,
        scratch_shapes=[
            pltpu.VMEM((width, width), BF),
            pltpu.VMEM((4, width, block), BF),
            pltpu.VMEM((4, block, width), BF),
            pltpu.VMEM((length, width), F32),
            pltpu.VMEM((length, width), F32),
            pltpu.VMEM((length, 128), F32),
            pltpu.VMEM((length, width), BF),
            pltpu.VMEM((length, width), BF),
            pltpu.VMEM((width, length), BF),
            pltpu.VMEM((length, width), F32),
            pltpu.VMEM((width, block), BF),
            pltpu.VMEM((length, block), BF),
            pltpu.VMEM((length, block), BF),
            pltpu.VMEM((8, LANES), F32),
        ],
        compiler_params=pltpu.CompilerParams(
            dimension_semantics=("arbitrary",), vmem_limit_bytes=VMEM_FEED
        ),
        name="feed",
        cost_estimate=CHEAP,
    )(pos, place, *args)


def weight_back_kernel(pos_ref, place_ref, small_ref, n_ref, *refs):
    grads_in, (send_ref, keep_ref, n_t, grads) = refs[:-4], refs[-4:]
    n_t[...] = n_ref[...].T
    for target in (send_ref, keep_ref):
        target[target.shape[0] - SMALL :, :] = small_ref[...]
    for m in range(4):
        total = None
        first = 0
        for j in range(len(grads_in) // 4):
            part = grads_in[4 * j + m]
            last = first + part.shape[0]
            term = dot(n_t[:, first:last], part[...])
            total = term if total is None else total + term
            first = last
        grads[m] = total.astype(BF)
    for m in range(4):
        scatter_shards(pos_ref, place_ref, grads.at[m], send_ref, keep_ref, m)


def weight_back(pos, place, small, n, halves):
    length, width = n.shape
    out = jax.ShapeDtypeStruct((2 * width + SMALL, width), BF)
    args = (small, n) + tuple(halves)
    return pl.pallas_call(
        weight_back_kernel,
        grid=(1,),
        in_specs=[pl.BlockSpec(memory_space=pltpu.SMEM)] * 2 + [whole(a) for a in args],
        out_specs=[whole(out)] * 2,
        out_shape=[out] * 2,
        scratch_shapes=[pltpu.VMEM((width, length), BF), pltpu.VMEM((4, width, width), BF)],
        compiler_params=pltpu.CompilerParams(
            dimension_semantics=("arbitrary",), vmem_limit_bytes=VMEM_BACK
        ),
        name="weight_back",
        cost_estimate=CHEAP,
    )(pos, place, *args)


def input_back_kernel(x_ref, dh_ref, w_ref, norm_ref, dnorm_ref, *refs):
    grads_in, (dx_ref, small_ref, sums) = refs[:-3], refs[-3:]
    step = pl.program_id(0)
    tile = x_ref.shape[0]

    @pl.when(step == 0)
    def _():
        sums[...] = jnp.zeros_like(sums)

    def rows_back(parts, first):
        rows = pl.ds(pl.multiple_of(first, tile), tile)
        dn = None
        for m in range(4):
            term = dot_nt(parts[m][rows, :], w_ref[m])
            dn = term if dn is None else dn + term
        unit, inv = normalise(x_ref[...].astype(F32))
        dx_ref[...] = dh_ref[...] + normalise_back(dn, unit, inv, norm_ref[0:1, :])
        sums[0:1, :] += jnp.sum(dn * unit, axis=0, keepdims=True)
        sums[1:2, :] += jnp.sum(dn, axis=0, keepdims=True)

    first = 0
    for j in range(len(grads_in) // 4):
        count = grads_in[4 * j].shape[0] // tile
        begin = first

        @pl.when((step >= begin) & (step < begin + count))
        def _():
            rows_back(grads_in[4 * j : 4 * j + 4], (step - begin) * tile)

        first += count

    @pl.when(step == pl.num_programs(0) - 1)
    def _():
        small_ref[...] = jnp.concatenate(
            [sums[0:2, :], dnorm_ref[0:2, :], jnp.zeros((SMALL - 4, sums.shape[1]), F32)], axis=0
        ).astype(BF)


def input_back(x, dh, w, norm, dnorm, halves):
    length, width = x.shape
    tile = 256
    block = pl.BlockSpec((tile, width), lambda i: (i, 0))
    small = jax.ShapeDtypeStruct((SMALL, width), BF)
    return pl.pallas_call(
        input_back_kernel,
        grid=(length // tile,),
        in_specs=[block] * 2 + [whole(w), whole(norm), whole(dnorm)] + [whole(a) for a in halves],
        out_specs=[block, whole(small)],
        out_shape=[jax.ShapeDtypeStruct((length, width), F32), small],
        scratch_shapes=[pltpu.VMEM((8, width), F32)],
        compiler_params=pltpu.CompilerParams(
            dimension_semantics=("arbitrary",), vmem_limit_bytes=VMEM_BACK
        ),
        name="input_back",
        cost_estimate=CHEAP,
    )(x, dh, w, norm, dnorm, *halves)


def bits_of(size):
    return [1 << b for b in range(size.bit_length() - 1)]


def exchange(values, even, odd):
    dp, shard = lax.axis_size("dp"), lax.axis_size("shard")
    perm = []
    for d in range(dp):
        for s in range(shard):
            axis, bit = odd if s % 2 else even
            other = (d ^ bit, s) if axis == "dp" else (d, s ^ bit)
            perm.append((d * shard + s, other[0] * shard + other[1]))
    return lax.ppermute(values, ("dp", "shard"), perm)


def swap(values, axis, bit):
    return exchange(values, (axis, bit), (axis, bit))


def after(values, *others):
    return lax.optimization_barrier((values,) + others)[0]


def places():
    dp, shard = lax.axis_index("dp"), lax.axis_index("shard")
    piece = jnp.arange(16, dtype=jnp.int32)
    far = (piece // 8) ^ (shard // 2)
    along = (piece % 8) ^ (dp % 8)
    bits = [(along >> b) & 1 for b in range(3)]
    even = far * 8 + bits[0] * 4 + bits[2] * 2 + (piece >> 1 & 1)
    odd = bits[0] * 8 + bits[1] * 4 + far * 2 + (piece >> 2 & 1)
    mine = shard % 2
    return jnp.stack(
        [jnp.where(mine == 0, even, odd), jnp.where(mine == 0, odd, even)]
    ).astype(jnp.int32)


HALVINGS = [
    (("shard", 2), ("dp", 1)),
    (("dp", 1), ("dp", 2)),
    (("dp", 4), ("shard", 2)),
]
MIDDLE = (("dp", 2), ("dp", 4))
GATHERS = [(("dp", 4), ("dp", 2)), (("dp", 1), ("dp", 1))]


def quarters():
    place = lax.axis_index("dp") % 8
    j = jnp.arange(4, dtype=jnp.int32)
    even = j % 2 + 2 * ((place // 4) ^ (j // 2))
    odd = 2 * (j % 2) + ((place // 2 % 2) ^ (j // 2))
    return jnp.where(lax.axis_index("shard") % 2 == 0, even, odd).astype(jnp.int32)


def low_sum(total):
    return lax.reduce_precision(total, 8, 7).astype(BF)


def add_up(parts, low, high):
    total = parts[0][low:high].astype(F32)
    for part in parts[1:]:
        total = total + part[low:high].astype(F32)
    return low_sum(total)


def add_rest(piece):
    for b in bits_of(lax.axis_size("dp"))[3:]:
        piece = add_up([piece, swap(piece, "dp", b)], 0, piece.shape[0])
    return piece


def adam(master, first, second, grad, rate, decay):
    first_new = 0.5 * first + 0.5 * grad
    second_new = 0.5 * second + 0.5 * grad * grad
    correction = 1.0 - 0.5**STEP
    update = first_new / correction / (jnp.sqrt(second_new / correction) + 1e-08)
    return master - rate * (update + decay * master), first_new, second_new


def gather_rows(index_ref, source, target, span, base):
    count = index_ref.shape[0]
    rows = LANES // 2 // count
    units = target.shape[0] // span
    for j in range(count):
        for u in range(units):
            place = pl.ds(pl.multiple_of(u * span + base + index_ref[j] * rows, rows), rows)
            first = (j * units + u) * rows
            target[place, :] = source[first : first + rows, :]


def squares_kernel(early_ref, late_ref, gn_ref, out_ref):
    total = 0.5 * jnp.sum(jnp.square(gn_ref[...]))
    for ref in (early_ref, late_ref):
        values = ref[...].astype(F32)
        total += jnp.sum(values * values)
    out_ref[...] = jnp.full(out_ref.shape, total, F32)


def squares(early, late, gn):
    vmem = pl.BlockSpec(memory_space=pltpu.VMEM)
    return pl.pallas_call(
        squares_kernel,
        in_specs=[vmem] * 3,
        out_specs=vmem,
        out_shape=jax.ShapeDtypeStruct((8, LANES), F32),
        compiler_params=pltpu.CompilerParams(vmem_limit_bytes=VMEM_UNPACK),
        name="squares",
        cost_estimate=CHEAP,
    )(early, late, gn)


def clip_factor(square_ref, other_ref):
    norm = jnp.sqrt(square_ref[0:1, 0:1] + other_ref[0:1, 0:1])
    return jnp.minimum(1.0, 1.0 / (norm + 1e-06))


def renew_kernel(
    side_ref, index_ref, square_ref, other_ref, early_ref, late_ref, gn_ref, nm, nf, ns,
    am, af, as_, um, uf, us, dm, df, ds, first_ref, second_ref, clip_ref, early, late
):
    factor = clip_factor(square_ref, other_ref)
    width = early.shape[1]
    half = LANES // 2
    step = pl.program_id(0)
    height = am.shape[1]

    @pl.when(step == 0)
    def _():
        gather_rows(index_ref, early_ref, early, half, 0)
        gather_rows(index_ref, late_ref, late, half, 0)
        new = adam(nm[...], nf[...], ns[...], gn_ref[...] * factor, 0.3, 0.0)
        last = FIRST_UNITS * half
        first_ref[last:, :] = jnp.zeros((SMALL, width), BF)
        first_ref[last : last + 4, 0:LANES] = new[0].astype(BF)
        clip_ref[0] = jnp.sqrt(square_ref[0:1, 0:1] + other_ref[0:1, 0:1])[0, 0]

    def span(unit):
        return pl.ds(pl.multiple_of(unit * half + step * height, height), height)

    blocks = um.shape[1] // width
    middle = FIRST_UNITS
    for unit in range(5 + blocks + dm.shape[0]):
        if unit < 4:
            source = late[span(unit), :]
        else:
            source = early[span(unit - 4), :]
        if unit < 5:
            state = am[unit], af[unit], as_[unit]
        elif unit < 5 + blocks:
            cols = slice((unit - 5) * width, (unit - 4) * width)
            state = um[:, cols], uf[:, cols], us[:, cols]
        else:
            state = [ref[unit - 5 - blocks] for ref in (dm, df, ds)]
        new = adam(*state, source.astype(F32) * factor, 0.05, 0.01)
        target, place = (first_ref, unit) if unit < middle else (second_ref, unit - middle)
        target[span(place), :] = new[0].astype(BF)


def renew(side, index, square, early, late, gn, attn, up, down, norm):
    five, part, width = attn[0].shape
    hidden = up[0].shape[1]
    steps = 2
    half = part // 2
    tile = half // steps
    down = [a.reshape(a.shape[0] // part, part, width) for a in down]
    units = five + hidden // width + down[0].shape[0]
    first = jax.ShapeDtypeStruct((FIRST_UNITS * half + SMALL, width), BF)
    second = jax.ShapeDtypeStruct(((units - FIRST_UNITS) * half, width), BF)
    tall = down[0].shape[0]
    return pl.pallas_call(
        renew_kernel,
        grid_spec=pltpu.PrefetchScalarGridSpec(
            num_scalar_prefetch=1,
            grid=(steps,),
            in_specs=[pl.BlockSpec(memory_space=pltpu.SMEM)]
            + [whole(a) for a in (*square, early, late, gn, *norm)]
            + [pl.BlockSpec((five, tile, width), lambda i, side: (0, steps * side[0] + i, 0))] * 3
            + [pl.BlockSpec((tile, hidden), lambda i, side: (steps * side[0] + i, 0))] * 3
            + [pl.BlockSpec((tall, tile, width), lambda i, side: (0, steps * side[0] + i, 0))] * 3,
            out_specs=[whole(first), whole(second), pl.BlockSpec(memory_space=pltpu.SMEM)],
            scratch_shapes=[pltpu.VMEM(early.shape, BF), pltpu.VMEM(late.shape, BF)],
        ),
        out_shape=[first, second, jax.ShapeDtypeStruct((1,), F32)],
        compiler_params=pltpu.CompilerParams(
            dimension_semantics=("arbitrary",), vmem_limit_bytes=VMEM_UPDATE
        ),
        name="renew",
        cost_estimate=CHEAP,
    )(side, index, *square, early, late, gn, *norm, *attn, *up, *down)


def update_kernel(
    side_ref, index_ref, square_ref, other_ref, early_ref, late_ref, got_ref, gn_ref, *refs
):
    am, af, as_, um, uf, us, dm, df, ds, nm, nf, ns = refs[:12]
    early, late = refs[-2:]
    outs, copy_low, copy_high, other_half = refs[12:-5], refs[-5], refs[-4], refs[-3]
    step = pl.program_id(0)
    factor = clip_factor(square_ref, other_ref)
    width = early.shape[1]
    part = late.shape[0] // 4
    blocks = um.shape[1] // width
    height = part // pl.num_programs(0)
    half = LANES // 2

    def keep(group, where, unit, size, new):
        for target, value in zip(outs[3 * group : 3 * group + 3], new):
            target[where] = value
        target, unit = (copy_low, unit) if unit < 8 else (copy_high, unit - 8)
        rows = pl.ds(pl.multiple_of(unit * part + step * size, size), size)
        target[rows, :] = new[0].astype(BF)

    @pl.when(step == 0)
    def _():
        mine = half * side_ref[0]
        count = late_ref.shape[0]
        gather_rows(index_ref, early_ref, early, part, mine)
        gather_rows(index_ref, late_ref, late, part, mine)
        gather_rows(index_ref, got_ref.at[:count, :], late, part, half - mine)
        gather_rows(index_ref, got_ref.at[count:, :], early, part, half - mine)
        new = adam(nm[...], nf[...], ns[...], gn_ref[...] * factor, 0.3, 0.0)
        outs[9][...], outs[10][...], outs[11][...] = new

    def span(base, size):
        return pl.ds(pl.multiple_of(base + step * size, size), size)

    for m in range(5):
        source = late[span(m * part, height), :] if m < 4 else early[span(0, height), :]
        new = adam(am[m], af[m], as_[m], source.astype(F32) * factor, 0.05, 0.01)
        keep(0, (m, slice(None), slice(None)), m, height, new)
    for j in range(blocks):
        source = early[span((j + 1) * part, height), :]
        cols = (slice(None), slice(j * width, (j + 1) * width))
        new = adam(um[cols], uf[cols], us[cols], source.astype(F32) * factor, 0.05, 0.01)
        keep(1, cols, 5 + j, height, new)
    tall = dm.shape[0]
    source = early[span((blocks + 1) * part, tall), :]
    new = adam(dm[...], df[...], ds[...], source.astype(F32) * factor, 0.05, 0.01)
    keep(2, (slice(None), slice(None)), 5 + blocks, tall, new)

    @pl.when(step == pl.num_programs(0) - 1)
    def _():
        count = other_half.shape[0] // half
        base = copy_high.shape[0] - count * part
        for j in range(count):
            rows = pl.ds(pl.multiple_of(base + j * part + half - half * side_ref[0], half), half)
            other_half[j * half : (j + 1) * half, :] = copy_high[rows, :]


def update(side, index, square, early, late, got, gn, attn, up, down, norm):
    steps = 4
    smem = pl.BlockSpec(memory_space=pltpu.SMEM)
    five, part, width = attn[0].shape
    specs = (
        [pl.BlockSpec((five, part // steps, width), lambda i: (0, i, 0))] * 3
        + [pl.BlockSpec((part // steps, up[0].shape[1]), lambda i: (i, 0))] * 3
        + [pl.BlockSpec((down[0].shape[0] // steps, width), lambda i: (i, 0))] * 3
        + [whole(norm[0])] * 3
    )
    arrays = tuple(attn) + tuple(up) + tuple(down) + tuple(norm)
    low = jax.ShapeDtypeStruct((8 * part, width), BF)
    tall, short = 2 * early.shape[0], 2 * late.shape[0]
    high = jax.ShapeDtypeStruct((tall + short - 8 * part, width), BF)
    other = jax.ShapeDtypeStruct((DIRECT_UNITS * part // 2, width), BF)
    return pl.pallas_call(
        update_kernel,
        grid=(steps,),
        in_specs=[smem] * 2 + [whole(a) for a in (*square, early, late, got, gn)] + specs,
        out_specs=specs + [whole(low), whole(high), whole(other)],
        out_shape=[jax.ShapeDtypeStruct(a.shape, F32) for a in arrays] + [low, high, other],
        scratch_shapes=[pltpu.VMEM((tall, width), BF), pltpu.VMEM((short, width), BF)],
        compiler_params=pltpu.CompilerParams(
            dimension_semantics=("arbitrary",), vmem_limit_bytes=VMEM_UPDATE
        ),
        name="update",
        cost_estimate=CHEAP,
    )(side, index, *square, early, late, got, gn, *arrays)


def place_unit(pos, source, unit, first, count, attn_ref, up_ref, down_ref, sem):
    width = attn_ref.shape[2]
    blocks = up_ref.shape[1] // width
    tall = down_ref.shape[0] // 4
    rows = pl.ds(pl.multiple_of(pos * LANES + first, count), count)
    if unit < 5:
        target = attn_ref.at[unit, rows, :]
    elif unit < 5 + blocks:
        target = up_ref.at[rows, pl.ds((unit - 5) * width, width)]
    else:
        base = pl.multiple_of(pos * tall + (unit - 5 - blocks) * LANES + first, count)
        target = down_ref.at[pl.ds(base, count), :]
    return pltpu.make_async_copy(source, target, sem)


def run_copies(copies):
    for copy in copies:
        copy.start()
    for copy in copies:
        copy.wait()


def place_whole(pos, piece, unit, outs, sems, copies):
    for j in range(piece.shape[0] // LANES):
        source = piece.at[pl.ds(j * LANES, LANES), :]
        copies.append(place_unit(pos, source, unit + j, 0, LANES, *outs, sems.at[len(copies)]))


def place_half(pos, side, piece, unit, outs, sems, copies):
    half = LANES // 2
    for j in range(piece.shape[0] // half):
        source = piece.at[pl.ds(j * half, half), :]
        copies.append(
            place_unit(pos, source, unit + j, half * side, half, *outs, sems.at[len(copies)])
        )


def unpack_near_kernel(pos_ref, side_ref, p0, p1, p2, p3, p4, p5, attn_ref, up_ref, down_ref, sems):
    copies = []
    outs = attn_ref, up_ref, down_ref
    for index, parts in enumerate(((p0, p1), (p2, p3))):
        place_whole(pos_ref[index], parts[0], 0, outs, sems, copies)
        place_whole(pos_ref[index], parts[1], 8, outs, sems, copies)
    for index, piece in enumerate((p4, p5)):
        place_half(pos_ref[2 + index], side_ref[0], piece, 0, outs, sems, copies)
    run_copies(copies)


def unpack_far_kernel(pos_ref, side_ref, *refs):
    pieces, outs, sems = refs[:8], refs[11:14], refs[14]
    copies = []
    other = side_ref[0] ^ 1
    for index in range(2):
        second, first_other, second_other, direct = pieces[4 * index : 4 * index + 4]
        pos = pos_ref[2 + index]
        place_half(pos, side_ref[0], second, FIRST_UNITS, outs, sems, copies)
        place_half(pos, other, first_other, 0, outs, sems, copies)
        place_half(pos, other, second_other, FIRST_UNITS, outs, sems, copies)
        unit = FIRST_UNITS + second_other.shape[0] // (LANES // 2)
        place_half(pos, other, direct, unit, outs, sems, copies)
    run_copies(copies)


def share_copies(pos, side, first, second, low, high, direct, width, hidden):
    units = (low.shape[0] + high.shape[0]) // LANES
    half = LANES // 2
    last_rows = swap(first[FIRST_UNITS * half :], "shard", 1)
    ours, first_too, low, high, direct = lax.optimization_barrier(
        (swap(first, "shard", 2), last_rows, low, high, direct)
    )
    other = swap(ours, "dp", 1)
    second_got = swap(after(second, ours), "shard", 2)
    near = [swap(part, "shard", 1) for part in (low, high)]
    ours_too = swap(ours, "shard", 1)
    a, b, c, d = [
        p[p.shape[0] - SMALL : p.shape[0] - SMALL + 4, :LANES]
        for p in (first, first_too, ours, ours_too)
    ]
    low_bit, high_bit = pos[0] % 2 == 1, pos[0] // 2 == 1
    a, b, c, d = [jnp.where(low_bit, v, u) for u, v in ((a, b), (b, a), (c, d), (d, c))]
    a, b, c, d = [jnp.where(high_bit, v, u) for u, v in ((a, c), (b, d), (c, a), (d, b))]
    norms = jnp.concatenate([a, b, c, d], axis=1)
    hbm = pl.BlockSpec(memory_space=pl.ANY)
    vmem = pl.BlockSpec(memory_space=pltpu.VMEM)
    smem = pl.BlockSpec(memory_space=pltpu.SMEM)
    shapes = [
        jax.ShapeDtypeStruct((5, width, width), BF),
        jax.ShapeDtypeStruct((width, hidden), BF),
        jax.ShapeDtypeStruct((hidden, width), BF),
    ]
    params = pltpu.CompilerParams(vmem_limit_bytes=VMEM_UNPACK)
    begun = pl.pallas_call(
        unpack_near_kernel,
        in_specs=[smem, smem] + [vmem] * 6,
        out_specs=[hbm] * 3,
        out_shape=shapes,
        scratch_shapes=[pltpu.SemaphoreType.DMA((2 * (units + FIRST_UNITS),))],
        compiler_params=params,
        name="unpack_near",
        cost_estimate=CHEAP,
    )(pos, side, after(low, norms), high, *near, ours, ours_too)
    second = after(second_got, begun[0])
    second_other = swap(second[: -direct.shape[0]], "dp", 1)
    direct = swap(after(direct, second), "shard", 2)
    far = [second, other, second_other, direct]
    far += [swap(after(f, begun[0]), "shard", 1) for f in far]
    done = pl.pallas_call(
        unpack_far_kernel,
        in_specs=[smem, smem] + [vmem] * 8 + [hbm] * 3,
        out_specs=[hbm] * 3,
        out_shape=shapes,
        scratch_shapes=[pltpu.SemaphoreType.DMA((4 * units,))],
        input_output_aliases={10: 0, 11: 1, 12: 2},
        compiler_params=params,
        name="unpack_far",
        cost_estimate=CHEAP,
    )(pos, side, *far, *begun)
    return tuple(done) + (norms,)


def shards(
    tokens, out_grad, domain_ids, domain_weight,
    attn_master, attn_first, attn_second,
    up_master, up_first, up_second,
    down_master, down_first, down_second,
    norm_master, norm_first, norm_second,
):
    length, width = tokens.shape
    hidden = up_master.shape[1]
    part = width // 4
    blocks = hidden // width
    dp = lax.axis_index("dp")
    shard = lax.axis_index("shard").astype(jnp.int32)
    pos = shard ^ jnp.arange(4, dtype=jnp.int32)
    half = (dp % 2).astype(jnp.int32)[None]
    place = places()

    small = jnp.pad(norm_master.astype(BF), ((0, SMALL - 4), (0, width - part)))
    rows = attn_master[:4].astype(BF).reshape(4 * part, width)
    own = jnp.concatenate([rows[: 2 * part], small, rows[2 * part :], jnp.zeros_like(small)])
    middle = own.shape[0] // 2
    near = swap(own, "shard", 1)
    ours = lax.dynamic_slice(own, (half[0] * middle, 0), (middle, width))
    far_a = swap(ours, "shard", 2)

    domains = domain_weight.shape[0]
    devices = lax.axis_size("dp") * lax.axis_size("shard") * domain_ids.shape[0]
    onehot = (domain_ids[:, None] == jnp.arange(domains, dtype=jnp.int32)[None, :]).astype(F32)
    counts = jnp.sum(onehot, axis=0)
    dp_bits = bits_of(lax.axis_size("dp"))
    for b in dp_bits[:2]:
        counts = counts + swap(counts, "dp", b)
    far_b = swap(after(far_a, counts), "dp", 1)
    second = jnp.concatenate(
        [attn_master[4].astype(BF)]
        + [up_master[:, j * width : (j + 1) * width].astype(BF) for j in range(blocks)]
    )
    second_far = swap(after(second, counts), "shard", 2)
    for b in dp_bits[2:]:
        counts = counts + after(swap(counts, "dp", b), far_b)
    counts_row = jnp.pad(counts.astype(BF)[None], ((0, SMALL - 1), (0, width - domains)))
    third = jnp.concatenate([down_master.astype(BF), counts_row])
    third_far = swap(third, "shard", 2)
    second = [second, swap(second, "shard", 1), second_far]
    third = [third, swap(third, "shard", 1), third_far]
    domain_rows = jnp.pad(
        jnp.stack([onehot[0], domain_weight * devices / domains]),
        ((0, 6), (0, LANES - domains)),
    )
    far_c = swap(far_a, "shard", 1)
    far = [far_a, far_b, far_c, swap(far_b, "shard", 1)]
    q, k, v, n, e, eb, z, o, weights, scores, keys, values, w, norm = attend(
        pos, half, tokens, [own, near] + far
    )
    for pieces in (second, third):
        pieces.append(swap(after(pieces[2], o), "shard", 1))
    y, dh, do, send, keep, dnorm = feed(
        pos, place, domain_rows, tokens, out_grad, o, norm, second, third
    )

    steps, plan, index = HALVINGS + [MIDDLE], GATHERS, quarters()
    pieces = 16
    rows = keep.shape[0] // pieces

    def forward_phase(parts, phase, rows):
        low = rows * pieces >> (phase + 1)
        return add_up(parts, low, 2 * low)

    saved = (q, k, v, eb, e, z, weights, scores, keys, values)
    chunks = length // CHUNK
    early = [keep, swap(send, "shard", 1)]
    later = mix_back(chunks - 1, 1, (), do, *saved)
    out = after(forward_phase(early, 0, rows), later[0])
    early.append(exchange(out, *steps[0]))
    sooner = mix_back(chunks - 2, chunks - 1, later[4:], after(do, out), *saved)
    back = list(sooner[:4]) + list(later[:4])
    out = after(forward_phase(early, 1, rows), back[0])
    early.append(exchange(out, *steps[1]))
    dx, small = input_back(tokens, after(dh, out), w, norm, dnorm, back)
    send, keep = weight_back(pos, place, small, n, back)
    turn = forward_phase(early, 2, rows)
    got = exchange(turn, *steps[2])
    late = [keep, swap(after(send, turn), "shard", 1)]
    height = keep.shape[0] - SMALL
    thin = height // pieces
    small = add_up(late, height, height + SMALL)

    def late_phase(phase):
        out = jnp.concatenate([forward_phase(late, phase, thin), small])
        return out, exchange(out, *steps[phase])

    def late_sum(got):
        late.append(got)
        return add_up([small, got[got.shape[0] - SMALL :]], 0, SMALL)

    turn, late_got = late_phase(0)
    small = late_sum(late_got)
    turn, late_got = late_phase(1)
    early.append(after(got, turn))
    turn = add_up(early, 0, 2 * rows)
    got = exchange(turn, *steps[3])
    small = late_sum(after(late_got, turn))
    early = turn
    turn, late_got = late_phase(2)
    early = add_rest(add_up([early, after(got, turn)], 0, 2 * rows))
    got = exchange(early, *plan[0])
    small = late_sum(after(late_got, early))
    out = jnp.concatenate([add_up(late, 0, 2 * thin), small])
    late_got = exchange(out, *steps[3])
    late = add_rest(add_up([out, late_got], 0, 2 * thin + SMALL))
    late, small = late[: 2 * thin], late[2 * thin :]
    late_got = exchange(late, *plan[0])
    norm_grad = lax.dynamic_slice(small[:4], (0, shard * part), (4, part)).astype(F32)
    early = jnp.concatenate([early, after(got, late)])
    late = jnp.concatenate([late, after(late_got, early)])
    square = squares(early, late, norm_grad)
    square = square + swap(square, "dp", 1)
    got = exchange(after(jnp.concatenate([late, early]), square), *plan[1])
    square = square + swap(square, "shard", 1)
    square = (square, swap(square, "shard", 2))
    attn = (attn_master, attn_first, attn_second)
    up = (up_master, up_first, up_second)
    down = (down_master, down_first, down_second)
    norms = (norm_master, norm_first, norm_second)
    first, second, clip_norm = renew(
        half, index, square, early, late, norm_grad, attn, up, down, norms
    )
    *new, low, high, direct = update(
        half, index, square, early, late, after(got, first), norm_grad, attn, up, down, norms
    )
    copies = share_copies(pos, half, first, second, low, high, direct, width, hidden)
    return (y, dx) + tuple(new) + (clip_norm.reshape(()),) + tuple(copies)


def solution(mesh):
    rows = P(("dp", "shard"), None)
    attn = (P(None, "shard", None),) * 3
    tall = (P("shard", None),) * 6
    norm = (P(None, "shard"),) * 3
    return jax.shard_map(
        shards,
        mesh=mesh,
        in_specs=(rows, rows, P(("dp", "shard")), P()) + attn + tall + norm,
        out_specs=(rows, rows) + attn + tall + norm + (P(),) * 5,
        check_vma=False,
    )
```
